32 devices in a mesh: rows: 16 (over z, y, x), seq: 2 (over core).
Axes of the slice: x: 2, y: 2, z: 4, core: 2. Of those that a mesh axis runs over, the one named last changes fastest.
Arguments:
- enc_input: bfloat16 [16, 512, 512], P('rows', 'seq'), may hold values from -6 to 6
- dec_input: bfloat16 [16, 128, 512], P('rows', 'seq'), may hold values from -6 to 6
- enc_segments: int32 [16, 512], P('rows'), may hold values from 0 to 3, as said below
- dec_segments: int32 [16, 128], P('rows'), may hold values from 0 to 3, as said below
- cotangent: bfloat16 [16, 128, 512], P('rows', 'seq'), may hold values from -6 to 6
- enc_norm_attn: float32 [512], replicated, may hold values from 0.5 to 1.5
- enc_query: bfloat16 [512, 512], replicated, may hold values from -0.03125 to 0.03125
- enc_key: bfloat16 [512, 512], replicated, may hold values from -0.25 to 0.25
- enc_value: bfloat16 [512, 512], replicated, may hold values from -0.25 to 0.25
- enc_mix: bfloat16 [512, 512], replicated, may hold values from -0.75 to 0.75
- enc_table: float32 [32, 8], replicated, may hold values from -4 to 4
- enc_norm_ff: float32 [512], replicated, may hold values from 0.5 to 1.5
- enc_up: bfloat16 [512, 2048], replicated, may hold values from -0.25 to 0.25
- enc_down: bfloat16 [2048, 512], replicated, may hold values from -0.1875 to 0.1875
- enc_norm_final: float32 [512], replicated, may hold values from 0.5 to 1.5
- dec_norm_self: float32 [512], replicated, may hold values from 0.5 to 1.5
- dec_query: bfloat16 [512, 512], replicated, may hold values from -0.03125 to 0.03125
- dec_key: bfloat16 [512, 512], replicated, may hold values from -0.25 to 0.25
- dec_value: bfloat16 [512, 512], replicated, may hold values from -0.25 to 0.25
- dec_mix: bfloat16 [512, 512], replicated, may hold values from -0.75 to 0.75
- dec_table: float32 [32, 8], replicated, may hold values from -4 to 4
- dec_norm_cross: float32 [512], replicated, may hold values from 0.5 to 1.5
- cross_query: bfloat16 [512, 512], replicated, may hold values from -0.03125 to 0.03125
- cross_key: bfloat16 [512, 512], replicated, may hold values from -0.25 to 0.25
- cross_value: bfloat16 [512, 512], replicated, may hold values from -0.25 to 0.25
- cross_mix: bfloat16 [512, 512], replicated, may hold values from -0.75 to 0.75
- dec_norm_ff: float32 [512], replicated, may hold values from 0.5 to 1.5
- dec_up: bfloat16 [512, 2048], replicated, may hold values from -0.25 to 0.25
- dec_down: bfloat16 [2048, 512], replicated, may hold values from -0.1875 to 0.1875
Outputs:
- enc_result: float32 [16, 512, 512], P('rows', 'seq')
- dec_result: float32 [16, 128, 512], P('rows', 'seq')
- enc_input_grad: float32 [16, 512, 512], P('rows', 'seq')
- dec_input_grad: float32 [16, 128, 512], P('rows', 'seq')
- row_norms: float32 [16], P('rows')
- grad_enc_norm_attn: float32 [512], P('rows')
- grad_enc_query: float32 [512, 512], P('rows', 'seq')
- grad_enc_key: float32 [512, 512], P('rows', 'seq')
- grad_enc_value: float32 [512, 512], P('rows', 'seq')
- grad_enc_mix: float32 [512, 512], P('rows', 'seq')
- grad_enc_table: float32 [32, 8], replicated
- grad_enc_norm_ff: float32 [512], P('rows')
- grad_enc_up: float32 [512, 2048], P('rows', 'seq')
- grad_enc_down: float32 [2048, 512], P('rows', 'seq')
- grad_enc_norm_final: float32 [512], P('rows')
- grad_dec_norm_self: float32 [512], P('rows')
- grad_dec_query: float32 [512, 512], P('rows', 'seq')
- grad_dec_key: float32 [512, 512], P('rows', 'seq')
- grad_dec_value: float32 [512, 512], P('rows', 'seq')
- grad_dec_mix: float32 [512, 512], P('rows', 'seq')
- grad_dec_table: float32 [32, 8], replicated
- grad_dec_norm_cross: float32 [512], P('rows')
- grad_cross_query: float32 [512, 512], P('rows', 'seq')
- grad_cross_key: float32 [512, 512], P('rows', 'seq')
- grad_cross_value: float32 [512, 512], P('rows', 'seq')
- grad_cross_mix: float32 [512, 512], P('rows', 'seq')
- grad_dec_norm_ff: float32 [512], P('rows')
- grad_dec_up: float32 [512, 2048], P('rows', 'seq')
- grad_dec_down: float32 [2048, 512], P('rows', 'seq')
The draws below stay inside these ranges and needn't reach their ends.
Inputs may be any that keep to these rules, and one draw needn't show every extreme that they name: `enc_segments`: along a row ids never fall, every id of 0 to 3 is present, and positions 255 and 256 hold the same id. `dec_segments`: along a row ids never fall, every id of 0 to 3 is present, and positions 63 and 64 hold the same id.
All inputs are finite; a program needn't handle non-finite values.
Results may differ from the reference program's by a relative error of at most 0.023.
Values may be sent and summed in bfloat16 or wider, within the bound.
No kernel may reach another device: no remote copies, remote signals or barrier semaphores. Data moves between devices by JAX's collectives and lax.ppermute only.
A program may use at most 192 MiB of HBM per device.

```python
import math
import jax
import jax.numpy as jnp
from jax import lax

D = 512
HEADS = 8
HEAD = 64
FF = 2048
BUCKETS = 32
MAX_DIST = 128
NDOC = 4
ROWS = 16
ENC = 512
DEC = 128


def packed_ids(key, length):
    middle = length // 2

    def draw_row(row_key):
        shuffled = jax.random.permutation(row_key, length - 2).astype(jnp.int32)
        borders = shuffled[:NDOC - 1] + 1
        borders = borders + (borders >= middle).astype(jnp.int32)
        places = jnp.arange(length, dtype=jnp.int32)
        return jnp.sum((places[:, None] >= borders[None, :]).astype(jnp.int32), axis=1).astype(jnp.int32)
    return jax.vmap(draw_row)(jax.random.split(key, ROWS))


def draw_enc_segments(key, part):
    key = jax.random.fold_in(key, 5)
    return packed_ids(key, ENC)


def draw_dec_segments(key, part):
    key = jax.random.fold_in(key, 6)
    return packed_ids(key, DEC)


def block_scale(rng, shape, cuts, smallest, high):
    level = 1.0
    for position, blocks in cuts:
        steps = jax.random.uniform(jax.random.fold_in(jax.random.fold_in(rng, 6), position), (blocks,), jnp.float32, smallest / len(cuts), high / len(cuts))
        level = level * jnp.repeat(jnp.exp(steps), shape[position] // blocks).reshape((-1,) + (1,) * (len(shape) - 1 - position))
    return level


def centred(key, dims, scale, most, cuts=(), kind=jnp.bfloat16):
    level = block_scale(key, dims, cuts, -0.22, 0.18) if cuts else 1.0
    entries = jax.random.normal(key, dims, jnp.float32) * scale * level
    return jnp.minimum(jnp.maximum(entries, -most), most).astype(kind)


def setup_inputs(seed: int = 0) -> dict:
    arg_keys = jax.random.split(jax.random.key(seed), 30)
    enc_input = centred(arg_keys[0], (ROWS, ENC, D), 1.0, 6.0, ((0, 16), (1, 2)))
    dec_input = centred(arg_keys[1], (ROWS, DEC, D), 1.0, 6.0, ((0, 16), (1, 2)))
    enc_segments = draw_enc_segments(jax.random.fold_in(arg_keys[29], 71), 0)
    dec_segments = draw_dec_segments(jax.random.fold_in(arg_keys[29], 71), 0)
    cotangent = centred(arg_keys[4], (ROWS, DEC, D), 1.0, 6.0, ((0, 16), (1, 2)))
    enc_norm_attn = jnp.clip(1.0 + 0.1 * jax.random.normal(arg_keys[5], (D,), jnp.float32), 0.5, 1.5)
    enc_query = centred(arg_keys[6], (D, HEADS * HEAD), (D * HEAD) ** -0.5, 0.03125)
    enc_key = centred(arg_keys[7], (D, HEADS * HEAD), D ** -0.5, 0.25)
    enc_value = centred(arg_keys[8], (D, HEADS * HEAD), D ** -0.5, 0.25)
    enc_mix = centred(arg_keys[9], (HEADS * HEAD, D), (HEADS * HEAD // 8) ** -0.5, 0.75)
    enc_table = centred(arg_keys[10], (BUCKETS, HEADS), 1.0, 4.0, (), jnp.float32)
    enc_norm_ff = jnp.clip(1.0 + 0.1 * jax.random.normal(arg_keys[11], (D,), jnp.float32), 0.5, 1.5)
    enc_up = centred(arg_keys[12], (D, FF), D ** -0.5, 0.25)
    enc_down = centred(arg_keys[13], (FF, D), (FF // 2) ** -0.5, 0.1875)
    enc_norm_final = jnp.clip(1.0 + 0.1 * jax.random.normal(arg_keys[14], (D,), jnp.float32), 0.5, 1.5)
    dec_norm_self = jnp.clip(1.0 + 0.1 * jax.random.normal(arg_keys[15], (D,), jnp.float32), 0.5, 1.5)
    dec_query = centred(arg_keys[16], (D, HEADS * HEAD), (D * HEAD) ** -0.5, 0.03125)
    dec_key = centred(arg_keys[17], (D, HEADS * HEAD), D ** -0.5, 0.25)
    dec_value = centred(arg_keys[18], (D, HEADS * HEAD), D ** -0.5, 0.25)
    dec_mix = centred(arg_keys[19], (HEADS * HEAD, D), (HEADS * HEAD // 8) ** -0.5, 0.75)
    dec_table = centred(arg_keys[20], (BUCKETS, HEADS), 1.0, 4.0, (), jnp.float32)
    dec_norm_cross = jnp.clip(1.0 + 0.1 * jax.random.normal(arg_keys[21], (D,), jnp.float32), 0.5, 1.5)
    cross_query = centred(arg_keys[22], (D, HEADS * HEAD), (D * HEAD) ** -0.5, 0.03125)
    cross_key = centred(arg_keys[23], (D, HEADS * HEAD), D ** -0.5, 0.25)
    cross_value = centred(arg_keys[24], (D, HEADS * HEAD), D ** -0.5, 0.25)
    cross_mix = centred(arg_keys[25], (HEADS * HEAD, D), (HEADS * HEAD // 8) ** -0.5, 0.75)
    dec_norm_ff = jnp.clip(1.0 + 0.1 * jax.random.normal(arg_keys[26], (D,), jnp.float32), 0.5, 1.5)
    dec_up = centred(arg_keys[27], (D, FF), D ** -0.5, 0.25)
    dec_down = centred(arg_keys[28], (FF, D), (FF // 2) ** -0.5, 0.1875)
    return {"enc_input": enc_input, "dec_input": dec_input, "enc_segments": enc_segments, "dec_segments": dec_segments, "cotangent": cotangent, "enc_norm_attn": enc_norm_attn, "enc_query": enc_query, "enc_key": enc_key, "enc_value": enc_value, "enc_mix": enc_mix, "enc_table": enc_table, "enc_norm_ff": enc_norm_ff, "enc_up": enc_up, "enc_down": enc_down, "enc_norm_final": enc_norm_final, "dec_norm_self": dec_norm_self, "dec_query": dec_query, "dec_key": dec_key, "dec_value": dec_value, "dec_mix": dec_mix, "dec_table": dec_table, "dec_norm_cross": dec_norm_cross, "cross_query": cross_query, "cross_key": cross_key, "cross_value": cross_value, "cross_mix": cross_mix, "dec_norm_ff": dec_norm_ff, "dec_up": dec_up, "dec_down": dec_down}


@jax.custom_vjp
def low(v):
    return lax.optimization_barrier(v.astype(jnp.bfloat16)).astype(jnp.float32)

@jax.custom_vjp
def low_back(v):
    return v

def low_keep(v):
    return (low(v), None)

def low_pass(kept, grad):
    return (grad,)

def back_keep(v):
    return (v, None)

def back_low(kept, grad):
    return (low(grad),)
low.defvjp(low_keep, low_pass)
low_back.defvjp(back_keep, back_low)
EPSILON = 1e-06
NEGATIVE = -1e+30

def cut_points(exact_span, bucket_half, reach):
    points = []
    for target in range(exact_span + 1, bucket_half):
        reach_at = exact_span
        while exact_span + int(math.log(reach_at / exact_span) / math.log(reach / exact_span) * (bucket_half - exact_span)) < target:
            reach_at += 1
        points.append(reach_at)
    return points

def bucket_index(offset, both_ways):
    if both_ways:
        bucket_half = BUCKETS // 2
        base_index = jnp.where(offset > 0, bucket_half, 0).astype(jnp.int32)
        distance = jnp.abs(offset)
    else:
        bucket_half = BUCKETS
        base_index = jnp.zeros_like(offset)
        distance = jnp.maximum(-offset, 0)
    exact_span = bucket_half // 2
    result = base_index + jnp.minimum(distance, exact_span)
    for border in cut_points(exact_span, bucket_half, MAX_DIST):
        result = result + (distance >= border).astype(jnp.int32)
    return result

def bias_of(query_pos, key_pos, table, both_ways):
    buckets = bucket_index(key_pos[None, :] - query_pos[:, None], both_ways)
    onehot = (buckets[:, :, None] == jnp.arange(BUCKETS, dtype=jnp.int32)).astype(jnp.float32)
    return jnp.einsum('qkb,bh->hqk', onehot, table, precision=lax.Precision.HIGHEST)

def rms_norm(values, gain):
    return values * lax.rsqrt(lax.optimization_barrier(jnp.mean(values * values, axis=-1, keepdims=True)) + EPSILON) * gain

def matmul(left, right):
    return jnp.dot(left, right, precision=lax.Precision.HIGHEST)

def project(normed, weight):
    return low(low_back(matmul(normed, weight))).reshape(normed.shape[0], HEADS, HEAD)

def attend(queries, keys, values, bias, allowed):
    scores = jnp.einsum('qhe,khe->hqk', queries, keys, precision=lax.Precision.HIGHEST)
    if bias is not None:
        scores = scores + bias
    scores = jnp.where(allowed[None], low_back(scores), NEGATIVE)
    highest = lax.optimization_barrier(jnp.max(scores, axis=-1, keepdims=True))
    weights = jnp.exp(scores - highest)
    probs = weights / lax.optimization_barrier(jnp.sum(weights, axis=-1, keepdims=True))
    mixed = jnp.einsum('hqk,khe->qhe', low(probs), values, precision=lax.Precision.HIGHEST)
    return low(low_back(mixed.reshape(mixed.shape[0], HEADS * HEAD)))

def feed_forward(stream, gain, w_up, w_down):
    normed = low(rms_norm(stream, gain))
    before = low_back(matmul(normed, w_up))
    return low_back(matmul(low(jax.nn.gelu(before)), w_down))

def row_forward(enc_row, dec_row, enc_ids, dec_ids, params):
    enc_norm_attn, enc_query, enc_key, enc_value, enc_mix, enc_table, enc_norm_ff, enc_up, enc_down, enc_norm_final, dec_norm_self, dec_query, dec_key, dec_value, dec_mix, dec_table, dec_norm_cross, cross_query, cross_key, cross_value, cross_mix, dec_norm_ff, dec_up, dec_down = params
    enc_pos = jnp.arange(ENC, dtype=jnp.int32)
    dec_pos = jnp.arange(DEC, dtype=jnp.int32)
    enc_normed = low(rms_norm(enc_row, enc_norm_attn))
    enc_allowed = enc_ids[:, None] == enc_ids[None, :]
    enc_mixed = attend(project(enc_normed, enc_query), project(enc_normed, enc_key), project(enc_normed, enc_value), bias_of(enc_pos, enc_pos, enc_table, True), enc_allowed)
    enc_mid = enc_row + low_back(matmul(enc_mixed, enc_mix))
    enc_after = enc_mid + feed_forward(enc_mid, enc_norm_ff, enc_up, enc_down)
    enc_state = low(rms_norm(enc_after, enc_norm_final))
    dec_normed = low(rms_norm(dec_row, dec_norm_self))
    dec_allowed = (dec_pos[None, :] <= dec_pos[:, None]) & (dec_ids[:, None] == dec_ids[None, :])
    dec_mixed = attend(project(dec_normed, dec_query), project(dec_normed, dec_key), project(dec_normed, dec_value), bias_of(dec_pos, dec_pos, dec_table, False), dec_allowed)
    dec_mid = dec_row + low_back(matmul(dec_mixed, dec_mix))
    cross_in = low(rms_norm(dec_mid, dec_norm_cross))
    cross_allowed = dec_ids[:, None] == enc_ids[None, :]
    cross_mixed = attend(project(cross_in, cross_query), project(enc_state, cross_key), project(enc_state, cross_value), None, cross_allowed)
    dec_cross = dec_mid + low_back(matmul(cross_mixed, cross_mix))
    dec_after = dec_cross + feed_forward(dec_cross, dec_norm_ff, dec_up, dec_down)
    return (enc_after, dec_after)

def reference(enc_input, dec_input, enc_segments, dec_segments, cotangent, enc_norm_attn, enc_query, enc_key, enc_value, enc_mix, enc_table, enc_norm_ff, enc_up, enc_down, enc_norm_final, dec_norm_self, dec_query, dec_key, dec_value, dec_mix, dec_table, dec_norm_cross, cross_query, cross_key, cross_value, cross_mix, dec_norm_ff, dec_up, dec_down):
    params = tuple((entry.astype(jnp.float32) for entry in (enc_norm_attn, enc_query, enc_key, enc_value, enc_mix, enc_table, enc_norm_ff, enc_up, enc_down, enc_norm_final, dec_norm_self, dec_query, dec_key, dec_value, dec_mix, dec_table, dec_norm_cross, cross_query, cross_key, cross_value, cross_mix, dec_norm_ff, dec_up, dec_down)))

    def whole(enc_all, dec_all, weights):

        def one_row(items):
            return row_forward(items[0], items[1], items[2], items[3], weights)
        return lax.map(jax.checkpoint(one_row), (enc_all, dec_all, enc_segments, dec_segments))
    outputs, backward = jax.vjp(whole, enc_input.astype(jnp.float32), dec_input.astype(jnp.float32), params)
    enc_grad, dec_grad, grads = backward((jnp.zeros_like(outputs[0]), cotangent.astype(jnp.float32)))
    row_norms = jnp.sqrt(lax.optimization_barrier(jnp.sum(enc_grad * enc_grad, axis=(1, 2))) + lax.optimization_barrier(jnp.sum(dec_grad * dec_grad, axis=(1, 2))))
    return (outputs[0], outputs[1], enc_grad, dec_grad, row_norms, grads[0], grads[1], grads[2], grads[3], grads[4], grads[5], grads[6], grads[7], grads[8], grads[9], grads[10], grads[11], grads[12], grads[13], grads[14], grads[15], grads[16], grads[17], grads[18], grads[19], grads[20], grads[21], grads[22], grads[23])
```

```python
import math

import jax
import jax.numpy as jnp
from jax import lax
from jax.sharding import PartitionSpec as P

D = 512
HEADS = 8
HEAD = 64
BUCKETS = 32
MAX_DIST = 128


EPSILON = 1e-06
NEGATIVE = -1e30


def shortened(shard):

    def short(part):
        return part.astype(jnp.bfloat16) if part.dtype == jnp.float32 else part

    return jax.tree.map(short, shard)


def cut_points(exact_span, bucket_half, reach):
    points = []
    for target in range(exact_span + 1, bucket_half):
        reach_at = exact_span
        while (
            exact_span
            + int(
                math.log(reach_at / exact_span)
                / math.log(reach / exact_span)
                * (bucket_half - exact_span)
            )
            < target
        ):
            reach_at += 1
        points.append(reach_at)
    return points


def bucket_index(offset, both_ways):
    if both_ways:
        bucket_half = BUCKETS // 2
        base_index = jnp.where(offset > 0, bucket_half, 0).astype(jnp.int32)
        distance = jnp.abs(offset)
    else:
        bucket_half = BUCKETS
        base_index = jnp.zeros_like(offset)
        distance = jnp.maximum(-offset, 0)
    exact_span = bucket_half // 2
    result = base_index + jnp.minimum(distance, exact_span)
    for border in cut_points(exact_span, bucket_half, MAX_DIST):
        result = result + (distance >= border).astype(jnp.int32)
    return result


def bias_terms(query_pos, key_pos, table, both_ways):
    buckets = bucket_index(key_pos[None, :] - query_pos[:, None], both_ways)
    onehot = buckets[:, :, None] == jnp.arange(BUCKETS, dtype=jnp.int32)
    bias = jnp.einsum(
        "qkb,bh->hqk", onehot.astype(jnp.float32), table, precision=lax.Precision.HIGHEST
    )
    return (bias, onehot.astype(jnp.bfloat16))


def table_grad(score_grad, onehot):
    return jnp.einsum("rhqk,qkb->bh", score_grad, onehot, preferred_element_type=jnp.float32)


def rms_norm(values, gain):
    return values * lax.rsqrt(jnp.mean(values * values, axis=-1, keepdims=True) + EPSILON) * gain


def norm_back(values, gain, cotan):
    _, backward = jax.vjp(rms_norm, values, gain)
    return backward(cotan)


def matmul(left, right):
    return jnp.dot(left, right, preferred_element_type=jnp.float32)


def contract_rows(left, right):
    return lax.dot_general(
        left, right, (((0,), (0,)), ((), ())), preferred_element_type=jnp.float32
    )


def contract_cols(left, right):
    return lax.dot_general(
        left, right, (((1,), (1,)), ((), ())), preferred_element_type=jnp.float32
    )


def bit_orders(rows_count):
    bits = rows_count.bit_length() - 1
    plain = list(range(bits))
    return (plain, plain if bits < 2 else [1, 0] + plain[2:])


def chunk_of(place, order):
    bits = len(order)
    return sum(((place >> (bits - 1 - s)) & 1) << order[s] for s in range(bits))


def swap_cores(values):
    return lax.ppermute(values, "seq", [(0, 1), (1, 0)])


def summed_shares(grads, rows_count):
    low = jnp.bfloat16
    core = lax.axis_index("seq")
    chip = lax.axis_index("rows")
    orders = bit_orders(rows_count)
    places = jnp.array(
        [[chunk_of(place, order) for place in range(rows_count)] for order in orders], jnp.int32
    )
    chunks = places[core] ^ chip
    kept, given, vectors = [], [], []
    for grad in grads:
        if grad.ndim == 1:
            vectors.append(grad)
            continue
        half = grad.shape[1] // 2
        for part, start in ((kept, core * half), (given, (1 - core) * half)):
            piece = lax.dynamic_slice_in_dim(grad, start, half, 1).astype(low)
            part.append(
                piece.reshape(rows_count, grad.shape[0] // rows_count, half // 256, 256)
                .transpose(0, 2, 1, 3)
                .reshape(rows_count, -1, 256)
            )
    kept = jnp.take(jnp.concatenate(kept, 1), chunks, axis=0)
    given = jnp.take(jnp.concatenate(given, 1), places[1 - core] ^ chip, axis=0)
    held = (kept.astype(jnp.float32) + swap_cores(given).astype(jnp.float32)).astype(low)
    for stage in range(len(orders[0])):
        half = held.shape[0] // 2
        pairs = [
            (chip_at * 2 + core_at, (chip_at ^ (1 << orders[core_at][stage])) * 2 + core_at)
            for chip_at in range(rows_count)
            for core_at in range(2)
        ]
        came = lax.ppermute(held[half:], ("rows", "seq"), pairs)
        held = held[:half].astype(jnp.float32) + came.astype(jnp.float32)
        if half > 1:
            held = held.astype(low)
    held = held[0]
    width = D // rows_count
    sums = lax.psum(jnp.stack(vectors), ("rows", "seq"))
    sums = lax.dynamic_slice_in_dim(sums, chip * width, width, 1)
    shares, row, vector = [], 0, 0
    for grad in grads:
        if grad.ndim == 1:
            shares.append(sums[vector])
            vector += 1
            continue
        lead, half = grad.shape[0] // rows_count, grad.shape[1] // 2
        count = lead * half // 256
        piece = held[row : row + count]
        row += count
        shares.append(piece.reshape(half // 256, lead, 256).transpose(1, 0, 2).reshape(lead, half))
    return shares


def masked_scores(queries, keys, bias, allowed):
    scores = jnp.einsum("rqhe,rkhe->rhqk", queries, keys, preferred_element_type=jnp.float32)
    if bias is not None:
        scores = scores + bias[None]
    return jnp.where(allowed[:, None], scores, NEGATIVE)


def attention_forward(queries, keys, values, bias, allowed):
    scores = masked_scores(queries, keys, bias, allowed)
    highest = jnp.max(scores, axis=-1, keepdims=True)
    weights = jnp.exp(scores - highest)
    totals = jnp.sum(weights, axis=-1, keepdims=True)
    mixed = jnp.einsum(
        "rhqk,rkhe->rqhe",
        (weights / totals).astype(jnp.bfloat16),
        values,
        preferred_element_type=jnp.float32,
    )
    return (mixed, highest + jnp.log(totals))


def attention_backward(queries, keys, values, bias, allowed, log_total, mixed_grad):
    probs = jnp.exp(masked_scores(queries, keys, bias, allowed) - log_total)
    probs_grad = jnp.einsum(
        "rqhe,rkhe->rhqk", mixed_grad, values, preferred_element_type=jnp.float32
    )
    inner = jnp.sum(probs_grad * probs, axis=-1, keepdims=True)
    score_grad = (probs * (probs_grad - inner)).astype(jnp.bfloat16)
    query_grad = jnp.einsum("rhqk,rkhe->rqhe", score_grad, keys, preferred_element_type=jnp.float32)
    key_grad = jnp.einsum(
        "rhqk,rqhe->rkhe", score_grad, queries, preferred_element_type=jnp.float32
    )
    value_grad = jnp.einsum(
        "rhqk,rqhe->rkhe",
        probs.astype(jnp.bfloat16),
        mixed_grad,
        preferred_element_type=jnp.float32,
    )
    return (query_grad, key_grad, value_grad, score_grad)


def feed_back(stream_grad, ff_normed, before, active, w_up, w_down):
    grad_low = stream_grad.astype(jnp.bfloat16)
    grad_down = contract_rows(active, grad_low)
    active_grad = contract_cols(grad_low, w_down)
    _, gelu_vjp = jax.vjp(jax.nn.gelu, before)
    before_grad = gelu_vjp(active_grad)[0].astype(jnp.bfloat16)
    grad_up = contract_rows(ff_normed, before_grad)
    return (contract_cols(before_grad, w_up), grad_up, grad_down)


def on_device(
    enc_input,
    dec_input,
    enc_segments,
    dec_segments,
    cotangent,
    enc_norm_attn,
    enc_query,
    enc_key,
    enc_value,
    enc_mix,
    enc_table,
    enc_norm_ff,
    enc_up,
    enc_down,
    enc_norm_final,
    dec_norm_self,
    dec_query,
    dec_key,
    dec_value,
    dec_mix,
    dec_table,
    dec_norm_cross,
    cross_query,
    cross_key,
    cross_value,
    cross_mix,
    dec_norm_ff,
    dec_up,
    dec_down,
):
    low_type = jnp.bfloat16
    seq_index = lax.axis_index("seq")
    seq_count = lax.axis_size("seq")
    rows_count = lax.axis_size("rows")
    batch_rows = enc_input.shape[0]
    enc_local = enc_input.shape[1]
    dec_local = dec_input.shape[1]
    enc_total = enc_local * seq_count
    dec_total = dec_local * seq_count
    enc_start = seq_index * enc_local
    dec_start = seq_index * dec_local
    enc_own = lax.dynamic_slice_in_dim(enc_segments, enc_start, enc_local, 1)
    dec_own = lax.dynamic_slice_in_dim(dec_segments, dec_start, dec_local, 1)
    enc_query_pos = enc_start + jnp.arange(enc_local, dtype=jnp.int32)
    dec_query_pos = dec_start + jnp.arange(dec_local, dtype=jnp.int32)
    enc_key_pos = jnp.arange(enc_total, dtype=jnp.int32)
    dec_key_pos = jnp.arange(dec_total, dtype=jnp.int32)

    def split_heads(values, length):
        return values.reshape(batch_rows, length, HEADS, HEAD)

    def merge_heads(values):
        return values.reshape(-1, HEADS * HEAD)

    enc_flat = enc_input.astype(jnp.float32).reshape(-1, D)
    enc_normed = rms_norm(enc_flat, enc_norm_attn).astype(low_type)
    enc_queries = split_heads(matmul(enc_normed, enc_query).astype(low_type), enc_local)
    enc_keys_own = split_heads(matmul(enc_normed, enc_key).astype(low_type), enc_local)
    enc_values_own = split_heads(matmul(enc_normed, enc_value).astype(low_type), enc_local)
    enc_keys_all, enc_values_all = (
        lax.all_gather(shortened(enc_keys_own), "seq", axis=1, tiled=True).astype(
            enc_keys_own.dtype
        ),
        lax.all_gather(shortened(enc_values_own), "seq", axis=1, tiled=True).astype(
            enc_values_own.dtype
        ),
    )
    enc_bias, enc_onehot = bias_terms(enc_query_pos, enc_key_pos, enc_table, True)
    enc_allowed = enc_own[:, :, None] == enc_segments[:, None, :]
    enc_mixed, enc_lse = attention_forward(
        enc_queries, enc_keys_all, enc_values_all, enc_bias, enc_allowed
    )
    enc_mixed_low = merge_heads(enc_mixed).astype(low_type)
    enc_mid = enc_flat + matmul(enc_mixed_low, enc_mix)
    enc_ff_in = rms_norm(enc_mid, enc_norm_ff).astype(low_type)
    enc_before = matmul(enc_ff_in, enc_up)
    enc_active = jax.nn.gelu(enc_before).astype(low_type)
    enc_after = enc_mid + matmul(enc_active, enc_down)
    enc_state = rms_norm(enc_after, enc_norm_final).astype(low_type)
    state_all = lax.all_gather(
        shortened(enc_state.reshape(batch_rows, enc_local, D)), "seq", axis=1, tiled=True
    )
    state_flat = state_all.reshape(-1, D)
    dec_flat = dec_input.astype(jnp.float32).reshape(-1, D)
    dec_normed = rms_norm(dec_flat, dec_norm_self).astype(low_type)
    dec_queries = split_heads(matmul(dec_normed, dec_query).astype(low_type), dec_local)
    dec_keys_own = split_heads(matmul(dec_normed, dec_key).astype(low_type), dec_local)
    dec_values_own = split_heads(matmul(dec_normed, dec_value).astype(low_type), dec_local)
    dec_keys_all, dec_values_all = (
        lax.all_gather(shortened(dec_keys_own), "seq", axis=1, tiled=True).astype(
            dec_keys_own.dtype
        ),
        lax.all_gather(shortened(dec_values_own), "seq", axis=1, tiled=True).astype(
            dec_values_own.dtype
        ),
    )
    dec_bias, dec_onehot = bias_terms(dec_query_pos, dec_key_pos, dec_table, False)
    causal = dec_key_pos[None, :] <= dec_query_pos[:, None]
    dec_allowed = causal[None] & (dec_own[:, :, None] == dec_segments[:, None, :])
    dec_mixed, dec_lse = attention_forward(
        dec_queries, dec_keys_all, dec_values_all, dec_bias, dec_allowed
    )
    dec_mixed_low = merge_heads(dec_mixed).astype(low_type)
    dec_mid = dec_flat + matmul(dec_mixed_low, dec_mix)
    cross_in = rms_norm(dec_mid, dec_norm_cross).astype(low_type)
    cross_queries = split_heads(matmul(cross_in, cross_query).astype(low_type), dec_local)
    cross_keys = split_heads(matmul(state_flat, cross_key).astype(low_type), enc_total)
    cross_values = split_heads(matmul(state_flat, cross_value).astype(low_type), enc_total)
    cross_allowed = dec_own[:, :, None] == enc_segments[:, None, :]
    cross_mixed, cross_lse = attention_forward(
        cross_queries, cross_keys, cross_values, None, cross_allowed
    )
    cross_mixed_low = merge_heads(cross_mixed).astype(low_type)
    dec_cross = dec_mid + matmul(cross_mixed_low, cross_mix)
    dec_ff_in = rms_norm(dec_cross, dec_norm_ff).astype(low_type)
    dec_before = matmul(dec_ff_in, dec_up)
    dec_active = jax.nn.gelu(dec_before).astype(low_type)
    dec_after = dec_cross + matmul(dec_active, dec_down)
    grad_stream = cotangent.astype(jnp.float32).reshape(-1, D)
    normed_grad, grad_dec_up, grad_dec_down = feed_back(
        grad_stream, dec_ff_in, dec_before, dec_active, dec_up, dec_down
    )
    back_in, grad_dec_norm_ff = norm_back(dec_cross, dec_norm_ff, normed_grad)
    grad_stream = grad_stream + back_in
    grad_low = grad_stream.astype(low_type)
    grad_cross_mix = contract_rows(cross_mixed_low, grad_low)
    mixed_grad = split_heads(contract_cols(grad_low, cross_mix).astype(low_type), dec_local)
    cq_grad, ck_grad, cv_grad, _ = attention_backward(
        cross_queries, cross_keys, cross_values, None, cross_allowed, cross_lse, mixed_grad
    )
    ck_own, cv_own = (
        lax.psum_scatter(ck_grad, "seq", scatter_dimension=1, tiled=True),
        lax.psum_scatter(cv_grad, "seq", scatter_dimension=1, tiled=True),
    )
    cq_low = merge_heads(cq_grad).astype(low_type)
    ck_low = merge_heads(ck_own).astype(low_type)
    cv_low = merge_heads(cv_own).astype(low_type)
    grad_cross_query = contract_rows(cross_in, cq_low)
    grad_cross_key = contract_rows(enc_state, ck_low)
    grad_cross_value = contract_rows(enc_state, cv_low)
    state_grad = contract_cols(ck_low, cross_key) + contract_cols(cv_low, cross_value)
    back_in, grad_dec_norm_cross = norm_back(
        dec_mid, dec_norm_cross, contract_cols(cq_low, cross_query)
    )
    grad_stream = grad_stream + back_in
    grad_low = grad_stream.astype(low_type)
    grad_dec_mix = contract_rows(dec_mixed_low, grad_low)
    mixed_grad = split_heads(contract_cols(grad_low, dec_mix).astype(low_type), dec_local)
    sq_grad, sk_grad, sv_grad, dec_score_grad = attention_backward(
        dec_queries, dec_keys_all, dec_values_all, dec_bias, dec_allowed, dec_lse, mixed_grad
    )
    table_dec_term = table_grad(dec_score_grad, dec_onehot)
    sk_own, sv_own = (
        lax.psum_scatter(sk_grad, "seq", scatter_dimension=1, tiled=True),
        lax.psum_scatter(sv_grad, "seq", scatter_dimension=1, tiled=True),
    )
    sq_low = merge_heads(sq_grad).astype(low_type)
    sk_low = merge_heads(sk_own).astype(low_type)
    sv_low = merge_heads(sv_own).astype(low_type)
    grad_dec_query = contract_rows(dec_normed, sq_low)
    grad_dec_key = contract_rows(dec_normed, sk_low)
    grad_dec_value = contract_rows(dec_normed, sv_low)
    normed_grad = (
        contract_cols(sq_low, dec_query)
        + contract_cols(sk_low, dec_key)
        + contract_cols(sv_low, dec_value)
    )
    back_in, grad_dec_norm_self = norm_back(dec_flat, dec_norm_self, normed_grad)
    dec_input_grad = grad_stream + back_in
    dec_terms = (
        [
            grad_dec_norm_self,
            grad_dec_query,
            grad_dec_key,
            grad_dec_value,
            grad_dec_mix,
            grad_dec_norm_cross,
            grad_cross_query,
            grad_cross_key,
            grad_cross_value,
            grad_cross_mix,
            grad_dec_norm_ff,
            grad_dec_up,
            grad_dec_down,
        ]
    )
    back_in, grad_enc_norm_final = norm_back(enc_after, enc_norm_final, state_grad)
    grad_stream = back_in
    normed_grad, grad_enc_up, grad_enc_down = feed_back(
        grad_stream, enc_ff_in, enc_before, enc_active, enc_up, enc_down
    )
    back_in, grad_enc_norm_ff = norm_back(enc_mid, enc_norm_ff, normed_grad)
    grad_stream = grad_stream + back_in
    grad_low = grad_stream.astype(low_type)
    grad_enc_mix = contract_rows(enc_mixed_low, grad_low)
    mixed_grad = split_heads(contract_cols(grad_low, enc_mix).astype(low_type), enc_local)
    eq_grad, ek_grad, ev_grad, enc_score_grad = attention_backward(
        enc_queries, enc_keys_all, enc_values_all, enc_bias, enc_allowed, enc_lse, mixed_grad
    )
    table_enc_term = table_grad(enc_score_grad, enc_onehot)
    ek_own, ev_own = (
        lax.psum_scatter(ek_grad, "seq", scatter_dimension=1, tiled=True),
        lax.psum_scatter(ev_grad, "seq", scatter_dimension=1, tiled=True),
    )
    eq_low = merge_heads(eq_grad).astype(low_type)
    ek_low = merge_heads(ek_own).astype(low_type)
    ev_low = merge_heads(ev_own).astype(low_type)
    grad_enc_query = contract_rows(enc_normed, eq_low)
    grad_enc_key = contract_rows(enc_normed, ek_low)
    grad_enc_value = contract_rows(enc_normed, ev_low)
    normed_grad = (
        contract_cols(eq_low, enc_query)
        + contract_cols(ek_low, enc_key)
        + contract_cols(ev_low, enc_value)
    )
    back_in, grad_enc_norm_attn = norm_back(enc_flat, enc_norm_attn, normed_grad)
    enc_input_grad = grad_stream + back_in
    enc_terms = (
        [
            grad_enc_norm_attn,
            grad_enc_query,
            grad_enc_key,
            grad_enc_value,
            grad_enc_mix,
            grad_enc_norm_ff,
            grad_enc_up,
            grad_enc_down,
            grad_enc_norm_final,
        ]
    )
    dec_summed = summed_shares(dec_terms, rows_count)
    enc_summed = summed_shares(enc_terms, rows_count)
    dec_shares, enc_shares = dec_summed, enc_summed
    enc_grad_rows = enc_input_grad.reshape(batch_rows, enc_local, D)
    dec_grad_rows = dec_input_grad.reshape(batch_rows, dec_local, D)
    row_squares = jnp.sum(enc_grad_rows * enc_grad_rows, axis=(1, 2)) + jnp.sum(
        dec_grad_rows * dec_grad_rows, axis=(1, 2)
    )
    table_enc_sum, table_dec_sum = lax.psum((table_enc_term, table_dec_term), ("rows", "seq"))
    row_norms = jnp.sqrt(lax.psum(row_squares, "seq"))
    return (
        enc_after.reshape(batch_rows, enc_local, D),
        dec_after.reshape(batch_rows, dec_local, D),
        enc_grad_rows,
        dec_grad_rows,
        row_norms,
        enc_shares[0],
        enc_shares[1],
        enc_shares[2],
        enc_shares[3],
        enc_shares[4],
        table_enc_sum,
        enc_shares[5],
        enc_shares[6],
        enc_shares[7],
        enc_shares[8],
        dec_shares[0],
        dec_shares[1],
        dec_shares[2],
        dec_shares[3],
        dec_shares[4],
        table_dec_sum,
        dec_shares[5],
        dec_shares[6],
        dec_shares[7],
        dec_shares[8],
        dec_shares[9],
        dec_shares[10],
        dec_shares[11],
        dec_shares[12],
    )


def solution(mesh):
    in_specs = (
        P("rows", "seq", None),
        P("rows", "seq", None),
        P("rows", None),
        P("rows", None),
        P("rows", "seq", None),
        P(),
        P(),
        P(),
        P(),
        P(),
        P(),
        P(),
        P(),
        P(),
        P(),
        P(),
        P(),
        P(),
        P(),
        P(),
        P(),
        P(),
        P(),
        P(),
        P(),
        P(),
        P(),
        P(),
        P(),
    )
    out_specs = (
        P("rows", "seq", None),
        P("rows", "seq", None),
        P("rows", "seq", None),
        P("rows", "seq", None),
        P("rows"),
        P("rows"),
        P("rows", "seq"),
        P("rows", "seq"),
        P("rows", "seq"),
        P("rows", "seq"),
        P(),
        P("rows"),
        P("rows", "seq"),
        P("rows", "seq"),
        P("rows"),
        P("rows"),
        P("rows", "seq"),
        P("rows", "seq"),
        P("rows", "seq"),
        P("rows", "seq"),
        P(),
        P("rows"),
        P("rows", "seq"),
        P("rows", "seq"),
        P("rows", "seq"),
        P("rows", "seq"),
        P("rows"),
        P("rows", "seq"),
        P("rows", "seq"),
    )
    return jax.shard_map(
        on_device, mesh=mesh, in_specs=in_specs, out_specs=out_specs, check_vma=False
    )
```

```python
import functools
import math

import jax
import jax.numpy as jnp
from jax import lax
from jax.experimental import pallas as pl
from jax.experimental.pallas import tpu as pltpu
from jax.sharding import PartitionSpec as P

D = 512
HEADS = 8
HEAD = 64
FF = 2048
BUCKETS = 32
MAX_DIST = 128
NDOC = 4
EPSILON = 1e-06
NEGATIVE = -1e30
BLOCK = 128
LANES = 256

LOW = jnp.bfloat16
FULL = jnp.float32
HIGH = lax.Precision.HIGHEST


def cut_points(exact_span, bucket_half, reach):
    points = []
    for target in range(exact_span + 1, bucket_half):
        reach_at = exact_span
        while (
            exact_span
            + int(
                math.log(reach_at / exact_span)
                / math.log(reach / exact_span)
                * (bucket_half - exact_span)
            )
            < target
        ):
            reach_at += 1
        points.append(reach_at)
    return points


def bucket_index(offset, both_ways):
    if both_ways:
        bucket_half = BUCKETS // 2
        base_index = jnp.where(offset > 0, bucket_half, 0).astype(jnp.int32)
        distance = jnp.abs(offset)
    else:
        bucket_half = BUCKETS
        base_index = jnp.zeros_like(offset)
        distance = jnp.maximum(-offset, 0)
    exact_span = bucket_half // 2
    result = base_index + jnp.minimum(distance, exact_span)
    for border in cut_points(exact_span, bucket_half, MAX_DIST):
        result = result + (distance >= border).astype(jnp.int32)
    return result


def dot(left, right, dims=((1,), (0,)), precision=None):
    return lax.dot_general(
        left, right, (dims, ((), ())), preferred_element_type=FULL, precision=precision
    )


def dot_cols(left, right):
    return dot(left, right, ((1,), (1,)))


def dot_rows(left, right):
    return dot(left, right, ((0,), (0,)))


def scale_of(values):
    return lax.rsqrt(jnp.mean(values * values, axis=-1, keepdims=True) + EPSILON)


def normed(values, gain):
    return (values * scale_of(values) * gain).astype(LOW)


def norm_back(values, gain, grad):
    scale = scale_of(values)
    unit = values * scale
    gain_grad = jnp.sum(grad * unit, axis=0, keepdims=True)
    grad = grad * gain
    return scale * (grad - unit * jnp.mean(grad * unit, axis=-1, keepdims=True)), gain_grad


def gelu_pair(values):
    root = math.sqrt(2.0 / math.pi)
    square = values * values
    tanh = jnp.tanh(root * values * (1.0 + 0.044715 * square))
    half = 0.5 + 0.5 * tanh
    slope = half + 0.5 * values * (1.0 - tanh * tanh) * (root + (3 * 0.044715 * root) * square)
    return values * half, slope


def iota(shape, axis):
    return lax.broadcasted_iota(jnp.int32, shape, axis)


def offsets(span, period, both_ways):
    place = iota((1, period), 1)
    offset = jnp.where(place < period - BLOCK, place, place - period) - span
    return (bucket_index(offset, both_ways) == iota((BUCKETS, period), 0)).astype(FULL)


def sheared(row, period):
    return pltpu.roll(
        jnp.broadcast_to(row, (BLOCK, period)), 0, 1, stride=1, stride_axis=0
    )


def unsheared(sums, period):
    rows = sums.shape[0]
    while rows > 8:
        rows //= 2
        sums = sums[:rows] + pltpu.roll(sums[rows:], period - rows, 1)
    total = sums[:1]
    for row in range(1, 8):
        total = total + pltpu.roll(sums[row : row + 1], period - row, 1)
    return total


def doc_columns(ids):
    wide = jnp.broadcast_to(ids.astype(FULL), (BLOCK, ids.shape[1]))
    return jnp.transpose(wide)


def doc_marks(ids):
    columns = doc_columns(ids)
    lane = iota(columns.shape, 1) % HEAD
    same = columns == lane.astype(FULL)
    query_marks = jnp.where((lane < NDOC) & jnp.logical_not(same), NEGATIVE, 0.0).astype(LOW)
    return query_marks, same.astype(FULL).astype(LOW)


def of_head(values, other, odd):
    lane = iota(values.shape, 1)
    mine = (lane >= HEAD) if odd else (lane < HEAD)
    return jnp.where(mine, values, other)


def softmax(scores):
    weights = jnp.exp(scores - jnp.max(scores, axis=-1, keepdims=True))
    return (weights * (1.0 / jnp.sum(weights, axis=-1, keepdims=True))).astype(LOW)


def score_back(probs, probs_grad):
    probs = probs.astype(FULL)
    inner = jnp.sum(probs * probs_grad, axis=-1, keepdims=True)
    return (probs * (probs_grad - inner)).astype(LOW)


def pair(index):
    return slice(index * 2 * HEAD, (index + 1) * 2 * HEAD)


def aligned(index, size):
    return pl.ds(pl.multiple_of(index * size, size), size)


class Fetch:
    def __init__(self, sems):
        self.sems = sems
        self.count = 0

    def __call__(self, source, target):
        copy = pltpu.make_async_copy(source, target, self.sems.at[self.count])
        self.count += 1
        copy.start()
        return copy


def bit_orders(rows_count):
    plain = list(range(rows_count.bit_length() - 1))
    return (plain, plain if len(plain) < 2 else [1, 0] + plain[2:])


def place_of(chunk, order):
    bits = len(order)
    return sum(((chunk >> order[s]) & 1) << (bits - 1 - s) for s in range(bits))


def chunk_of(place, order):
    bits = len(order)
    return sum(((place >> (bits - 1 - s)) & 1) << order[s] for s in range(bits))


def in_order(rows_count):
    return (D // rows_count) % 16 == 0


class Shares:
    def __init__(self, rows_count, payload):
        self.rows_count, self.payload, self.row = rows_count, payload, 0
        core, chip = lax.axis_index("seq"), lax.axis_index("rows")
        orders = bit_orders(rows_count)
        own = [place_of(chip, order) for order in orders]
        self.places = [
            jnp.where(core == 0, place_of(chunk, orders[0]) ^ own[0], place_of(chunk, orders[1]) ^ own[1])
            for chunk in range(rows_count)
        ] if in_order(rows_count) else [0]

    def put(self, grad):
        chunks = len(self.places)
        lead = grad.shape[0] // chunks
        for chunk in range(chunks):
            self.payload[self.places[chunk], self.row : self.row + lead, :] = grad[
                chunk * lead : (chunk + 1) * lead
            ].astype(LOW)
        self.row += lead


VMEM = pl.BlockSpec(memory_space=pltpu.VMEM)
HBM = pl.BlockSpec(memory_space=pl.ANY)


def call(kernel, ins, outs, scratch=(), flops=0, n_sems=0, name=None):
    specs = [HBM if where == "hbm" else VMEM for _, where in ins]
    arrays = [array for array, _ in ins]
    shapes = [jax.ShapeDtypeStruct(shape, kind) for shape, kind in outs]
    size = sum(a.size * a.dtype.itemsize for a in arrays) + sum(
        math.prod(s.shape) * s.dtype.itemsize for s in shapes
    )
    scratch = [pltpu.VMEM(shape, kind) for shape, kind in scratch]
    if n_sems:
        scratch.append(pltpu.SemaphoreType.DMA((n_sems,)))
    return pl.pallas_call(
        kernel,
        out_shape=shapes,
        in_specs=specs,
        out_specs=[VMEM] * len(shapes),
        scratch_shapes=scratch,
        compiler_params=pltpu.CompilerParams(vmem_limit_bytes=44 * 1024 * 1024),
        cost_estimate=pl.CostEstimate(
            flops=flops, bytes_accessed=size, transcendentals=0
        ),
        name=name,
    )(*arrays)


def enc_attention_kernel(
    x_own, x_other, gain, ids, table, query_all, key_all, value_all,
    mixed, probs, queries, keys, values, x_normed,
    w_query, w_key, w_value, biases, sems,
):
    core = lax.axis_index("seq")
    fetch = Fetch(sems)
    width = w_query.shape[1]
    copies = [
        fetch(source.at[:, aligned(core, width)], target)
        for source, target in ((query_all, w_query), (key_all, w_key), (value_all, w_value))
    ]
    half = x_own.shape[0]
    length = 2 * half
    for part, at in ((x_own, core), (x_other, 1 - core)):
        x_normed[aligned(at, half), :] = normed(part[...].astype(FULL), gain[...])
    span, period = length - BLOCK, 2 * length
    biases[...] = dot(table[...], offsets(span, period, True), ((0,), (0,)), HIGH)
    query_marks, key_marks = doc_marks(ids[...])
    for copy, weight, target in zip(copies, (w_query, w_key, w_value), (queries, keys, values)):
        copy.wait()
        target[...] = dot(x_normed[...], weight[...]).astype(LOW)
    for p in range(width // (2 * HEAD)):
        key_pair, value_pair = keys[:, pair(p)], values[:, pair(p)]
        halves = []
        for odd in range(2):
            head = 2 * p + odd
            bias = sheared(biases[pl.ds(core * (HEADS // 2) + head, 1), :], period)
            marked_keys = of_head(key_pair, key_marks, odd)
            parts = []
            for block in range(length // BLOCK):
                rows = slice(block * BLOCK, (block + 1) * BLOCK)
                marked = of_head(queries[rows, pair(p)], query_marks[rows], odd)
                first = span - block * BLOCK
                weights = softmax(dot_cols(marked, marked_keys) + bias[:, first : first + length])
                probs[head, rows, :] = weights
                parts.append(dot(weights, value_pair))
            halves.append(parts)
        for block in range(length // BLOCK):
            rows = slice(block * BLOCK, (block + 1) * BLOCK)
            mixed[rows, pair(p)] = of_head(halves[0][block], halves[1][block], 0).astype(LOW)


def dec_attention_kernel(
    x_own, x_other, gain, ids, table, query_hbm, key_hbm, value_hbm, mix_hbm, gain_cross, cross_hbm,
    probs, queries, keys, values, x_normed, mixed, mid, cross_in, cross_queries,
    x_all, w_query, w_key, w_value, w_mix, w_cross, sems,
):
    core = lax.axis_index("seq")
    fetch = Fetch(sems)
    copies = [
        fetch(source, target)
        for source, target in (
            (query_hbm, w_query), (key_hbm, w_key), (value_hbm, w_value), (mix_hbm, w_mix), (cross_hbm, w_cross),
        )
    ]
    half = x_own.shape[0]
    length = 2 * half
    for part, at in ((x_own, core), (x_other, 1 - core)):
        x_all[aligned(at, half), :] = part[...].astype(FULL)
    x_normed[...] = normed(x_all[...], gain[...])
    period = 2 * BLOCK
    biases = dot(table[...], offsets(0, period, False), ((0,), (0,)), HIGH)
    query_marks, key_marks = doc_marks(ids[...])
    later = iota((BLOCK, BLOCK), 1) > iota((BLOCK, BLOCK), 0)
    for copy, weight, target in zip(copies, (w_query, w_key, w_value), (queries, keys, values)):
        copy.wait()
        target[...] = dot(x_normed[...], weight[...]).astype(LOW)
    for p in range(HEADS // 2):
        query_pair, key_pair, value_pair = queries[:, pair(p)], keys[:, pair(p)], values[:, pair(p)]
        halves = []
        for odd in range(2):
            head = 2 * p + odd
            bias = sheared(biases[head : head + 1], period)[:, :length]
            scores = dot_cols(of_head(query_pair, query_marks, odd), of_head(key_pair, key_marks, odd))
            weights = softmax(jnp.where(later, NEGATIVE, scores + bias))
            probs[head] = weights
            halves.append(dot(weights, value_pair))
        mixed[:, pair(p)] = of_head(halves[0], halves[1], 0).astype(LOW)
    copies[3].wait()
    mid[...] = x_all[...] + dot(mixed[...], w_mix[...])
    cross_in[...] = normed(mid[...], gain_cross[...])
    copies[4].wait()
    cross_queries[...] = dot(cross_in[...], w_cross[...]).astype(LOW)


def enc_ff_kernel(
    x_own, x_other, mixed_own, mixed_other, mix_hbm, gain, up_hbm, down_hbm,
    mid, after, after_low, active, slope, ff_in,
    mix_own, mix_other, w_up, w_down, sems,
):
    core = lax.axis_index("seq")
    fetch = Fetch(sems)
    width, hidden = mixed_own.shape[1], w_up.shape[1]
    copies = [
        fetch(mix_hbm.at[aligned(core, width), :], mix_own),
        fetch(mix_hbm.at[aligned(1 - core, width), :], mix_other),
        fetch(up_hbm.at[:, aligned(core, hidden)], w_up),
        fetch(down_hbm.at[aligned(core, hidden), :], w_down),
    ]
    half = x_own.shape[0]
    copies[0].wait()
    copies[1].wait()
    for part, at in ((x_own, core), (x_other, 1 - core)):
        mid[aligned(at, half), :] = part[...].astype(FULL)
    mid[...] += dot(mixed_own[...], mix_own[...]) + dot(mixed_other[...], mix_other[...])
    ff_in[...] = normed(mid[...], gain[...])
    copies[2].wait()
    copies[3].wait()
    total = None
    for start in range(0, hidden, 256):
        cols = slice(start, start + 256)
        act, grow = gelu_pair(dot(ff_in[...], w_up[:, cols]))
        act = act.astype(LOW)
        active[:, cols] = act
        slope[:, cols] = grow.astype(LOW)
        term = dot(act, w_down[cols, :])
        total = term if total is None else total + term
    after[...] = mid[...] + total
    after_low[...] = total.astype(LOW)


def decoder_kernel(
    rows_count,
    after_part, came, gain_final, enc_ids, dec_ids, cross_queries, dec_mid, gain_ff, cot_own, cot_other,
    key_hbm, value_hbm, mix_hbm, up_hbm, down_hbm,
    enc_result, after, state, keys, values, probs, mixed, dec_result, stream, gain_grad, cross, payload,
    cot, out, before_grad, w_key, w_value, w_mix, w_up, w_down, active, sems,
):
    core = lax.axis_index("seq")
    fetch = Fetch(sems)
    copies = [
        fetch(source, target)
        for source, target in (
            (key_hbm, w_key), (value_hbm, w_value), (mix_hbm, w_mix), (up_hbm, w_up), (down_hbm, w_down),
        )
    ]
    length = dec_mid.shape[0]
    half, enc_half = length // 2, after.shape[0] // 2
    for part, at in ((cot_own, core), (cot_other, 1 - core)):
        cot[aligned(at, half), :] = part[...]
    after[...] = after_part[...] + came[...].astype(FULL)
    enc_result[...] = after[aligned(core, enc_half), :]
    state[...] = normed(after[...], gain_final[...])
    _, key_marks = doc_marks(enc_ids[...])
    query_marks, _ = doc_marks(dec_ids[...])
    copies[0].wait()
    keys[...] = dot(state[...], w_key[...]).astype(LOW)
    copies[1].wait()
    values[...] = dot(state[...], w_value[...]).astype(LOW)
    for p in range(HEADS // 2):
        query_pair, key_pair, value_pair = cross_queries[:, pair(p)], keys[:, pair(p)], values[:, pair(p)]
        halves = []
        for odd in range(2):
            scores = dot_cols(of_head(query_pair, query_marks, odd), of_head(key_pair, key_marks, odd))
            weights = softmax(scores)
            probs[2 * p + odd] = weights
            halves.append(dot(weights, value_pair))
        mixed[:, pair(p)] = of_head(halves[0], halves[1], 0).astype(LOW)
    copies[2].wait()
    cross[...] = dec_mid[...] + dot(mixed[...], w_mix[...])
    ff_in = normed(cross[...], gain_ff[...])
    copies[3].wait()
    copies[4].wait()
    total = cross[...]
    normed_grad = jnp.zeros_like(total)
    for start in range(0, FF, 512):
        cols = slice(start, start + 512)
        act, grow = gelu_pair(dot(ff_in, w_up[:, cols]))
        act = act.astype(LOW)
        active[:, cols] = act
        total = total + dot(act, w_down[cols, :])
        grad = (grow * dot_cols(cot[...], w_down[cols, :])).astype(LOW)
        before_grad[:, cols] = grad
        normed_grad = normed_grad + dot_cols(grad, w_up[:, cols])
    out[...] = total
    dec_result[...] = out[aligned(core, half), :]
    shares = Shares(rows_count, payload)
    for start in range(0, FF // 2, LANES):
        shares.put(dot_rows(ff_in, before_grad[:, pl.ds(pl.multiple_of(core * (FF // 2) + start, LANES), LANES)]))
    shares.put(dot_rows(active[...], cot[:, aligned(core, LANES)]))
    back, gain_grad[...] = norm_back(cross[...], gain_ff[...], normed_grad)
    stream[...] = cot[...].astype(FULL) + back


def cross_back_kernel(
    rows_count,
    stream, dec_mid, gain_cross, cross_in, queries, keys, values, probs, mixed, state, after, gain_final,
    query_hbm, key_hbm, value_hbm, mix_hbm,
    enc_stream, enc_low, gain_final_grad, stream_out, gain_grad, payload,
    w_query, w_key, w_value, w_mix, low, query_grad, key_grad, value_grad, score_grads, sems,
):
    core = lax.axis_index("seq")
    fetch = Fetch(sems)
    copies = [
        fetch(source, target)
        for source, target in ((mix_hbm, w_mix), (key_hbm, w_key), (value_hbm, w_value), (query_hbm, w_query))
    ]
    shares = Shares(rows_count, payload)
    low[...] = stream[...].astype(LOW)
    copies[0].wait()
    mixed_grad = dot_cols(low[...], w_mix[...]).astype(LOW)
    for p in range(HEADS // 2):
        query_pair, key_pair, value_pair = queries[:, pair(p)], keys[:, pair(p)], values[:, pair(p)]
        grad_pair = mixed_grad[:, pair(p)]
        found = []
        for odd in range(2):
            weights = probs[2 * p + odd]
            grad_head = of_head(grad_pair, jnp.zeros_like(grad_pair), odd)
            score_grad = score_back(weights, dot_cols(grad_head, value_pair))
            found.append(
                (dot(score_grad, key_pair), dot_rows(score_grad, query_pair), dot_rows(weights, grad_pair))
            )
        for target, even, odd in zip((query_grad, key_grad, value_grad), *found):
            target[:, pair(p)] = of_head(even, odd, 0).astype(LOW)
    copies[1].wait()
    copies[2].wait()
    state_grad = dot_cols(key_grad[...], w_key[...]) + dot_cols(value_grad[...], w_value[...])
    back, gain_final_grad[...] = norm_back(after[...], gain_final[...], state_grad)
    enc_stream[...] = back
    enc_low[...] = back.astype(LOW)
    copies[3].wait()
    back, gain_grad[...] = norm_back(dec_mid[...], gain_cross[...], dot_cols(query_grad[...], w_query[...]))
    stream_out[...] = stream[...] + back
    own = aligned(core, LANES)
    shares.put(dot_rows(cross_in[...], query_grad[:, own]))
    shares.put(dot_rows(state[...], key_grad[:, own]))
    shares.put(dot_rows(state[...], value_grad[:, own]))
    shares.put(dot_rows(mixed[...], low[:, own]))


def dec_back_kernel(
    rows_count,
    stream, x_own, x_other, gain, x_normed, queries, keys, values, probs, mixed,
    query_hbm, key_hbm, value_hbm, mix_hbm,
    input_grad, gain_grad, table_grad, squares, payload,
    w_query, w_key, w_value, w_mix, low, query_grad, key_grad, value_grad, sums, x_all, total, sems,
):
    core = lax.axis_index("seq")
    fetch = Fetch(sems)
    copies = [
        fetch(source, target)
        for source, target in ((mix_hbm, w_mix), (query_hbm, w_query), (key_hbm, w_key), (value_hbm, w_value))
    ]
    shares = Shares(rows_count, payload)
    half = x_own.shape[0]
    length = 2 * half
    for part, at in ((x_own, core), (x_other, 1 - core)):
        x_all[aligned(at, half), :] = part[...].astype(FULL)
    low[...] = stream[...].astype(LOW)
    copies[0].wait()
    mixed_grad = dot_cols(low[...], w_mix[...]).astype(LOW)
    period = 2 * BLOCK
    for p in range(HEADS // 2):
        query_pair, key_pair, value_pair = queries[:, pair(p)], keys[:, pair(p)], values[:, pair(p)]
        grad_pair = mixed_grad[:, pair(p)]
        found = []
        for odd in range(2):
            weights = probs[2 * p + odd]
            grad_head = of_head(grad_pair, jnp.zeros_like(grad_pair), odd)
            score_grad = score_back(weights, dot_cols(grad_head, value_pair))
            found.append(
                (dot(score_grad, key_pair), dot_rows(score_grad, query_pair), dot_rows(weights, grad_pair))
            )
            wide = jnp.concatenate([score_grad.astype(FULL), jnp.zeros((BLOCK, BLOCK), FULL)], axis=1)
            sums[2 * p + odd : 2 * p + odd + 1, :] = unsheared(wide, period)
        for target, even, odd in zip((query_grad, key_grad, value_grad), *found):
            target[:, pair(p)] = of_head(even, odd, 0).astype(LOW)
    table_grad[...] = dot(sums[...], offsets(0, period, False), ((1,), (1,)), HIGH)
    for copy in copies[1:]:
        copy.wait()
    normed_grad = (
        dot_cols(query_grad[...], w_query[...])
        + dot_cols(key_grad[...], w_key[...])
        + dot_cols(value_grad[...], w_value[...])
    )
    back, gain_grad[...] = norm_back(x_all[...], gain[...], normed_grad)
    total[...] = stream[...] + back
    input_grad[...] = total[aligned(core, half), :]
    squares[...] = jnp.sum(total[...] * total[...], axis=0, keepdims=True)
    own = aligned(core, LANES)
    for grad in (query_grad, key_grad, value_grad):
        shares.put(dot_rows(x_normed[...], grad[:, own]))
    shares.put(dot_rows(mixed[...], low[:, own]))


def enc_ff_back_kernel(
    low, slope, up_hbm, down_hbm,
    before_grad, part, part_low,
    w_up, w_down, sems,
):
    core = lax.axis_index("seq")
    fetch = Fetch(sems)
    hidden = w_up.shape[1]
    copies = [
        fetch(down_hbm.at[aligned(core, hidden), :], w_down),
        fetch(up_hbm.at[:, aligned(core, hidden)], w_up),
    ]
    for copy in copies:
        copy.wait()
    total = None
    for start in range(0, hidden, 256):
        cols = slice(start, start + 256)
        grad = (slope[:, cols].astype(FULL) * dot_cols(low[...], w_down[cols, :])).astype(LOW)
        before_grad[:, cols] = grad
        term = dot_cols(grad, w_up[:, cols])
        total = term if total is None else total + term
    part[...] = total
    part_low[...] = total.astype(LOW)


def enc_ff_weights_kernel(rows_count, ff_in, before_grad, active_own, active_other, low, payload, both):
    core = lax.axis_index("seq")
    shares = Shares(rows_count, payload)
    for start in range(0, before_grad.shape[1], LANES):
        shares.put(dot_rows(ff_in[...], before_grad[:, start : start + LANES]))
    hidden = active_own.shape[1]
    own = low[:, aligned(core, LANES)]
    both[aligned(core, hidden), :] = dot_rows(active_own[...], own)
    both[aligned(1 - core, hidden), :] = dot_rows(active_other[...], own)
    shares.put(both[...])


def enc_attention_back_kernel(
    part, came, mid, gain, stream, mix_hbm, queries, keys, values, probs, query_hbm, key_hbm, value_hbm,
    low, stream_out, gain_grad, query_grad, key_grad, value_grad, table_grad, normed_part, normed_low,
    w_mix, w_query, w_key, w_value, score_grads, diagonals, sums, sems,
):
    core = lax.axis_index("seq")
    fetch = Fetch(sems)
    width = w_query.shape[1]
    copies = [fetch(mix_hbm.at[aligned(core, width), :], w_mix)] + [
        fetch(source.at[:, aligned(core, width)], target)
        for source, target in ((query_hbm, w_query), (key_hbm, w_key), (value_hbm, w_value))
    ]
    length = mid.shape[0]
    span, period = length - BLOCK, 2 * length
    normed_grad = part[...] + came[...].astype(FULL)
    back, gain_grad[...] = norm_back(mid[...], gain[...], normed_grad)
    stream_out[...] = stream[...] + back
    low[...] = stream_out[...].astype(LOW)
    copies[0].wait()
    mixed_grad = dot_cols(low[...], w_mix[...]).astype(LOW)
    sums[...] = jnp.zeros_like(sums)
    for p in range(width // (2 * HEAD)):
        query_pair, key_pair, value_pair = queries[:, pair(p)], keys[:, pair(p)], values[:, pair(p)]
        grad_pair = mixed_grad[:, pair(p)]
        found = []
        for odd in range(2):
            head = 2 * p + odd
            grad_head = of_head(grad_pair, jnp.zeros_like(grad_pair), odd)
            diagonals[...] = jnp.zeros_like(diagonals)
            for block in range(length // BLOCK):
                rows = slice(block * BLOCK, (block + 1) * BLOCK)
                score_grad = score_back(probs[head, rows, :], dot_cols(grad_head[rows], value_pair))
                score_grads[rows, :] = score_grad
                first = span - block * BLOCK
                diagonals[:, first : first + length] += score_grad.astype(FULL)
            sums[pl.ds(core * (HEADS // 2) + head, 1), :] = unsheared(diagonals[...], period)
            found.append(
                (
                    dot(score_grads[...], key_pair),
                    dot_rows(score_grads[...], query_pair),
                    dot_rows(probs[head], grad_pair),
                )
            )
        for target, even, odd in zip((query_grad, key_grad, value_grad), *found):
            target[:, pair(p)] = of_head(even, odd, 0).astype(LOW)
    table_grad[...] = dot(sums[...], offsets(span, period, True), ((1,), (1,)), HIGH)
    for copy in copies[1:]:
        copy.wait()
    normed_part[...] = (
        dot_cols(query_grad[...], w_query[...])
        + dot_cols(key_grad[...], w_key[...])
        + dot_cols(value_grad[...], w_value[...])
    )
    normed_low[: length, :] = normed_part[...].astype(LOW)
    normed_low[length:, :] = jnp.zeros((normed_low.shape[0] - length, D), LOW)
    normed_low[length : length + HEADS, :BUCKETS] = table_grad[...].astype(LOW)


def enc_finish_kernel(
    rows_count,
    normed_part, came, stream, x_own, x_other, gain, x_normed, query_grad, key_grad, value_grad,
    mixed_own, mixed_other, low, table_enc, table_dec, dec_squares,
    g_ff, g_final, g_self, g_cross, g_dec_ff,
    input_grad, row_norm, payload, small,
    x_all, total, both,
):
    core = lax.axis_index("seq")
    shares = Shares(rows_count, payload)
    half = x_own.shape[0]
    length = 2 * half
    for part, at in ((x_own, core), (x_other, 1 - core)):
        x_all[aligned(at, half), :] = part[...].astype(FULL)
    for grad in (query_grad, key_grad, value_grad):
        shares.put(dot_rows(x_normed[...], grad[...]))
    width = mixed_own.shape[1]
    own = low[:, aligned(core, LANES)]
    both[aligned(core, width), :] = dot_rows(mixed_own[...], own)
    both[aligned(1 - core, width), :] = dot_rows(mixed_other[...], own)
    shares.put(both[...])
    normed_grad = normed_part[...] + came[:length, :].astype(FULL)
    back, gain_grad = norm_back(x_all[...], gain[...], normed_grad)
    total[...] = stream[...] + back
    input_grad[...] = total[aligned(core, half), :]
    squares = jnp.sum(total[...] * total[...], axis=0, keepdims=True) + dec_squares[...]
    row_norm[...] = jnp.sqrt(jnp.sum(squares, axis=1, keepdims=True))
    small[...] = jnp.zeros_like(small)
    small[:HEADS, :BUCKETS] = table_enc[...] + came[length : length + HEADS, :BUCKETS].astype(FULL)
    small[:HEADS, BLOCK : BLOCK + BUCKETS] = table_dec[...]
    for row, grad in enumerate(
        (gain_grad, g_ff[...], g_final[...], g_self[...], g_cross[...], g_dec_ff[...])
    ):
        for part in range(2):
            small[HEADS + 2 * row + part : HEADS + 2 * row + part + 1, :] = grad[:, part * LANES : (part + 1) * LANES]


SMALL = 32


def on_device(
    rows_count,
    enc_input,
    dec_input,
    enc_segments,
    dec_segments,
    cotangent,
    enc_norm_attn,
    enc_query,
    enc_key,
    enc_value,
    enc_mix,
    enc_table,
    enc_norm_ff,
    enc_up,
    enc_down,
    enc_norm_final,
    dec_norm_self,
    dec_query,
    dec_key,
    dec_value,
    dec_mix,
    dec_table,
    dec_norm_cross,
    cross_query,
    cross_key,
    cross_value,
    cross_mix,
    dec_norm_ff,
    dec_up,
    dec_down,
):
    orders = bit_orders(rows_count)
    chip, core = lax.axis_index("rows"), lax.axis_index("seq")
    x_own, d_own, c_own = enc_input[0], dec_input[0], cotangent[0]
    half, d_half = x_own.shape[0], d_own.shape[0]
    enc, dec = 2 * half, 2 * d_half
    width, hidden = D // 2, FF // 2

    def swap(values):
        return lax.ppermute(values, "seq", [(0, 1), (1, 0)])

    def row(gain):
        return gain.reshape(1, -1)

    def v(*arrays):
        return [(array, "vmem") for array in arrays]

    def h(*arrays):
        return [(array, "hbm") for array in arrays]

    square = (D, D)
    ordered = in_order(rows_count)

    def payload_shape(lead_total):
        if ordered:
            return ((rows_count, lead_total // rows_count, LANES), LOW)
        return ((1, lead_total, LANES), LOW)

    x_other, d_other, c_other = swap(x_own), swap(d_own), swap(c_own)

    mixed, probs, queries, keys, values, x_normed = call(
        enc_attention_kernel,
        v(x_own, x_other, row(enc_norm_attn), enc_segments, enc_table) + h(enc_query, enc_key, enc_value),
        [
            ((enc, width), LOW), ((HEADS // 2, enc, enc), LOW),
            ((enc, width), LOW), ((enc, width), LOW), ((enc, width), LOW), ((enc, D), LOW),
        ],
        [((D, width), LOW)] * 3 + [((HEADS, 2 * enc), FULL)],
        flops=2 * enc * D * width * 3 + 16 * enc * enc * HEAD * 4,
        n_sems=3, name="enc_attention",
    )
    mixed_other = swap(mixed)
    d_probs, d_queries, d_keys, d_values, d_normed, d_mixed, d_mid, cross_in, cross_queries = call(
        dec_attention_kernel,
        v(d_own, d_other, row(dec_norm_self), dec_segments, dec_table)
        + h(dec_query, dec_key, dec_value, dec_mix) + v(row(dec_norm_cross)) + h(cross_query),
        [((HEADS, dec, dec), LOW)] + [((dec, D), LOW)] * 5 + [((dec, D), FULL)] + [((dec, D), LOW)] * 2,
        [((dec, D), FULL)] + [(square, LOW)] * 5,
        flops=2 * dec * D * D * 5 * 2, n_sems=5, name="dec_attention",
    )
    mid, after_part, after_low, active, slope, ff_in = call(
        enc_ff_kernel,
        v(x_own, x_other, mixed, mixed_other) + h(enc_mix) + v(row(enc_norm_ff)) + h(enc_up, enc_down),
        [((enc, D), FULL), ((enc, D), FULL), ((enc, D), LOW), ((enc, hidden), LOW), ((enc, hidden), LOW), ((enc, D), LOW)],
        [((width, D), LOW)] * 2 + [((D, hidden), LOW), ((hidden, D), LOW)],
        flops=2 * enc * D * (D + 2 * hidden), n_sems=4, name="enc_ff",
    )
    after_came, active_other = swap(after_low), swap(active)
    (
        enc_result, after, state, c_keys, c_values, c_probs, c_mixed, dec_result, stream, g_dec_ff, cross, pay_dec_ff,
    ) = call(
        functools.partial(decoder_kernel, rows_count),
        v(after_part, after_came, row(enc_norm_final), enc_segments, dec_segments, cross_queries, d_mid,
          row(dec_norm_ff), c_own, c_other)
        + h(cross_key, cross_value, cross_mix, dec_up, dec_down),
        [
            ((half, D), FULL), ((enc, D), FULL), ((enc, D), LOW), ((enc, D), LOW), ((enc, D), LOW),
            ((HEADS, dec, enc), LOW), ((dec, D), LOW), ((d_half, D), FULL), ((dec, D), FULL), ((1, D), FULL),
            ((dec, D), FULL), payload_shape(4 * D + FF),
        ],
        [((dec, D), LOW), ((dec, D), FULL), ((dec, FF), LOW)] + [(square, LOW)] * 3
        + [((D, FF), LOW), ((FF, D), LOW), ((dec, FF), LOW)],
        flops=2 * enc * D * D * 2 + 2 * dec * D * FF * 8, n_sems=5, name="decoder",
    )
    enc_stream, enc_low, g_final, stream, g_cross, pay_cross = call(
        functools.partial(cross_back_kernel, rows_count),
        v(stream, d_mid, row(dec_norm_cross), cross_in, cross_queries, c_keys, c_values, c_probs, c_mixed, state, after,
          row(enc_norm_final))
        + h(cross_query, cross_key, cross_value, cross_mix),
        [((enc, D), FULL), ((enc, D), LOW), ((1, D), FULL), ((dec, D), FULL), ((1, D), FULL), payload_shape(4 * D)],
        [(square, LOW)] * 4 + [((dec, D), LOW), ((dec, D), LOW), ((enc, D), LOW), ((enc, D), LOW), ((dec, enc), LOW)],
        flops=2 * enc * D * D * 6, n_sems=4, name="cross_back",
    )
    before_grad, part, part_low = call(
        enc_ff_back_kernel,
        v(enc_low, slope) + h(enc_up, enc_down),
        [((enc, hidden), LOW), ((enc, D), FULL), ((enc, D), LOW)],
        [((D, hidden), LOW), ((hidden, D), LOW)],
        flops=2 * enc * D * hidden * 2, n_sems=2, name="enc_ff_back",
    )
    part_came = swap(part_low)
    (pay_enc_ff,) = call(
        functools.partial(enc_ff_weights_kernel, rows_count),
        v(ff_in, before_grad, active, active_other, enc_low),
        [payload_shape(4 * D + FF)],
        [((FF, LANES), FULL)],
        flops=2 * enc * D * FF * 2, name="enc_ff_weights",
    )
    low, enc_stream, g_ff, query_grad, key_grad, value_grad, table_enc, normed_part, normed_low = call(
        enc_attention_back_kernel,
        v(part, part_came, mid, row(enc_norm_ff), enc_stream) + h(enc_mix) + v(queries, keys, values, probs)
        + h(enc_query, enc_key, enc_value),
        [
            ((enc, D), LOW), ((enc, D), FULL), ((1, D), FULL), ((enc, width), LOW), ((enc, width), LOW),
            ((enc, width), LOW), ((HEADS, BUCKETS), FULL), ((enc, D), FULL), ((enc + 16, D), LOW),
        ],
        [((width, D), LOW)] + [((D, width), LOW)] * 3
        + [((enc, enc), LOW), ((BLOCK, 2 * enc), FULL), ((HEADS, 2 * enc), FULL)],
        flops=2 * enc * D * width * 4 + 2 * enc * enc * 128 * 16, n_sems=4, name="enc_attention_back",
    )
    normed_came = swap(normed_low)
    dec_input_grad, g_self, table_dec, dec_squares, pay_dec = call(
        functools.partial(dec_back_kernel, rows_count),
        v(stream, d_own, d_other, row(dec_norm_self), d_normed, d_queries, d_keys, d_values, d_probs, d_mixed)
        + h(dec_query, dec_key, dec_value, dec_mix),
        [((d_half, D), FULL), ((1, D), FULL), ((HEADS, BUCKETS), FULL), ((1, D), FULL), payload_shape(4 * D)],
        [(square, LOW)] * 4 + [((dec, D), LOW)] * 4 + [((HEADS, 2 * BLOCK), FULL), ((dec, D), FULL), ((dec, D), FULL)],
        flops=2 * dec * D * D * 8 * 2, n_sems=4, name="dec_back",
    )
    enc_input_grad, row_norm, pay_enc, small = call(
        functools.partial(enc_finish_kernel, rows_count),
        v(normed_part, normed_came, enc_stream, x_own, x_other, row(enc_norm_attn), x_normed, query_grad, key_grad,
          value_grad, mixed, mixed_other, low, table_enc, table_dec, dec_squares, g_ff, g_final, g_self, g_cross,
          g_dec_ff),
        [((half, D), FULL), ((1, 1), FULL), payload_shape(4 * D), ((SMALL, LANES), FULL)],
        [((enc, D), FULL), ((enc, D), FULL), ((D, LANES), FULL)],
        flops=2 * enc * D * D * 2, name="enc_finish",
    )

    def arranged(payload, leads):
        if ordered:
            return payload
        places = jnp.array([[chunk_of(q, order) for q in range(rows_count)] for order in orders], jnp.int32)
        parts, start = [], 0
        for lead in leads:
            parts.append(payload[0, start : start + lead].reshape(rows_count, -1, LANES))
            start += lead
        return jnp.take(jnp.concatenate(parts, 1), places[core] ^ chip, axis=0)

    def summed(held, extra=None):
        for stage in range(len(orders[0])):
            n, lead, _ = held.shape
            pairs = [
                (at * 2 + c, (at ^ (1 << orders[c][stage])) * 2 + c)
                for at in range(rows_count)
                for c in range(2)
            ]
            sent = held[n // 2 :].reshape(-1, LANES)
            if extra is not None:
                sent = jnp.concatenate([sent, extra.astype(LOW)], 0)
            came = lax.ppermute(sent, ("rows", "seq"), pairs).astype(FULL)
            if extra is not None:
                extra = extra + came[n // 2 * lead :]
            held = held[: n // 2].astype(FULL) + came[: n // 2 * lead].reshape(n // 2, lead, LANES)
            if n > 2:
                held = held.astype(LOW)
        return held[0], extra

    square_leads, ff_leads = [D] * 4, [D] * 4 + [FF]
    sum_dec_ff, _ = summed(arranged(pay_dec_ff, ff_leads))
    sum_cross, _ = summed(arranged(pay_cross, square_leads))
    sum_dec, _ = summed(arranged(pay_dec, square_leads))
    sum_enc_ff, _ = summed(arranged(pay_enc_ff, ff_leads))
    sum_enc, small = summed(arranged(pay_enc, square_leads), small)

    lead = D // rows_count

    def squares_of(total):
        return [total[i * lead : (i + 1) * lead] for i in range(4)]

    def ff_of(total):
        return jnp.concatenate(squares_of(total), axis=1), total[4 * lead :]

    gains = small[HEADS : HEADS + 12].reshape(6, D)
    gains = lax.dynamic_slice_in_dim(gains, chip * lead, lead, 1)
    tables = [small[:HEADS, :BUCKETS].T, small[:HEADS, BLOCK : BLOCK + BUCKETS].T]
    enc_q, enc_k, enc_v, enc_m = squares_of(sum_enc)
    dec_q, dec_k, dec_v, dec_m = squares_of(sum_dec)
    cross_q, cross_k, cross_v, cross_m = squares_of(sum_cross)
    enc_u, enc_d = ff_of(sum_enc_ff)
    dec_u, dec_d = ff_of(sum_dec_ff)
    return (
        enc_result[None], dec_result[None], enc_input_grad[None], dec_input_grad[None], row_norm[0],
        gains[0], enc_q, enc_k, enc_v, enc_m, tables[0], gains[1], enc_u, enc_d, gains[2],
        gains[3], dec_q, dec_k, dec_v, dec_m, tables[1], gains[4], cross_q, cross_k, cross_v, cross_m,
        gains[5], dec_u, dec_d,
    )


def solution(mesh):
    split, line, copied = P("rows", "seq", None), P("rows", None), P()
    in_specs = (split, split, line, line, split) + (copied,) * 24
    block, vector = P("rows", "seq"), P("rows")
    out_specs = (
        (split,) * 4 + (vector,)
        + (vector,) + (block,) * 4 + (copied, vector, block, block, vector)
        + (vector,) + (block,) * 4 + (copied, vector) + (block,) * 4 + (vector, block, block)
    )
    return jax.shard_map(
        functools.partial(on_device, mesh.shape["rows"]),
        mesh=mesh, in_specs=in_specs, out_specs=out_specs, check_vma=False,
    )
```

```python
import functools
import math

import jax
import jax.numpy as jnp
from jax import lax
from jax.experimental import pallas as pl
from jax.experimental.pallas import tpu as pltpu
from jax.sharding import PartitionSpec as P

D = 512
HEADS = 8
HEAD = 64
FF = 2048
BUCKETS = 32
MAX_DIST = 128
NDOC = 4
EPSILON = 1e-06
NEGATIVE = -1e30
BLOCK = 128
LANES = 256

LOW = jnp.bfloat16
FULL = jnp.float32
HIGH = lax.Precision.HIGHEST


def cut_points(exact_span, bucket_half, reach):
    points = []
    for target in range(exact_span + 1, bucket_half):
        reach_at = exact_span
        while (
            exact_span
            + int(
                math.log(reach_at / exact_span)
                / math.log(reach / exact_span)
                * (bucket_half - exact_span)
            )
            < target
        ):
            reach_at += 1
        points.append(reach_at)
    return points


def bucket_index(offset, both_ways):
    if both_ways:
        bucket_half = BUCKETS // 2
        base_index = jnp.where(offset > 0, bucket_half, 0).astype(jnp.int32)
        distance = jnp.abs(offset)
    else:
        bucket_half = BUCKETS
        base_index = jnp.zeros_like(offset)
        distance = jnp.maximum(-offset, 0)
    exact_span = bucket_half // 2
    result = base_index + jnp.minimum(distance, exact_span)
    for border in cut_points(exact_span, bucket_half, MAX_DIST):
        result = result + (distance >= border).astype(jnp.int32)
    return result


def dot(left, right, dims=((1,), (0,)), precision=None):
    return lax.dot_general(
        left, right, (dims, ((), ())), preferred_element_type=FULL, precision=precision
    )


def dot_cols(left, right):
    return dot(left, right, ((1,), (1,)))


def dot_rows(left, right):
    return dot(left, right, ((0,), (0,)))


def scale_of(values):
    return lax.rsqrt(jnp.mean(values * values, axis=-1, keepdims=True) + EPSILON)


def normed(values, gain):
    return (values * scale_of(values) * gain).astype(LOW)


def norm_back(values, gain, grad):
    scale = scale_of(values)
    unit = values * scale
    gain_grad = jnp.sum(grad * unit, axis=0, keepdims=True)
    grad = grad * gain
    return scale * (grad - unit * jnp.mean(grad * unit, axis=-1, keepdims=True)), gain_grad


def gelu_pair(values):
    root = math.sqrt(2.0 / math.pi)
    square = values * values
    tanh = jnp.tanh(root * values * (1.0 + 0.044715 * square))
    half = 0.5 + 0.5 * tanh
    slope = half + 0.5 * values * (1.0 - tanh * tanh) * (root + (3 * 0.044715 * root) * square)
    return values * half, slope


def iota(shape, axis):
    return lax.broadcasted_iota(jnp.int32, shape, axis)


def offsets(span, period, both_ways):
    place = iota((1, period), 1)
    offset = span - jnp.where(place < period - BLOCK, place, place - period)
    return (bucket_index(offset, both_ways) == iota((BUCKETS, period), 0)).astype(FULL)


def sheared(row, period):
    return pltpu.roll(
        jnp.broadcast_to(row, (BLOCK, period)), 0, 1, stride=1, stride_axis=0
    )


def unsheared(sums, period):
    rows = sums.shape[0]
    while rows > 8:
        rows //= 2
        sums = sums[:rows] + pltpu.roll(sums[rows:], period - rows, 1)
    total = sums[:1]
    for row in range(1, 8):
        total = total + pltpu.roll(sums[row : row + 1], period - row, 1)
    return total


def doc_columns(ids):
    wide = jnp.broadcast_to(ids.astype(FULL), (BLOCK, ids.shape[1]))
    return jnp.transpose(wide)


def doc_marks(ids):
    columns = doc_columns(ids)
    lane = iota(columns.shape, 1)
    same = columns == lane.astype(FULL)
    query_marks = jnp.where((lane < NDOC) & jnp.logical_not(same), NEGATIVE, 0.0).astype(LOW)
    return query_marks, same.astype(FULL).astype(LOW)


def apart(values):
    lane = iota(values.shape, 1)
    zeros = jnp.zeros_like(values)
    return jnp.concatenate([jnp.where(lane < HEAD, values, zeros), jnp.where(lane >= HEAD, values, zeros)], 0)


def pair_scores(key_pair, query_pair, key_marks, query_marks):
    left = jnp.concatenate([key_pair, key_marks], 1)
    right = jnp.concatenate([apart(query_pair), jnp.concatenate([query_marks, query_marks], 0)], 1)
    return dot_cols(left, right)


def put_pair(target, p, both):
    length = both.shape[1] // 2
    target[one(2 * p), :] = both[:HEAD, :length].astype(LOW)
    target[one(2 * p + 1), :] = both[HEAD:, length:].astype(LOW)


def softmax(scores):
    weights = jnp.exp(scores - jnp.max(scores, axis=0, keepdims=True))
    return (weights * (1.0 / jnp.sum(weights, axis=0, keepdims=True))).astype(LOW)


def score_back(probs, probs_grad):
    probs = probs.astype(FULL)
    inner = jnp.sum(probs * probs_grad, axis=0, keepdims=True)
    return (probs * (probs_grad - inner)).astype(LOW)


def one(head):
    return slice(head * HEAD, (head + 1) * HEAD)


def pair(index):
    return slice(index * 2 * HEAD, (index + 1) * 2 * HEAD)


def aligned(index, size):
    return pl.ds(pl.multiple_of(index * size, size), size)


class Lazy:
    def __init__(self, ref, copy):
        self.ref, self.copy = ref, copy

    @property
    def shape(self):
        return self.ref.shape

    def __getitem__(self, index):
        if self.copy is not None:
            self.copy.wait()
            self.copy = None
        return self.ref[index]


def cut(source, mode):
    if mode == "all":
        return source
    core = lax.axis_index("seq")
    rows, cols = source.shape
    at = 1 - core if mode.endswith("other") else core
    if mode.startswith("cols"):
        return source.at[:, aligned(at, cols // 2)]
    return source.at[aligned(at, rows // 2), :]


def cut_shape(shape, mode):
    if mode == "all":
        return shape
    return (shape[0], shape[1] // 2) if mode.startswith("cols") else (shape[0] // 2, shape[1])


def bit_orders(rows_count, late=True):
    plain = list(range(rows_count.bit_length() - 1))
    if len(plain) < 3:
        return (plain, plain)
    if late:
        return (plain, [1, 0] + plain[2:])
    return ([2, 0, 1] + plain[3:], [2, 1, 0] + plain[3:])


def place_of(chunk, order):
    bits = len(order)
    return sum(((chunk >> order[s]) & 1) << (bits - 1 - s) for s in range(bits))


def chunk_of(place, order):
    bits = len(order)
    return sum(((place >> (bits - 1 - s)) & 1) << order[s] for s in range(bits))


def in_order(rows_count):
    return (D // rows_count) % 16 == 0


class Shares:
    def __init__(self, rows_count, payload, late=True):
        self.rows_count, self.payload, self.row = rows_count, payload, 0
        core, chip = lax.axis_index("seq"), lax.axis_index("rows")
        orders = bit_orders(rows_count, late)
        own = [place_of(chip, order) for order in orders]
        self.places = [
            jnp.where(core == 0, place_of(chunk, orders[0]) ^ own[0], place_of(chunk, orders[1]) ^ own[1])
            for chunk in range(rows_count)
        ] if in_order(rows_count) else [0]

    def put(self, grad):
        chunks = len(self.places)
        lead = grad.shape[0] // chunks
        for chunk in range(chunks):
            self.payload[self.places[chunk], self.row : self.row + lead, :] = grad[
                chunk * lead : (chunk + 1) * lead
            ].astype(LOW)
        self.row += lead

    def split(self, kept, sent):
        if not in_order(self.rows_count):
            kept[: self.row] = self.payload[0]
            return
        half = self.rows_count // 2
        shape = (half * self.row, LANES)
        sent[: half * self.row] = self.payload[half:].reshape(shape)
        kept[: half * self.row] = self.payload[:half].reshape(shape)


VMEM = pl.BlockSpec(memory_space=pltpu.VMEM)
HBM = pl.BlockSpec(memory_space=pltpu.HBM)
ANY = pl.BlockSpec(memory_space=pl.ANY)
MIB = 1024 * 1024


def call(token, kernel, ins, outs, scratch=(), cost=0.0, limit=24, name=None, after=(), through=()):
    n_ins, n_outs = len(ins), len(outs)
    ins = list(ins) + [(token, "vmem")] * (token is not None) + [(array, "any") for array in (*after, *through)]
    outs = list(outs) + [(array.shape, array.dtype) for array in through] + [((8, BLOCK), FULL)]
    specs = [{"vmem": VMEM, "any": ANY}.get(how, HBM) for _, how in ins]
    arrays = [
        array if how in ("vmem", "any") else pltpu.with_memory_space_constraint(array, pltpu.HBM) for array, how in ins
    ]
    shapes = [jax.ShapeDtypeStruct(shape, kind) for shape, kind in outs]
    lazy = [i for i, (_, how) in enumerate(ins) if how not in ("vmem", "any")]
    scratch = [pltpu.VMEM(shape, kind) for shape, kind in scratch]
    n_own = len(scratch)
    scratch += [pltpu.VMEM(cut_shape(arrays[i].shape, ins[i][1]), arrays[i].dtype) for i in lazy]
    if lazy:
        scratch.append(pltpu.SemaphoreType.DMA((len(lazy),)))

    def body(*refs):
        operands = list(refs[: len(ins)])
        rest = refs[len(ins) :]
        results, own = rest[: len(outs)], rest[len(outs) : len(outs) + n_own]
        landing = rest[len(outs) + n_own :]
        for place, i in enumerate(lazy):
            copy = pltpu.make_async_copy(cut(operands[i], ins[i][1]), landing[place], landing[-1].at[place])
            copy.start()
            operands[i] = Lazy(landing[place], copy)
        results[-1][...] = jnp.zeros((8, BLOCK), FULL)
        kernel(*operands[:n_ins], *results[: n_outs], *own)
        for i in lazy:
            if operands[i].copy is not None:
                operands[i].copy.wait()

    found = pl.pallas_call(
        body,
        out_shape=shapes,
        in_specs=specs,
        out_specs=[VMEM] * n_outs + [ANY] * len(through) + [VMEM],
        input_output_aliases={len(ins) - len(through) + i: n_outs + i for i in range(len(through))},
        scratch_shapes=scratch,
        compiler_params=pltpu.CompilerParams(vmem_limit_bytes=limit * MIB),
        cost_estimate=pl.CostEstimate(
            flops=1000 + int(cost * 1.15e9), bytes_accessed=1000, transcendentals=0
        ),
        name=name,
    )(*arrays)
    return found[-1], found[:-1]


def enc_attention_kernel(
    x_own, x_other, gain, ids, table, w_query, w_key, w_value,
    mixed, probs, queries, keys, values, x_normed,
    biases,
):
    core = lax.axis_index("seq")
    width = w_query.shape[1]
    half = x_own.shape[0]
    length = 2 * half
    for part, at in ((x_own, core), (x_other, 1 - core)):
        x_normed[aligned(at, half), :] = normed(part[...].astype(FULL), gain[...])
    span, period = length - BLOCK, 2 * length
    biases[...] = dot(table[...], offsets(span, period, True), precision=HIGH)
    query_marks, key_marks = doc_marks(ids[...])
    for weight, target in zip((w_query, w_key, w_value), (queries, keys, values)):
        target[...] = dot(x_normed[...], weight[...]).astype(LOW)
    values_t = jnp.transpose(values[...])
    for p in range(HEADS // 4):
        shift = []
        for head in (2 * p, 2 * p + 1):
            bias = sheared(biases[pl.ds(core * (HEADS // 2) + head, 1), :], period)
            shift.append(jnp.concatenate([bias[:, span - key : span - key + length] for key in range(0, length, BLOCK)], 0))
        scores = pair_scores(keys[:, pair(p)], queries[:, pair(p)], key_marks, query_marks)
        weights = softmax(scores + jnp.concatenate(shift, 1))
        probs[p] = weights
        put_pair(mixed, p, dot(values_t[pair(p)], weights))


def dec_attention_kernel(
    x_own, x_other, gain, ids, table, w_query, w_key, w_value, w_mix, gain_cross, w_cross,
    probs, queries, keys, values, x_normed, mixed, mid, cross_in, cross_queries,
    x_all,
):
    core = lax.axis_index("seq")
    half = x_own.shape[0]
    length = 2 * half
    for part, at in ((x_own, core), (x_other, 1 - core)):
        x_all[aligned(at, half), :] = part[...].astype(FULL)
    x_normed[...] = normed(x_all[...], gain[...])
    period = 2 * BLOCK
    biases = dot(table[...], offsets(0, period, False), precision=HIGH)
    query_marks, key_marks = doc_marks(ids[...])
    later = iota((BLOCK, BLOCK), 0) > iota((BLOCK, BLOCK), 1)
    for weight, target in zip((w_query, w_key, w_value), (queries, keys, values)):
        target[...] = dot(x_normed[...], weight[...]).astype(LOW)
    values_t = jnp.transpose(values[...])
    for p in range(HEADS // 2):
        bias = [
            jnp.where(later, NEGATIVE, sheared(biases[head : head + 1], period)[:, :length]) for head in (2 * p, 2 * p + 1)
        ]
        scores = pair_scores(keys[:, pair(p)], queries[:, pair(p)], key_marks, query_marks)
        weights = softmax(scores + jnp.concatenate(bias, 1))
        probs[p] = weights
        put_pair(mixed, p, dot(values_t[pair(p)], weights))
    mid[...] = x_all[...] + dot_rows(mixed[...], w_mix[...])
    cross_in[...] = normed(mid[...], gain_cross[...])
    cross_queries[...] = dot(cross_in[...], w_cross[...]).astype(LOW)


def enc_ff_kernel(
    x_own, x_other, mixed_own, mixed_other, mix_own, mix_other, gain, w_up, w_down,
    mid, after, after_low, active, ff_in,
):
    core = lax.axis_index("seq")
    hidden = w_up.shape[1]
    half = x_own.shape[0]
    length = 2 * half
    for part, at in ((x_own, core), (x_other, 1 - core)):
        mid[aligned(at, half), :] = part[...].astype(FULL)
    mid[...] += dot_rows(mixed_own[...], mix_own[...]) + dot_rows(mixed_other[...], mix_other[...])
    ff_in[...] = normed(mid[...], gain[...])
    total = None
    for start in range(0, hidden, 256):
        cols = slice(start, start + 256)
        act, grow = gelu_pair(dot(ff_in[...], w_up[:, cols]))
        act = act.astype(LOW)
        active[:length, cols] = act
        active[length:, cols] = grow.astype(LOW)
        term = dot(act, w_down[cols, :])
        total = term if total is None else total + term
    after[...] = mid[...] + total
    after_low[...] = total.astype(LOW)


def decoder_kernel(
    rows_count,
    after_part, came, gain_final, enc_ids, dec_ids, cross_queries, dec_mid, gain_ff, cot_own, cot_other,
    w_key, w_value, w_mix, w_up, w_down,
    enc_result, after, state, keys, values, probs, mixed, dec_result, stream, gain_grad, kept, sent,
    payload, cross, cot, out, before_grad, active,
):
    core = lax.axis_index("seq")
    length = dec_mid.shape[0]
    half, enc_half = length // 2, after.shape[0] // 2
    for part, at in ((cot_own, core), (cot_other, 1 - core)):
        cot[aligned(at, half), :] = part[...]
    after[...] = after_part[...] + came[...].astype(FULL)
    enc_result[...] = after[aligned(core, enc_half), :]
    state[...] = normed(after[...], gain_final[...])
    _, key_marks = doc_marks(enc_ids[...])
    query_marks, _ = doc_marks(dec_ids[...])
    keys[...] = dot(state[...], w_key[...]).astype(LOW)
    values[...] = dot(state[...], w_value[...]).astype(LOW)
    values_t = jnp.transpose(values[...])
    for p in range(HEADS // 2):
        weights = softmax(pair_scores(keys[:, pair(p)], cross_queries[:, pair(p)], key_marks, query_marks))
        probs[p] = weights
        put_pair(mixed, p, dot(values_t[pair(p)], weights))
    cross[...] = dec_mid[...] + dot_rows(mixed[...], w_mix[...])
    ff_in = normed(cross[...], gain_ff[...])
    total = cross[...]
    normed_grad = jnp.zeros_like(total)
    for start in range(0, FF, 512):
        cols = slice(start, start + 512)
        act, grow = gelu_pair(dot(ff_in, w_up[:, cols]))
        act = act.astype(LOW)
        active[:, cols] = act
        total = total + dot(act, w_down[cols, :])
        grad = (grow * dot_cols(cot[...], w_down[cols, :])).astype(LOW)
        before_grad[:, cols] = grad
        normed_grad = normed_grad + dot_cols(grad, w_up[:, cols])
    out[...] = total
    dec_result[...] = out[aligned(core, half), :]
    shares = Shares(rows_count, payload)
    for start in range(0, FF // 2, LANES):
        shares.put(dot_rows(ff_in, before_grad[:, pl.ds(pl.multiple_of(core * (FF // 2) + start, LANES), LANES)]))
    shares.put(dot_rows(active[...], cot[:, aligned(core, LANES)]))
    shares.split(kept, sent)
    back, gain_grad[...] = norm_back(cross[...], gain_ff[...], normed_grad)
    stream[...] = cot[...].astype(FULL) + back


def cross_back_kernel(
    rows_count,
    stream, dec_mid, gain_cross, cross_in, queries, keys, values, probs, mixed, state, after, gain_final,
    w_mix, w_key, w_value, w_query,
    enc_stream, enc_low, gain_final_grad, stream_out, gain_grad, kept, sent,
    payload, low, query_grad_t, query_grad, key_grad, value_grad,
):
    core = lax.axis_index("seq")
    shares = Shares(rows_count, payload, False)
    low[...] = stream[...].astype(LOW)
    mixed_grad = dot_cols(low[...], w_mix[...]).astype(LOW)
    keys_t = jnp.transpose(keys[...])
    for p in range(HEADS // 2):
        weights, grads = probs[p], apart(mixed_grad[:, pair(p)])
        score_grad = score_back(weights, dot_cols(values[:, pair(p)], grads))
        put_pair(query_grad_t, p, dot(keys_t[pair(p)], score_grad))
        key_grad[:, pair(p)] = dot(score_grad, apart(queries[:, pair(p)])).astype(LOW)
        value_grad[:, pair(p)] = dot(weights, grads).astype(LOW)
    query_grad[...] = jnp.transpose(query_grad_t[...])
    state_grad = dot_cols(key_grad[...], w_key[...]) + dot_cols(value_grad[...], w_value[...])
    back, gain_final_grad[...] = norm_back(after[...], gain_final[...], state_grad)
    enc_stream[...] = back
    enc_low[...] = back.astype(LOW)
    back, gain_grad[...] = norm_back(dec_mid[...], gain_cross[...], dot_cols(query_grad[...], w_query[...]))
    stream_out[...] = stream[...] + back
    own = aligned(core, LANES)
    shares.put(dot_rows(cross_in[...], query_grad[:, own]))
    shares.put(dot_rows(state[...], key_grad[:, own]))
    shares.put(dot_rows(state[...], value_grad[:, own]))
    shares.put(dot(mixed[...], low[:, own]))
    shares.split(kept, sent)


def dec_back_kernel(
    rows_count,
    stream, x_own, x_other, gain, x_normed, queries, keys, values, probs, mixed,
    w_mix, w_query, w_key, w_value,
    input_grad, gain_grad, table_grad, squares, kept, sent,
    payload, low, query_grad_t, query_grad, key_grad, value_grad, sums, x_all, total,
):
    core = lax.axis_index("seq")
    shares = Shares(rows_count, payload, False)
    half = x_own.shape[0]
    length = 2 * half
    for part, at in ((x_own, core), (x_other, 1 - core)):
        x_all[aligned(at, half), :] = part[...].astype(FULL)
    low[...] = stream[...].astype(LOW)
    mixed_grad = dot_cols(low[...], w_mix[...]).astype(LOW)
    period = 2 * BLOCK
    keys_t = jnp.transpose(keys[...])
    for p in range(HEADS // 2):
        weights, grads = probs[p], apart(mixed_grad[:, pair(p)])
        score_grad = score_back(weights, dot_cols(values[:, pair(p)], grads))
        put_pair(query_grad_t, p, dot(keys_t[pair(p)], score_grad))
        key_grad[:, pair(p)] = dot(score_grad, apart(queries[:, pair(p)])).astype(LOW)
        value_grad[:, pair(p)] = dot(weights, grads).astype(LOW)
        for odd in range(2):
            head, grad = 2 * p + odd, score_grad[:, odd * length : (odd + 1) * length].astype(FULL)
            wide = jnp.concatenate([grad, jnp.zeros((BLOCK, BLOCK), FULL)], axis=1)
            sums[head : head + 1, :] = unsheared(wide, period)
    query_grad[...] = jnp.transpose(query_grad_t[...])
    table_grad[...] = dot(sums[...], offsets(0, period, False), ((1,), (1,)), HIGH)
    normed_grad = (
        dot_cols(query_grad[...], w_query[...])
        + dot_cols(key_grad[...], w_key[...])
        + dot_cols(value_grad[...], w_value[...])
    )
    back, gain_grad[...] = norm_back(x_all[...], gain[...], normed_grad)
    total[...] = stream[...] + back
    input_grad[...] = total[aligned(core, half), :]
    squares[...] = jnp.sum(total[...] * total[...], axis=0, keepdims=True)
    own = aligned(core, LANES)
    for grad in (query_grad, key_grad, value_grad):
        shares.put(dot_rows(x_normed[...], grad[:, own]))
    shares.put(dot(mixed[...], low[:, own]))
    shares.split(kept, sent)


def enc_ff_back_kernel(
    low, active_own, active_other, down_own, up_own, down_other, up_other,
    before_grad, part,
):
    hidden = up_own.shape[1]
    length = low.shape[0]
    total = None
    for active, w_down, w_up, own in ((active_own, down_own, up_own, 1), (active_other, down_other, up_other, 0)):
        for start in range(0, hidden, 256):
            cols = slice(start, start + 256)
            grad = (active[length:, cols].astype(FULL) * dot_cols(low[...], w_down[cols, :])).astype(LOW)
            if own:
                before_grad[:, cols] = grad
            term = dot_cols(grad, w_up[:, cols])
            total = term if total is None else total + term
    part[...] = total


def enc_ff_weights_kernel(rows_count, ff_in, before_grad, active_own, active_other, low, kept, sent, payload, both):
    core = lax.axis_index("seq")
    shares = Shares(rows_count, payload)
    for start in range(0, before_grad.shape[1], LANES):
        shares.put(dot_rows(ff_in[...], before_grad[:, start : start + LANES]))
    hidden, length = active_own.shape[1], low.shape[0]
    own = low[:, aligned(core, LANES)]
    both[aligned(core, hidden), :] = dot_rows(active_own[:length], own)
    both[aligned(1 - core, hidden), :] = dot_rows(active_other[:length], own)
    shares.put(both[...])
    shares.split(kept, sent)


def enc_attention_back_kernel(
    part, mid, gain, stream, w_mix, queries, keys, values, probs, w_query, w_key, w_value,
    low, stream_out, gain_grad, query_grad, key_grad, value_grad, table_grad, normed_part, normed_first, normed_last,
    diagonals, sums, query_grad_t,
):
    core = lax.axis_index("seq")
    width = w_query.shape[1]
    length = mid.shape[0]
    span, period = length - BLOCK, 2 * length
    back, gain_grad[...] = norm_back(mid[...], gain[...], part[...])
    stream_out[...] = stream[...] + back
    low[...] = stream_out[...].astype(LOW)
    mixed_grad = dot_cols(low[...], w_mix[...]).astype(LOW)
    sums[...] = jnp.zeros_like(sums)
    keys_t = jnp.transpose(keys[...])
    for p in range(HEADS // 4):
        weights, grads = probs[p], apart(mixed_grad[:, pair(p)])
        score_grad = score_back(weights, dot_cols(values[:, pair(p)], grads))
        put_pair(query_grad_t, p, dot(keys_t[pair(p)], score_grad))
        key_grad[:, pair(p)] = dot(score_grad, apart(queries[:, pair(p)])).astype(LOW)
        value_grad[:, pair(p)] = dot(weights, grads).astype(LOW)
        for odd in range(2):
            diagonals[...] = jnp.zeros_like(diagonals)
            for key in range(0, length, BLOCK):
                grad = score_grad[key : key + BLOCK, odd * length : (odd + 1) * length]
                diagonals[:, span - key : span - key + length] += grad.astype(FULL)
            sums[pl.ds(core * (HEADS // 2) + 2 * p + odd, 1), :] = unsheared(diagonals[...], period)
    query_grad[...] = jnp.transpose(query_grad_t[...])
    table_grad[...] = dot(sums[...], offsets(span, period, True), ((1,), (1,)), HIGH)
    normed_part[...] = (
        dot_cols(query_grad[...], w_query[...])
        + dot_cols(key_grad[...], w_key[...])
        + dot_cols(value_grad[...], w_value[...])
    )
    half = normed_first.shape[0]
    normed_first[...] = normed_part[:half].astype(LOW)
    normed_last[:half, :] = normed_part[half:].astype(LOW)
    normed_last[half:, :] = jnp.zeros((normed_last.shape[0] - half, D), LOW)
    normed_last[half : half + HEADS, :BUCKETS] = table_grad[...].astype(LOW)


def enc_finish_kernel(
    rows_count,
    normed_part, came_first, came_last, stream, x_own, x_other, gain, x_normed, query_grad, key_grad, value_grad,
    mixed_own, mixed_other, low, table_enc, table_dec, dec_squares,
    g_ff, g_final, g_self, g_cross, g_dec_ff,
    input_grad, row_norm, kept, sent,
    payload, x_all, total, both, small,
):
    core = lax.axis_index("seq")
    shares = Shares(rows_count, payload)
    half = x_own.shape[0]
    for part, at in ((x_own, core), (x_other, 1 - core)):
        x_all[aligned(at, half), :] = part[...].astype(FULL)
    for grad in (query_grad, key_grad, value_grad):
        shares.put(dot_rows(x_normed[...], grad[...]))
    width = mixed_own.shape[0]
    own = low[:, aligned(core, LANES)]
    both[aligned(core, width), :] = dot(mixed_own[...], own)
    both[aligned(1 - core, width), :] = dot(mixed_other[...], own)
    shares.put(both[...])
    normed_grad = normed_part[...] + jnp.concatenate([came_first[...], came_last[:half]], 0).astype(FULL)
    back, gain_grad = norm_back(x_all[...], gain[...], normed_grad)
    total[...] = stream[...] + back
    input_grad[...] = total[aligned(core, half), :]
    squares = jnp.sum(total[...] * total[...], axis=0, keepdims=True) + dec_squares[...]
    row_norm[...] = jnp.sqrt(jnp.sum(squares, axis=1, keepdims=True))
    small[...] = jnp.zeros_like(small)
    small[:HEADS, :BUCKETS] = table_enc[...] + came_last[half : half + HEADS, :BUCKETS].astype(FULL)
    small[:HEADS, BLOCK : BLOCK + BUCKETS] = table_dec[...]
    for row, grad in enumerate(
        (gain_grad, g_ff[...], g_final[...], g_self[...], g_cross[...], g_dec_ff[...])
    ):
        for part in range(2):
            small[HEADS + 2 * row + part : HEADS + 2 * row + part + 1, :] = grad[:, part * LANES : (part + 1) * LANES]
    shares.split(kept, sent)
    kept[kept.shape[0] - SMALL :, :] = small[...].astype(LOW)
    if in_order(rows_count):
        sent[sent.shape[0] - SMALL :, :] = small[...].astype(LOW)


def sum_kernel(*refs, segments, extra):
    new_kept, new_sent = refs[-2:]
    row = 0
    for index, sizes in enumerate(segments):
        kept, came = refs[2 * index : 2 * index + 2]
        at = 0
        for size in sizes:
            half = size // 2
            new_sent[row : row + half] = kept[at + half : at + size] + came[at + half : at + size]
            new_kept[row : row + half] = kept[at : at + half] + came[at : at + half]
            row, at = row + half, at + size
    if extra:
        both = kept[at:] + came[at:]
        new_kept[row:] = both
        new_sent[row:] = both


def last_sum(kept, came, rows):
    return kept[rows].astype(FULL) + came[rows].astype(FULL)


def last_kernel(kept, came, *outs):
    row = 0
    for out in outs:
        lead = out.shape[0]
        if out.shape[1] < LANES:
            break
        for start in range(0, out.shape[1], LANES):
            out[:, start : start + LANES] = last_sum(kept, came, slice(row, row + lead))
            row += lead
    else:
        return
    small = last_sum(kept, came, slice(row, kept.shape[0]))
    gains = jnp.concatenate(
        [
            jnp.concatenate([small[HEADS + 2 * i + part : HEADS + 2 * i + part + 1] for i in range(6)] + [small[:2]], 0)
            for part in range(2)
        ],
        1,
    )
    lead = outs[-8].shape[1]
    start = lax.axis_index("rows") * lead
    gains = pltpu.roll(gains, jnp.where(start == 0, 0, D - start), 1)
    for i in range(6):
        outs[i - 8][...] = gains[i : i + 1, :lead]
    outs[-2][...] = small[:HEADS, :BUCKETS]
    outs[-1][...] = small[:HEADS, BLOCK : BLOCK + BUCKETS]


SMALL = 32
SUM_COST = 1.0


def on_device(
    rows_count,
    enc_input,
    dec_input,
    enc_segments,
    dec_segments,
    cotangent,
    enc_norm_attn,
    enc_query,
    enc_key,
    enc_value,
    enc_mix,
    enc_table,
    enc_norm_ff,
    enc_up,
    enc_down,
    enc_norm_final,
    dec_norm_self,
    dec_query,
    dec_key,
    dec_value,
    dec_mix,
    dec_table,
    dec_norm_cross,
    cross_query,
    cross_key,
    cross_value,
    cross_mix,
    dec_norm_ff,
    dec_up,
    dec_down,
):
    chip, core = lax.axis_index("rows"), lax.axis_index("seq")
    x_own, d_own, c_own = enc_input[0], dec_input[0], cotangent[0]
    half, d_half = x_own.shape[0], d_own.shape[0]
    enc, dec = 2 * half, 2 * d_half
    width, hidden = D // 2, FF // 2

    def swap(values):
        return lax.ppermute(values, "seq", [(0, 1), (1, 0)])

    def row(gain):
        return gain.reshape(1, -1)

    def v(*arrays):
        return [(array, "vmem") for array in arrays]

    def h(*arrays):
        return [(array, "all") for array in arrays]

    def cols(*arrays):
        return [(array, "cols") for array in arrays]

    square = (D, D)
    ordered = in_order(rows_count)

    def payload(total, extra=0):
        if ordered:
            return [((total // 2 + extra, LANES), LOW)] * 2, [((rows_count, total // rows_count, LANES), LOW)]
        return [((total + extra, LANES), LOW), ((16, LANES), LOW)], [((1, total, LANES), LOW)]

    squares, ffs, last = payload(4 * D), payload(4 * D + FF), payload(4 * D, SMALL)

    lead = D // rows_count

    def arranged(pay, leads, extra, orders):
        if ordered:
            return pay
        places = jnp.array([[chunk_of(q, order) for q in range(rows_count)] for order in orders], jnp.int32)
        parts, start = [], 0
        for count in leads:
            parts.append(pay[0][start : start + count].reshape(rows_count, -1, LANES))
            start += count
        chunks = jnp.take(jnp.concatenate(parts, 1), places[core] ^ chip, axis=0)
        return [
            jnp.concatenate([part.reshape(-1, LANES), pay[0][start : start + extra]], 0)
            for part in (chunks[: rows_count // 2], chunks[rows_count // 2 :])
        ]

    class Sum:
        def __init__(self, pay, leads, outs, late, name, extra=0):
            self.orders = bit_orders(rows_count, late)
            self.kept, self.sent = arranged(pay, leads, extra, self.orders)
            self.segments = [self.kept.shape[0] - extra]
            self.outs, self.extra, self.name, self.stage, self.found = outs, extra, name, 0, None
            self.send()

        def send(self):
            pairs = [
                (at * 2 + c, (at ^ (1 << self.orders[c][self.stage])) * 2 + c)
                for at in range(rows_count)
                for c in range(2)
            ]
            self.came = lax.ppermute(self.sent, ("rows", "seq"), pairs)
            self.stage += 1

        def add(self, token, *others, after=()):
            every = (self, *others)
            for other in others:
                assert other.stage == self.stage and other.orders[0][self.stage :] == self.orders[0][self.stage :]
                assert not self.extra
            name = f"{self.name}_{self.stage}"
            operands = v(*[array for each in every for array in (each.kept, each.came)])
            if self.stage == len(self.orders[0]):
                token, self.found = call(
                    token, last_kernel, operands,
                    [out for each in every for out in each.outs], limit=8, name=name, after=after,
                )
                return token
            segments = [each.segments for each in every]
            self.extra = every[-1].extra
            self.segments = [size // 2 for sizes in segments for size in sizes]
            self.outs = [out for each in every for out in each.outs]
            shape = (sum(self.segments) + self.extra, LANES)
            token, (self.kept, self.sent) = call(
                token, functools.partial(sum_kernel, segments=segments, extra=self.extra), operands,
                [(shape, LOW)] * 2, limit=8, name=name, after=after, cost=SUM_COST,
            )
            self.send()
            return token

    ff_outs = [((lead, hidden), FULL), ((FF // rows_count, LANES), FULL)]
    square_outs = [((lead, LANES), FULL)] * 4
    small_outs = [((1, lead), FULL)] * 6 + [((HEADS, BUCKETS), FULL)] * 2

    x_other, d_other, c_other = swap(x_own), swap(d_own), swap(c_own)

    token, (mixed, probs, queries, keys, values, x_normed) = call(
        None,
        enc_attention_kernel,
        h(x_own) + v(x_other) + h(row(enc_norm_attn), enc_segments, enc_table.T) + cols(enc_query, enc_key, enc_value),
        [
            ((width, enc), LOW), ((HEADS // 4, enc, 2 * enc), LOW),
            ((enc, width), LOW), ((enc, width), LOW), ((enc, width), LOW), ((enc, D), LOW),
        ],
        [((HEADS, 2 * enc), FULL)],
        name="enc_attention",
    )
    mixed_other = swap(mixed)
    token, (d_probs, d_queries, d_keys, d_values, d_normed, d_mixed, d_mid, cross_in, cross_queries) = call(
        token,
        dec_attention_kernel,
        h(d_own) + v(d_other)
        + h(row(dec_norm_self), dec_segments, dec_table.T, dec_query, dec_key, dec_value, dec_mix, row(dec_norm_cross),
            cross_query),
        [((HEADS // 2, dec, 2 * dec), LOW)] + [((dec, D), LOW)] * 4 + [((D, dec), LOW), ((dec, D), FULL)] + [((dec, D), LOW)] * 2,
        [((dec, D), FULL)],
        name="dec_attention", after=[c_other],
    )
    token, (mid, after_part, after_low, active, ff_in) = call(
        token,
        enc_ff_kernel,
        h(x_own) + v(x_other, mixed, mixed_other)
        + [(enc_mix, "rows"), (enc_mix, "rows_other"), (row(enc_norm_ff), "all"), (enc_up, "cols"), (enc_down, "rows")],
        [((enc, D), FULL), ((enc, D), FULL), ((enc, D), LOW), ((2 * enc, hidden), LOW), ((enc, D), LOW)],
        name="enc_ff",
    )
    after_came = swap(after_low)
    token, (
        enc_result, after, state, c_keys, c_values, c_probs, c_mixed, dec_result, stream, g_dec_ff, *pay_first, active,
    ) = call(
        token,
        functools.partial(decoder_kernel, rows_count),
        v(after_part, after_came) + h(row(enc_norm_final), enc_segments, dec_segments) + v(cross_queries, d_mid)
        + h(row(dec_norm_ff), c_own) + v(c_other) + h(cross_key, cross_value, cross_mix, dec_up, dec_down),
        [
            ((half, D), FULL), ((enc, D), FULL), ((enc, D), LOW), ((enc, D), LOW), ((enc, D), LOW),
            ((HEADS // 2, enc, 2 * dec), LOW), ((D, dec), LOW), ((d_half, D), FULL), ((dec, D), FULL), ((1, D), FULL),
        ] + ffs[0],
        ffs[1] + [((dec, D), FULL), ((dec, D), LOW), ((dec, D), FULL), ((dec, FF), LOW), ((dec, FF), LOW)],
        name="decoder", through=[active],
    )
    active_other = swap(active)
    first = Sum(pay_first, [D] * 4 + [FF], ff_outs, True, "sum_dec_ff")
    token, (enc_stream, enc_low, g_final, stream, g_cross, *pay_cross) = call(
        token,
        functools.partial(cross_back_kernel, rows_count),
        v(stream, d_mid) + h(row(dec_norm_cross)) + v(cross_in, cross_queries, c_keys, c_values, c_probs, c_mixed, state, after,
          )
        + h(row(enc_norm_final), cross_mix, cross_key, cross_value, cross_query),
        [((enc, D), FULL), ((enc, D), LOW), ((1, D), FULL), ((dec, D), FULL), ((1, D), FULL)] + squares[0],
        squares[1] + [((dec, D), LOW), ((D, dec), LOW), ((dec, D), LOW), ((enc, D), LOW), ((enc, D), LOW)],
        name="cross_back",
    )
    second = Sum(pay_cross, [D] * 4, square_outs, False, "sum_cross")
    token, (before_grad, part) = call(
        token,
        enc_ff_back_kernel,
        v(enc_low, active, active_other)
        + [(enc_down, "rows"), (enc_up, "cols"), (enc_down, "rows_other"), (enc_up, "cols_other")],
        [((enc, hidden), LOW), ((enc, D), FULL)],
        name="enc_ff_back",
    )
    token, pay_enc_ff = call(
        token,
        functools.partial(enc_ff_weights_kernel, rows_count),
        v(ff_in, before_grad, active, active_other, enc_low),
        ffs[0],
        ffs[1] + [((FF, LANES), FULL)],
        name="enc_ff_weights",
    )
    third = Sum(pay_enc_ff, [D] * 4 + [FF], ff_outs, True, "sum_enc_ff")
    token = first.add(token)
    token, (dec_input_grad, g_self, table_dec, dec_squares, *pay_dec) = call(
        token,
        functools.partial(dec_back_kernel, rows_count),
        v(stream) + h(d_own) + v(d_other) + h(row(dec_norm_self))
        + v(d_normed, d_queries, d_keys, d_values, d_probs, d_mixed)
        + h(dec_mix, dec_query, dec_key, dec_value),
        [((d_half, D), FULL), ((1, D), FULL), ((HEADS, BUCKETS), FULL), ((1, D), FULL)] + squares[0],
        squares[1] + [((dec, D), LOW), ((D, dec), LOW)] + [((dec, D), LOW)] * 3 + [((HEADS, 2 * BLOCK), FULL), ((dec, D), FULL), ((dec, D), FULL)],
        name="dec_back",
    )
    fourth = Sum(pay_dec, [D] * 4, square_outs, False, "sum_dec")
    token, (low, enc_stream, g_ff, query_grad, key_grad, value_grad, table_enc, normed_part, *normed_low) = call(
        token,
        enc_attention_back_kernel,
        v(part, mid) + h(row(enc_norm_ff)) + v(enc_stream) + [(enc_mix, "rows")]
        + v(queries, keys, values, probs) + cols(enc_query, enc_key, enc_value),
        [
            ((enc, D), LOW), ((enc, D), FULL), ((1, D), FULL), ((enc, width), LOW), ((enc, width), LOW),
            ((enc, width), LOW), ((HEADS, BUCKETS), FULL), ((enc, D), FULL), ((half, D), LOW),
            ((half + 16, D), LOW),
        ],
        [((BLOCK, 2 * enc), FULL), ((HEADS, 2 * enc), FULL), ((width, enc), LOW)],
        name="enc_attention_back", cost=8.0, after=[second.came],
    )
    normed_came = [swap(part) for part in normed_low]
    token, (enc_input_grad, row_norm, *pay_enc) = call(
        token,
        functools.partial(enc_finish_kernel, rows_count),
        v(normed_part, *normed_came, enc_stream) + h(x_own) + v(x_other) + h(row(enc_norm_attn)) + v(x_normed, query_grad, key_grad,
          value_grad, mixed, mixed_other, low, table_enc, table_dec, dec_squares, g_ff, g_final, g_self, g_cross,
          g_dec_ff),
        [((half, D), FULL), ((1, 1), FULL)] + last[0],
        last[1] + [((enc, D), FULL), ((enc, D), FULL), ((D, LANES), FULL), ((SMALL, LANES), FULL)],
        name="enc_finish",
    )

    fifth = Sum(pay_enc, [D] * 4, square_outs + small_outs, True, "sum_enc", SMALL)
    token = first.add(token)
    token = second.add(token, fourth)
    token = third.add(token)
    token = fifth.add(token)
    waiting = [third, first, fifth, second]
    while waiting:
        for each in waiting:
            token = each.add(token)
        waiting = [each for each in waiting if each.found is None]
    dec_u, dec_d = first.found
    enc_u, enc_d = third.found
    cross_q, cross_k, cross_v, cross_m, dec_q, dec_k, dec_v, dec_m = second.found
    enc_q, enc_k, enc_v, enc_m, *small = fifth.found
    gains = [gain[0] for gain in small[:6]]
    tables = [small[6].T, small[7].T]
    return (
        enc_result[None], dec_result[None], enc_input_grad[None], dec_input_grad[None], row_norm[0],
        gains[0], enc_q, enc_k, enc_v, enc_m, tables[0], gains[1], enc_u, enc_d, gains[2],
        gains[3], dec_q, dec_k, dec_v, dec_m, tables[1], gains[4], cross_q, cross_k, cross_v, cross_m,
        gains[5], dec_u, dec_d,
    )


def solution(mesh):
    split, line, copied = P("rows", "seq", None), P("rows", None), P()
    in_specs = (split, split, line, line, split) + (copied,) * 24
    block, vector = P("rows", "seq"), P("rows")
    out_specs = (
        (split,) * 4 + (vector,)
        + (vector,) + (block,) * 4 + (copied, vector, block, block, vector)
        + (vector,) + (block,) * 4 + (copied, vector) + (block,) * 4 + (vector, block, block)
    )
    return jax.shard_map(
        functools.partial(on_device, mesh.shape["rows"]),
        mesh=mesh, in_specs=in_specs, out_specs=out_specs, check_vma=False,
    )
```

```python
import functools
import math

import jax
import jax.numpy as jnp
from jax import lax
from jax.experimental import pallas as pl
from jax.experimental.pallas import tpu as pltpu
from jax.sharding import PartitionSpec as P

D = 512
HEADS = 8
HEAD = 64
FF = 2048
BUCKETS = 32
MAX_DIST = 128
NDOC = 4
EPSILON = 1e-06
NEGATIVE = -1e30
BLOCK = 128
LANES = 256

LOW = jnp.bfloat16
FULL = jnp.float32
HIGH = lax.Precision.HIGHEST


def cut_points(exact_span, bucket_half, reach):
    points = []
    for target in range(exact_span + 1, bucket_half):
        reach_at = exact_span
        while (
            exact_span
            + int(
                math.log(reach_at / exact_span)
                / math.log(reach / exact_span)
                * (bucket_half - exact_span)
            )
            < target
        ):
            reach_at += 1
        points.append(reach_at)
    return points


def bucket_index(offset, both_ways):
    if both_ways:
        bucket_half = BUCKETS // 2
        base_index = jnp.where(offset > 0, bucket_half, 0).astype(jnp.int32)
        distance = jnp.abs(offset)
    else:
        bucket_half = BUCKETS
        base_index = jnp.zeros_like(offset)
        distance = jnp.maximum(-offset, 0)
    exact_span = bucket_half // 2
    result = base_index + jnp.minimum(distance, exact_span)
    for border in cut_points(exact_span, bucket_half, MAX_DIST):
        result = result + (distance >= border).astype(jnp.int32)
    return result


def dot(left, right, dims=((1,), (0,)), precision=None):
    return lax.dot_general(
        left, right, (dims, ((), ())), preferred_element_type=FULL, precision=precision
    )


def dot_cols(left, right):
    return dot(left, right, ((1,), (1,)))


def dot_rows(left, right):
    return dot(left, right, ((0,), (0,)))


def scale_of(values):
    return lax.rsqrt(jnp.mean(values * values, axis=-1, keepdims=True) + EPSILON)


def normed(values, gain):
    return (values * scale_of(values) * gain).astype(LOW)


def norm_back(values, gain, grad):
    scale = scale_of(values)
    unit = values * scale
    gain_grad = jnp.sum(grad * unit, axis=0, keepdims=True)
    grad = grad * gain
    return scale * (grad - unit * jnp.mean(grad * unit, axis=-1, keepdims=True)), gain_grad


def gelu_pair(values):
    root = math.sqrt(2.0 / math.pi)
    square = values * values
    tanh = jnp.tanh(root * values * (1.0 + 0.044715 * square))
    half = 0.5 + 0.5 * tanh
    slope = half + 0.5 * values * (1.0 - tanh * tanh) * (root + (3 * 0.044715 * root) * square)
    return values * half, slope


def iota(shape, axis):
    return lax.broadcasted_iota(jnp.int32, shape, axis)


def offsets(span, period, both_ways):
    place = iota((1, period), 1)
    offset = span - jnp.where(place < period - BLOCK, place, place - period)
    return (bucket_index(offset, both_ways) == iota((BUCKETS, period), 0)).astype(FULL)


def sheared(row, period):
    return pltpu.roll(
        jnp.broadcast_to(row, (BLOCK, period)), 0, 1, stride=1, stride_axis=0
    )


def unsheared(sums, period):
    rows = sums.shape[0]
    while rows > 8:
        rows //= 2
        sums = sums[:rows] + pltpu.roll(sums[rows:], period - rows, 1)
    total = sums[:1]
    for row in range(1, 8):
        total = total + pltpu.roll(sums[row : row + 1], period - row, 1)
    return total


def doc_columns(ids):
    wide = jnp.broadcast_to(ids.astype(FULL), (BLOCK, ids.shape[1]))
    return jnp.transpose(wide)


def doc_marks(ids):
    columns = doc_columns(ids)
    lane = iota(columns.shape, 1)
    same = columns == lane.astype(FULL)
    query_marks = jnp.where((lane < NDOC) & jnp.logical_not(same), NEGATIVE, 0.0).astype(LOW)
    return query_marks, same.astype(FULL).astype(LOW)


def apart(values):
    lane = iota(values.shape, 1)
    zeros = jnp.zeros_like(values)
    return jnp.concatenate([jnp.where(lane < HEAD, values, zeros), jnp.where(lane >= HEAD, values, zeros)], 0)


def pair_scores(key_pair, query_pair, key_marks, query_marks):
    left = jnp.concatenate([key_pair, key_marks], 1)
    right = jnp.concatenate([apart(query_pair), jnp.concatenate([query_marks, query_marks], 0)], 1)
    return dot_cols(left, right)


def put_pair(target, p, both):
    length = both.shape[1] // 2
    target[one(2 * p), :] = both[:HEAD, :length].astype(LOW)
    target[one(2 * p + 1), :] = both[HEAD:, length:].astype(LOW)


def softmax(scores):
    weights = jnp.exp(scores - jnp.max(scores, axis=0, keepdims=True))
    return (weights * (1.0 / jnp.sum(weights, axis=0, keepdims=True))).astype(LOW)


def score_back(probs, probs_grad):
    probs = probs.astype(FULL)
    inner = jnp.sum(probs * probs_grad, axis=0, keepdims=True)
    return (probs * (probs_grad - inner)).astype(LOW)


def one(head):
    return slice(head * HEAD, (head + 1) * HEAD)


def pair(index):
    return slice(index * 2 * HEAD, (index + 1) * 2 * HEAD)


def aligned(index, size):
    return pl.ds(pl.multiple_of(index * size, size), size)


class Lazy:
    def __init__(self, ref, copy):
        self.ref, self.copy = ref, copy

    @property
    def shape(self):
        return self.ref.shape

    def __getitem__(self, index):
        if self.copy is not None:
            self.copy.wait()
            self.copy = None
        return self.ref[index]


def cut(source, mode):
    if mode == "all":
        return source
    core = lax.axis_index("seq")
    rows, cols = source.shape
    at = 1 - core if mode.endswith("other") else core
    if mode.startswith("cols"):
        return source.at[:, aligned(at, cols // 2)]
    return source.at[aligned(at, rows // 2), :]


def cut_shape(shape, mode):
    if mode == "all":
        return shape
    return (shape[0], shape[1] // 2) if mode.startswith("cols") else (shape[0] // 2, shape[1])


ROUTES = {"xyz": (0, 1, 2), "zxy": (2, 0, 1), "xzy": (0, 2, 1)}


def bit_orders(rows_count, route):
    bits = list(range(rows_count.bit_length() - 1))
    if len(bits) < 3:
        return (bits, bits)
    first = [*ROUTES[route], *bits[3:]]
    return (first, [{0: 1, 1: 0}.get(bit, bit) for bit in first])


def place_of(chunk, order):
    bits = len(order)
    return sum(((chunk >> order[s]) & 1) << (bits - 1 - s) for s in range(bits))


def chunk_of(place, order):
    bits = len(order)
    return sum(((place >> (bits - 1 - s)) & 1) << order[s] for s in range(bits))


def in_order(rows_count):
    return (D // rows_count) % 16 == 0


class Shares:
    def __init__(self, rows_count, payload, route):
        self.rows_count, self.payload, self.row = rows_count, payload, 0
        core, chip = lax.axis_index("seq"), lax.axis_index("rows")
        orders = bit_orders(rows_count, route)
        own = [place_of(chip, order) for order in orders]
        self.places = [
            jnp.where(core == 0, place_of(chunk, orders[0]) ^ own[0], place_of(chunk, orders[1]) ^ own[1])
            for chunk in range(rows_count)
        ] if in_order(rows_count) else [0]

    def put(self, grad):
        chunks = len(self.places)
        lead = grad.shape[0] // chunks
        for chunk in range(chunks):
            self.payload[self.places[chunk], self.row : self.row + lead, :] = grad[
                chunk * lead : (chunk + 1) * lead
            ].astype(LOW)
        self.row += lead

    def split(self, kept, sent):
        if not in_order(self.rows_count):
            kept[: self.row] = self.payload[0]
            return
        half = self.rows_count // 2
        shape = (half * self.row, LANES)
        sent[: half * self.row] = self.payload[half:].reshape(shape)
        kept[: half * self.row] = self.payload[:half].reshape(shape)


VMEM = pl.BlockSpec(memory_space=pltpu.VMEM)
HBM = pl.BlockSpec(memory_space=pltpu.HBM)
ANY = pl.BlockSpec(memory_space=pl.ANY)
MIB = 1024 * 1024


def call(token, kernel, ins, outs, scratch=(), limit=24, name=None, after=(), through=()):
    n_ins, n_outs = len(ins), len(outs)
    ins = list(ins) + [(token, "vmem")] * (token is not None) + [(array, "any") for array in (*after, *through)]
    outs = list(outs) + [(array.shape, array.dtype) for array in through] + [((8, BLOCK), FULL)]
    specs = [{"vmem": VMEM, "any": ANY}.get(how, HBM) for _, how in ins]
    arrays = [
        array if how in ("vmem", "any") else pltpu.with_memory_space_constraint(array, pltpu.HBM) for array, how in ins
    ]
    shapes = [jax.ShapeDtypeStruct(shape, kind) for shape, kind in outs]
    lazy = [i for i, (_, how) in enumerate(ins) if how not in ("vmem", "any")]
    scratch = [pltpu.VMEM(shape, kind) for shape, kind in scratch]
    n_own = len(scratch)
    scratch += [pltpu.VMEM(cut_shape(arrays[i].shape, ins[i][1]), arrays[i].dtype) for i in lazy]
    if lazy:
        scratch.append(pltpu.SemaphoreType.DMA((len(lazy),)))

    def body(*refs):
        operands = list(refs[: len(ins)])
        rest = refs[len(ins) :]
        results, own = rest[: len(outs)], rest[len(outs) : len(outs) + n_own]
        landing = rest[len(outs) + n_own :]
        for place, i in enumerate(lazy):
            copy = pltpu.make_async_copy(cut(operands[i], ins[i][1]), landing[place], landing[-1].at[place])
            copy.start()
            operands[i] = Lazy(landing[place], copy)
        results[-1][...] = jnp.zeros((8, BLOCK), FULL)
        kernel(*operands[:n_ins], *results[: n_outs], *own)
        for i in lazy:
            if operands[i].copy is not None:
                operands[i].copy.wait()

    found = pl.pallas_call(
        body,
        out_shape=shapes,
        in_specs=specs,
        out_specs=[VMEM] * n_outs + [ANY] * len(through) + [VMEM],
        input_output_aliases={len(ins) - len(through) + i: n_outs + i for i in range(len(through))},
        scratch_shapes=scratch,
        compiler_params=pltpu.CompilerParams(vmem_limit_bytes=limit * MIB),
        cost_estimate=pl.CostEstimate(
            flops=1000 + int(SCALE * COST.get(name, SUM_COST) * 1.15e9), bytes_accessed=1000, transcendentals=0
        ),
        name=name,
    )(*arrays)
    return found[-1], found[:-1]


def enc_attention_kernel(
    x_own, x_other, gain, ids, table, w_query, w_key, w_value,
    mixed, probs, queries, keys, values, x_normed,
    biases,
):
    core = lax.axis_index("seq")
    width = w_query.shape[1]
    half = x_own.shape[0]
    length = 2 * half
    for part, at in ((x_own, core), (x_other, 1 - core)):
        x_normed[aligned(at, half), :] = normed(part[...].astype(FULL), gain[...])
    span, period = length - BLOCK, 2 * length
    biases[...] = dot(table[...], offsets(span, period, True), precision=HIGH)
    query_marks, key_marks = doc_marks(ids[...])
    for weight, target in zip((w_query, w_key, w_value), (queries, keys, values)):
        target[...] = dot(x_normed[...], weight[...]).astype(LOW)
    values_t = jnp.transpose(values[...])
    for p in range(HEADS // 4):
        shift = []
        for head in (2 * p, 2 * p + 1):
            bias = sheared(biases[pl.ds(core * (HEADS // 2) + head, 1), :], period)
            shift.append(jnp.concatenate([bias[:, span - key : span - key + length] for key in range(0, length, BLOCK)], 0))
        scores = pair_scores(keys[:, pair(p)], queries[:, pair(p)], key_marks, query_marks)
        weights = softmax(scores + jnp.concatenate(shift, 1))
        probs[p] = weights
        put_pair(mixed, p, dot(values_t[pair(p)], weights))


def dec_attention_kernel(
    x_own, x_other, gain, ids, table, w_query, w_key, w_value,
    probs, queries, keys, values, x_normed, mixed, x_all,
):
    core = lax.axis_index("seq")
    half = x_own.shape[0]
    length = 2 * half
    for part, at in ((x_own, core), (x_other, 1 - core)):
        x_all[aligned(at, half), :] = part[...].astype(FULL)
    x_normed[...] = normed(x_all[...], gain[...])
    period = 2 * BLOCK
    biases = dot(table[...], offsets(0, period, False), precision=HIGH)
    query_marks, key_marks = doc_marks(ids[...])
    later = iota((BLOCK, BLOCK), 0) > iota((BLOCK, BLOCK), 1)
    for weight, target in zip((w_query, w_key, w_value), (queries, keys, values)):
        target[...] = dot(x_normed[...], weight[...]).astype(LOW)
    values_t = jnp.transpose(values[...])
    for p in range(HEADS // 2):
        bias = [
            jnp.where(later, NEGATIVE, sheared(biases[head : head + 1], period)[:, :length]) for head in (2 * p, 2 * p + 1)
        ]
        scores = pair_scores(keys[:, pair(p)], queries[:, pair(p)], key_marks, query_marks)
        weights = softmax(scores + jnp.concatenate(bias, 1))
        probs[p] = weights
        put_pair(mixed, p, dot(values_t[pair(p)], weights))


def dec_mid_kernel(x_all, mixed, w_mix, gain_cross, w_cross, mid, cross_in, cross_queries):
    mid[...] = x_all[...] + dot_rows(mixed[...], w_mix[...])
    cross_in[...] = normed(mid[...], gain_cross[...])
    cross_queries[...] = dot(cross_in[...], w_cross[...]).astype(LOW)


def enc_ff_kernel(
    x_own, x_other, mixed_own, mixed_other, mix_own, mix_other, gain, w_up, w_down,
    mid, after, after_low, active, ff_in,
):
    core = lax.axis_index("seq")
    hidden = w_up.shape[1] // 2
    half = x_own.shape[0]
    length = 2 * half
    for part, at in ((x_own, core), (x_other, 1 - core)):
        mid[aligned(at, half), :] = part[...].astype(FULL)
    mid[...] += dot_rows(mixed_own[...], mix_own[...]) + dot_rows(mixed_other[...], mix_other[...])
    ff_in[...] = normed(mid[...], gain[...])
    total = None
    for start in range(0, hidden, 512):
        cols = slice(start, start + 512)
        place = pl.ds(pl.multiple_of(core * hidden + start, 256), 512)
        act, grow = gelu_pair(dot(ff_in[...], w_up[:, place]))
        act = act.astype(LOW)
        active[:length, cols] = act
        active[length:, cols] = grow.astype(LOW)
        term = dot(act, w_down[place, :])
        total = term if total is None else total + term
    after[...] = mid[...] + total
    after_low[...] = total.astype(LOW)


def decoder_kernel(
    rows_count,
    after_part, came, gain_final, enc_ids, dec_ids, cross_queries, dec_mid, gain_ff, cot_own, cot_other,
    w_key, w_value, w_mix, w_up, w_down,
    enc_result, after, state, keys, values, probs, mixed, dec_result, stream, gain_grad, kept, sent,
    payload, cross, cot, out, before_grad, active,
):
    core = lax.axis_index("seq")
    length = dec_mid.shape[0]
    half, enc_half = length // 2, after.shape[0] // 2
    for part, at in ((cot_own, core), (cot_other, 1 - core)):
        cot[aligned(at, half), :] = part[...]
    after[...] = after_part[...] + came[...].astype(FULL)
    enc_result[...] = after[aligned(core, enc_half), :]
    state[...] = normed(after[...], gain_final[...])
    _, key_marks = doc_marks(enc_ids[...])
    query_marks, _ = doc_marks(dec_ids[...])
    keys[...] = dot(state[...], w_key[...]).astype(LOW)
    values[...] = dot(state[...], w_value[...]).astype(LOW)
    values_t = jnp.transpose(values[...])
    for p in range(HEADS // 2):
        weights = softmax(pair_scores(keys[:, pair(p)], cross_queries[:, pair(p)], key_marks, query_marks))
        probs[p] = weights
        put_pair(mixed, p, dot(values_t[pair(p)], weights))
    cross[...] = dec_mid[...] + dot_rows(mixed[...], w_mix[...])
    ff_in = normed(cross[...], gain_ff[...])
    total = cross[...]
    normed_grad = jnp.zeros_like(total)
    for start in range(0, FF, 2048):
        cols = slice(start, start + 2048)
        act, grow = gelu_pair(dot(ff_in, w_up[:, cols]))
        act = act.astype(LOW)
        active[:, cols] = act
        total = total + dot(act, w_down[cols, :])
        grad = (grow * dot_cols(cot[...], w_down[cols, :])).astype(LOW)
        before_grad[:, cols] = grad
        normed_grad = normed_grad + dot_cols(grad, w_up[:, cols])
    out[...] = total
    dec_result[...] = out[aligned(core, half), :]
    shares = Shares(rows_count, payload, "xyz")
    for start in range(0, FF // 2, LANES):
        shares.put(dot_rows(ff_in, before_grad[:, pl.ds(pl.multiple_of(core * (FF // 2) + start, LANES), LANES)]))
    shares.put(dot_rows(active[...], cot[:, aligned(core, LANES)]))
    shares.split(kept, sent)
    back, gain_grad[...] = norm_back(cross[...], gain_ff[...], normed_grad)
    stream[...] = cot[...].astype(FULL) + back


def cross_back_kernel(
    rows_count,
    stream, dec_mid, gain_cross, cross_in, queries, keys, values, probs, mixed, state, after, gain_final,
    w_mix, w_key, w_value, w_query,
    enc_stream, enc_low, gain_final_grad, stream_out, gain_grad, kept, sent,
    payload, low, query_grad_t, query_grad, key_grad, value_grad,
):
    core = lax.axis_index("seq")
    shares = Shares(rows_count, payload, "zxy")
    low[...] = stream[...].astype(LOW)
    mixed_grad = dot_cols(low[...], w_mix[...]).astype(LOW)
    keys_t = jnp.transpose(keys[...])
    for p in range(HEADS // 2):
        weights, grads = probs[p], apart(mixed_grad[:, pair(p)])
        score_grad = score_back(weights, dot_cols(values[:, pair(p)], grads))
        put_pair(query_grad_t, p, dot(keys_t[pair(p)], score_grad))
        key_grad[:, pair(p)] = dot(score_grad, apart(queries[:, pair(p)])).astype(LOW)
        value_grad[:, pair(p)] = dot(weights, grads).astype(LOW)
    query_grad[...] = jnp.transpose(query_grad_t[...])
    state_grad = dot_cols(key_grad[...], w_key[...]) + dot_cols(value_grad[...], w_value[...])
    back, gain_final_grad[...] = norm_back(after[...], gain_final[...], state_grad)
    enc_stream[...] = back
    enc_low[...] = back.astype(LOW)
    back, gain_grad[...] = norm_back(dec_mid[...], gain_cross[...], dot_cols(query_grad[...], w_query[...]))
    stream_out[...] = stream[...] + back
    own = aligned(core, LANES)
    shares.put(dot_rows(cross_in[...], query_grad[:, own]))
    shares.put(dot_rows(state[...], key_grad[:, own]))
    shares.put(dot_rows(state[...], value_grad[:, own]))
    shares.put(dot(mixed[...], low[:, own]))
    shares.split(kept, sent)


def dec_back_kernel(
    rows_count,
    stream, x_own, x_other, gain, x_normed, queries, keys, values, probs, mixed,
    w_mix, w_query, w_key, w_value,
    input_grad, gain_grad, table_grad, squares, kept, sent,
    payload, low, query_grad_t, query_grad, key_grad, value_grad, sums, x_all, total,
):
    core = lax.axis_index("seq")
    shares = Shares(rows_count, payload, "xzy")
    half = x_own.shape[0]
    length = 2 * half
    for part, at in ((x_own, core), (x_other, 1 - core)):
        x_all[aligned(at, half), :] = part[...].astype(FULL)
    low[...] = stream[...].astype(LOW)
    mixed_grad = dot_cols(low[...], w_mix[...]).astype(LOW)
    period = 2 * BLOCK
    keys_t = jnp.transpose(keys[...])
    for p in range(HEADS // 2):
        weights, grads = probs[p], apart(mixed_grad[:, pair(p)])
        score_grad = score_back(weights, dot_cols(values[:, pair(p)], grads))
        put_pair(query_grad_t, p, dot(keys_t[pair(p)], score_grad))
        key_grad[:, pair(p)] = dot(score_grad, apart(queries[:, pair(p)])).astype(LOW)
        value_grad[:, pair(p)] = dot(weights, grads).astype(LOW)
        for odd in range(2):
            head, grad = 2 * p + odd, score_grad[:, odd * length : (odd + 1) * length].astype(FULL)
            wide = jnp.concatenate([grad, jnp.zeros((BLOCK, BLOCK), FULL)], axis=1)
            sums[head : head + 1, :] = unsheared(wide, period)
    query_grad[...] = jnp.transpose(query_grad_t[...])
    table_grad[...] = dot(sums[...], offsets(0, period, False), ((1,), (1,)), HIGH)
    normed_grad = (
        dot_cols(query_grad[...], w_query[...])
        + dot_cols(key_grad[...], w_key[...])
        + dot_cols(value_grad[...], w_value[...])
    )
    back, gain_grad[...] = norm_back(x_all[...], gain[...], normed_grad)
    total[...] = stream[...] + back
    input_grad[...] = total[aligned(core, half), :]
    squares[...] = jnp.sum(total[...] * total[...], axis=0, keepdims=True)
    own = aligned(core, LANES)
    for grad in (query_grad, key_grad, value_grad):
        shares.put(dot_rows(x_normed[...], grad[:, own]))
    shares.put(dot(mixed[...], low[:, own]))
    shares.split(kept, sent)


def enc_ff_back_kernel(
    low, active_own, active_other, w_down, w_up,
    before_grad, part,
):
    core = lax.axis_index("seq")
    hidden = w_up.shape[1] // 2
    length = low.shape[0]
    total = None
    for active, at, own in ((active_own, core, 1), (active_other, 1 - core, 0)):
        for start in range(0, hidden, 512):
            cols = slice(start, start + 512)
            place = pl.ds(pl.multiple_of(at * hidden + start, 256), 512)
            grad = (active[length:, cols].astype(FULL) * dot_cols(low[...], w_down[place, :])).astype(LOW)
            if own:
                before_grad[:, cols] = grad
            term = dot_cols(grad, w_up[:, place])
            total = term if total is None else total + term
    part[...] = total


def enc_ff_weights_kernel(rows_count, ff_in, before_grad, active_own, active_other, low, kept, sent, payload, both):
    core = lax.axis_index("seq")
    shares = Shares(rows_count, payload, "xzy")
    for start in range(0, before_grad.shape[1], LANES):
        shares.put(dot_rows(ff_in[...], before_grad[:, start : start + LANES]))
    hidden, length = active_own.shape[1], low.shape[0]
    own = low[:, aligned(core, LANES)]
    both[aligned(core, hidden), :] = dot_rows(active_own[:length], own)
    both[aligned(1 - core, hidden), :] = dot_rows(active_other[:length], own)
    shares.put(both[...])
    shares.split(kept, sent)


def enc_attention_back_kernel(
    part, mid, gain, stream, w_mix, queries, keys, values, probs, w_query, w_key, w_value,
    low, stream_out, gain_grad, query_grad, key_grad, value_grad, table_grad, normed_part, normed_first, normed_last,
    diagonals, sums, query_grad_t,
):
    core = lax.axis_index("seq")
    width = w_query.shape[1]
    length = mid.shape[0]
    span, period = length - BLOCK, 2 * length
    back, gain_grad[...] = norm_back(mid[...], gain[...], part[...])
    stream_out[...] = stream[...] + back
    low[...] = stream_out[...].astype(LOW)
    mixed_grad = dot_cols(low[...], w_mix[...]).astype(LOW)
    sums[...] = jnp.zeros_like(sums)
    keys_t = jnp.transpose(keys[...])
    for p in range(HEADS // 4):
        weights, grads = probs[p], apart(mixed_grad[:, pair(p)])
        score_grad = score_back(weights, dot_cols(values[:, pair(p)], grads))
        put_pair(query_grad_t, p, dot(keys_t[pair(p)], score_grad))
        key_grad[:, pair(p)] = dot(score_grad, apart(queries[:, pair(p)])).astype(LOW)
        value_grad[:, pair(p)] = dot(weights, grads).astype(LOW)
        for odd in range(2):
            diagonals[...] = jnp.zeros_like(diagonals)
            for key in range(0, length, BLOCK):
                grad = score_grad[key : key + BLOCK, odd * length : (odd + 1) * length]
                diagonals[:, span - key : span - key + length] += grad.astype(FULL)
            sums[pl.ds(core * (HEADS // 2) + 2 * p + odd, 1), :] = unsheared(diagonals[...], period)
    query_grad[...] = jnp.transpose(query_grad_t[...])
    table_grad[...] = dot(sums[...], offsets(span, period, True), ((1,), (1,)), HIGH)
    normed_part[...] = (
        dot_cols(query_grad[...], w_query[...])
        + dot_cols(key_grad[...], w_key[...])
        + dot_cols(value_grad[...], w_value[...])
    )
    half = normed_first.shape[0]
    normed_first[...] = normed_part[:half].astype(LOW)
    normed_last[:half, :] = normed_part[half:].astype(LOW)
    normed_last[half:, :] = jnp.zeros((normed_last.shape[0] - half, D), LOW)
    normed_last[half : half + HEADS, :BUCKETS] = table_grad[...].astype(LOW)


def enc_finish_kernel(
    rows_count,
    normed_part, came_first, came_last, stream, x_own, x_other, gain, x_normed, query_grad, key_grad, value_grad,
    mixed_own, mixed_other, low, table_enc, table_dec, dec_squares,
    g_ff, g_final, g_self, g_cross, g_dec_ff,
    input_grad, row_norm, kept, sent,
    payload, x_all, total, both, small,
):
    core = lax.axis_index("seq")
    shares = Shares(rows_count, payload, "xyz")
    half = x_own.shape[0]
    for part, at in ((x_own, core), (x_other, 1 - core)):
        x_all[aligned(at, half), :] = part[...].astype(FULL)
    for grad in (query_grad, key_grad, value_grad):
        shares.put(dot_rows(x_normed[...], grad[...]))
    width = mixed_own.shape[0]
    own = low[:, aligned(core, LANES)]
    both[aligned(core, width), :] = dot(mixed_own[...], own)
    both[aligned(1 - core, width), :] = dot(mixed_other[...], own)
    shares.put(both[...])
    normed_grad = normed_part[...] + jnp.concatenate([came_first[...], came_last[:half]], 0).astype(FULL)
    back, gain_grad = norm_back(x_all[...], gain[...], normed_grad)
    total[...] = stream[...] + back
    input_grad[...] = total[aligned(core, half), :]
    squares = jnp.sum(total[...] * total[...], axis=0, keepdims=True) + dec_squares[...]
    row_norm[...] = jnp.sqrt(jnp.sum(squares, axis=1, keepdims=True))
    small[...] = jnp.zeros_like(small)
    small[:HEADS, :BUCKETS] = table_enc[...] + came_last[half : half + HEADS, :BUCKETS].astype(FULL)
    small[:HEADS, BLOCK : BLOCK + BUCKETS] = table_dec[...]
    for row, grad in enumerate(
        (gain_grad, g_ff[...], g_final[...], g_self[...], g_cross[...], g_dec_ff[...])
    ):
        for part in range(2):
            small[HEADS + 2 * row + part : HEADS + 2 * row + part + 1, :] = grad[:, part * LANES : (part + 1) * LANES]
    shares.split(kept, sent)
    kept[kept.shape[0] - SMALL :, :] = small[...].astype(LOW)
    if in_order(rows_count):
        sent[sent.shape[0] - SMALL :, :] = small[...].astype(LOW)


def sum_kernel(*refs, segments, extra):
    new_kept, new_sent = refs[-2:]
    row = 0
    for index, sizes in enumerate(segments):
        kept, came = refs[2 * index : 2 * index + 2]
        at = 0
        for size in sizes:
            half = size // 2
            new_sent[row : row + half] = kept[at + half : at + size] + came[at + half : at + size]
            new_kept[row : row + half] = kept[at : at + half] + came[at : at + half]
            row, at = row + half, at + size
    if extra:
        both = kept[at:] + came[at:]
        new_kept[row:] = both
        new_sent[row:] = both


def last_sum(kept, came, rows):
    return kept[rows].astype(FULL) + came[rows].astype(FULL)


def last_kernel(kept, came, *outs):
    row = 0
    for out in outs:
        lead = out.shape[0]
        if out.shape[1] < LANES:
            break
        for start in range(0, out.shape[1], LANES):
            out[:, start : start + LANES] = last_sum(kept, came, slice(row, row + lead))
            row += lead
    else:
        return
    small = last_sum(kept, came, slice(row, kept.shape[0]))
    gains = jnp.concatenate(
        [
            jnp.concatenate([small[HEADS + 2 * i + part : HEADS + 2 * i + part + 1] for i in range(6)] + [small[:2]], 0)
            for part in range(2)
        ],
        1,
    )
    lead = outs[-8].shape[1]
    start = lax.axis_index("rows") * lead
    gains = pltpu.roll(gains, jnp.where(start == 0, 0, D - start), 1)
    for i in range(6):
        outs[i - 8][...] = gains[i : i + 1, :lead]
    outs[-2][...] = small[:HEADS, :BUCKETS]
    outs[-1][...] = small[:HEADS, BLOCK : BLOCK + BUCKETS]


SMALL = 32
TAIL = [0, 1, 3, 1, 0, 2, 4, 3, 2, 1, 4, 3, 0, 4, 2, 3, 4]
COST = {
    "enc_attention": 5.0, "dec_attention": 2.9, "dec_mid": 1.9, "enc_ff": 4.5, "decoder": 9.1, "cross_back": 5.0, "enc_ff_back": 3.2,
    "enc_ff_weights": 1.9, "enc_attention_back": 6.2, "dec_back": 4.6, "enc_finish": 3.5,
}
SCALE = 1.0
SUM_COST = 0.5


def on_device(
    rows_count,
    enc_input,
    dec_input,
    enc_segments,
    dec_segments,
    cotangent,
    enc_norm_attn,
    enc_query,
    enc_key,
    enc_value,
    enc_mix,
    enc_table,
    enc_norm_ff,
    enc_up,
    enc_down,
    enc_norm_final,
    dec_norm_self,
    dec_query,
    dec_key,
    dec_value,
    dec_mix,
    dec_table,
    dec_norm_cross,
    cross_query,
    cross_key,
    cross_value,
    cross_mix,
    dec_norm_ff,
    dec_up,
    dec_down,
):
    chip, core = lax.axis_index("rows"), lax.axis_index("seq")
    x_own, d_own, c_own = enc_input[0], dec_input[0], cotangent[0]
    half, d_half = x_own.shape[0], d_own.shape[0]
    enc, dec = 2 * half, 2 * d_half
    width, hidden = D // 2, FF // 2

    def swap(values):
        return lax.ppermute(values, "seq", [(0, 1), (1, 0)])

    def row(gain):
        return gain.reshape(1, -1)

    def v(*arrays):
        return [(array, "vmem") for array in arrays]

    def h(*arrays):
        return [(array, "all") for array in arrays]

    def cols(*arrays):
        return [(array, "cols") for array in arrays]

    square = (D, D)
    ordered = in_order(rows_count)

    def payload(total, extra=0):
        if ordered:
            return [((total // 2 + extra, LANES), LOW)] * 2, [((rows_count, total // rows_count, LANES), LOW)]
        return [((total + extra, LANES), LOW), ((16, LANES), LOW)], [((1, total, LANES), LOW)]

    squares, ffs, last = payload(4 * D), payload(4 * D + FF), payload(4 * D, SMALL)

    lead = D // rows_count

    def arranged(pay, leads, extra, orders):
        if ordered:
            return pay
        places = jnp.array([[chunk_of(q, order) for q in range(rows_count)] for order in orders], jnp.int32)
        parts, start = [], 0
        for count in leads:
            parts.append(pay[0][start : start + count].reshape(rows_count, -1, LANES))
            start += count
        chunks = jnp.take(jnp.concatenate(parts, 1), places[core] ^ chip, axis=0)
        return [
            jnp.concatenate([part.reshape(-1, LANES), pay[0][start : start + extra]], 0)
            for part in (chunks[: rows_count // 2], chunks[rows_count // 2 :])
        ]

    class Sum:
        def __init__(self, pay, leads, outs, route, name, extra=0):
            self.orders = bit_orders(rows_count, route)
            self.kept, self.sent = arranged(pay, leads, extra, self.orders)
            self.segments = [self.kept.shape[0] - extra]
            self.outs, self.extra, self.name, self.stage, self.found = outs, extra, name, 0, None
            self.send()

        def send(self):
            pairs = [
                (at * 2 + c, (at ^ (1 << self.orders[c][self.stage])) * 2 + c)
                for at in range(rows_count)
                for c in range(2)
            ]
            self.came = lax.ppermute(self.sent, ("rows", "seq"), pairs)
            self.stage += 1

        def add(self, token, *others, after=()):
            if self.found is not None:
                return token
            every = (self, *others)
            for other in others:
                assert other.stage == self.stage and other.orders[0][self.stage :] == self.orders[0][self.stage :]
                assert not self.extra
            name = f"{self.name}_{self.stage}"
            operands = v(*[array for each in every for array in (each.kept, each.came)])
            if self.stage == len(self.orders[0]):
                token, self.found = call(
                    token, last_kernel, operands,
                    [out for each in every for out in each.outs], limit=8, name=name, after=after,
                )
                return token
            segments = [each.segments for each in every]
            self.extra = every[-1].extra
            self.segments = [size // 2 for sizes in segments for size in sizes]
            self.outs = [out for each in every for out in each.outs]
            shape = (sum(self.segments) + self.extra, LANES)
            token, (self.kept, self.sent) = call(
                token, functools.partial(sum_kernel, segments=segments, extra=self.extra), operands,
                [(shape, LOW)] * 2, limit=8, name=name, after=after,
            )
            self.send()
            return token

    ff_outs = [((lead, hidden), FULL), ((FF // rows_count, LANES), FULL)]
    square_outs = [((lead, LANES), FULL)] * 4
    small_outs = [((1, lead), FULL)] * 6 + [((HEADS, BUCKETS), FULL)] * 2

    x_other, d_other, c_other = swap(x_own), swap(d_own), swap(c_own)

    token, (mixed, probs, queries, keys, values, x_normed) = call(
        None,
        enc_attention_kernel,
        h(x_own) + v(x_other) + h(row(enc_norm_attn), enc_segments, enc_table.T) + cols(enc_query, enc_key, enc_value),
        [
            ((width, enc), LOW), ((HEADS // 4, enc, 2 * enc), LOW),
            ((enc, width), LOW), ((enc, width), LOW), ((enc, width), LOW), ((enc, D), LOW),
        ],
        [((HEADS, 2 * enc), FULL)],
        name="enc_attention",
    )
    mixed_other = swap(mixed)
    token, (d_probs, d_queries, d_keys, d_values, d_normed, d_mixed, d_all) = call(
        token,
        dec_attention_kernel,
        h(d_own) + v(d_other)
        + h(row(dec_norm_self), dec_segments, dec_table.T) + v(dec_query, dec_key, dec_value),
        [((HEADS // 2, dec, 2 * dec), LOW)] + [((dec, D), LOW)] * 4 + [((D, dec), LOW), ((dec, D), FULL)],
        name="dec_attention", after=[c_other],
    )
    token, (mid, after_part, after_low, active, ff_in) = call(
        token,
        enc_ff_kernel,
        h(x_own) + v(x_other, mixed, mixed_other)
        + [(enc_mix, "rows"), (enc_mix, "rows_other"), (row(enc_norm_ff), "all")] + v(enc_up, enc_down),
        [((enc, D), FULL), ((enc, D), FULL), ((enc, D), LOW), ((2 * enc, hidden), LOW), ((enc, D), LOW)],
        name="enc_ff",
    )
    after_came = swap(after_low)
    token, (d_mid, cross_in, cross_queries) = call(
        token,
        dec_mid_kernel,
        v(d_all, d_mixed, dec_mix) + h(row(dec_norm_cross)) + v(cross_query),
        [((dec, D), FULL), ((dec, D), LOW), ((dec, D), LOW)],
        name="dec_mid",
    )
    token, (
        enc_result, after, state, c_keys, c_values, c_probs, c_mixed, dec_result, stream, g_dec_ff, *pay_first, active,
    ) = call(
        token,
        functools.partial(decoder_kernel, rows_count),
        v(after_part, after_came) + h(row(enc_norm_final), enc_segments, dec_segments) + v(cross_queries, d_mid)
        + h(row(dec_norm_ff), c_own) + v(c_other, cross_key, cross_value, cross_mix, dec_up, dec_down),
        [
            ((half, D), FULL), ((enc, D), FULL), ((enc, D), LOW), ((enc, D), LOW), ((enc, D), LOW),
            ((HEADS // 2, enc, 2 * dec), LOW), ((D, dec), LOW), ((d_half, D), FULL), ((dec, D), FULL), ((1, D), FULL),
        ] + ffs[0],
        ffs[1] + [((dec, D), FULL), ((dec, D), LOW), ((dec, D), FULL), ((dec, FF), LOW), ((dec, FF), LOW)],
        name="decoder", through=[active],
    )
    active_other = swap(active)
    first = Sum(pay_first, [D] * 4 + [FF], ff_outs, "xyz", "sum_dec_ff")
    token, (enc_stream, enc_low, g_final, stream, g_cross, *pay_cross) = call(
        token,
        functools.partial(cross_back_kernel, rows_count),
        v(stream, d_mid) + h(row(dec_norm_cross)) + v(cross_in, cross_queries, c_keys, c_values, c_probs, c_mixed, state, after,
          )
        + h(row(enc_norm_final)) + v(cross_mix, cross_key, cross_value, cross_query),
        [((enc, D), FULL), ((enc, D), LOW), ((1, D), FULL), ((dec, D), FULL), ((1, D), FULL)] + squares[0],
        squares[1] + [((dec, D), LOW), ((D, dec), LOW), ((dec, D), LOW), ((enc, D), LOW), ((enc, D), LOW)],
        name="cross_back",
    )
    second = Sum(pay_cross, [D] * 4, square_outs, "zxy", "sum_cross")
    token, (before_grad, part) = call(
        token,
        enc_ff_back_kernel,
        v(enc_low, active, active_other)
        + v(enc_down, enc_up),
        [((enc, hidden), LOW), ((enc, D), FULL)],
        name="enc_ff_back",
    )
    token, pay_enc_ff = call(
        token,
        functools.partial(enc_ff_weights_kernel, rows_count),
        v(ff_in, before_grad, active, active_other, enc_low),
        ffs[0],
        ffs[1] + [((FF, LANES), FULL)],
        name="enc_ff_weights",
    )
    third = Sum(pay_enc_ff, [D] * 4 + [FF], ff_outs, "xzy", "sum_enc_ff")
    token = first.add(token)
    token, (low, enc_stream, g_ff, query_grad, key_grad, value_grad, table_enc, normed_part, *normed_low) = call(
        token,
        enc_attention_back_kernel,
        v(part, mid) + h(row(enc_norm_ff)) + v(enc_stream) + [(enc_mix, "rows")]
        + v(queries, keys, values, probs) + cols(enc_query, enc_key, enc_value),
        [
            ((enc, D), LOW), ((enc, D), FULL), ((1, D), FULL), ((enc, width), LOW), ((enc, width), LOW),
            ((enc, width), LOW), ((HEADS, BUCKETS), FULL), ((enc, D), FULL), ((half, D), LOW),
            ((half + 16, D), LOW),
        ],
        [((BLOCK, 2 * enc), FULL), ((HEADS, 2 * enc), FULL), ((width, enc), LOW)],
        name="enc_attention_back",
    )
    normed_came = [swap(part) for part in normed_low]
    token, (dec_input_grad, g_self, table_dec, dec_squares, *pay_dec) = call(
        token,
        functools.partial(dec_back_kernel, rows_count),
        v(stream) + h(d_own) + v(d_other) + h(row(dec_norm_self))
        + v(d_normed, d_queries, d_keys, d_values, d_probs, d_mixed)
        + v(dec_mix, dec_query, dec_key, dec_value),
        [((d_half, D), FULL), ((1, D), FULL), ((HEADS, BUCKETS), FULL), ((1, D), FULL)] + squares[0],
        squares[1] + [((dec, D), LOW), ((D, dec), LOW)] + [((dec, D), LOW)] * 3 + [((HEADS, 2 * BLOCK), FULL), ((dec, D), FULL), ((dec, D), FULL)],
        name="dec_back",
    )
    fourth = Sum(pay_dec, [D] * 4, square_outs, "xzy", "sum_dec")
    token = third.add(token)
    token = second.add(token)
    token, (enc_input_grad, row_norm, *pay_enc) = call(
        token,
        functools.partial(enc_finish_kernel, rows_count),
        v(normed_part, *normed_came, enc_stream) + h(x_own) + v(x_other) + h(row(enc_norm_attn)) + v(x_normed, query_grad, key_grad,
          value_grad, mixed, mixed_other, low, table_enc, table_dec, dec_squares, g_ff, g_final, g_self, g_cross,
          g_dec_ff),
        [((half, D), FULL), ((1, 1), FULL)] + last[0],
        last[1] + [((enc, D), FULL), ((enc, D), FULL), ((D, LANES), FULL), ((SMALL, LANES), FULL)],
        name="enc_finish",
    )

    fifth = Sum(pay_enc, [D] * 4, square_outs + small_outs, "xyz", "sum_enc", SMALL)
    sums = [first, second, third, fourth, fifth]
    for which in TAIL:
        token = sums[which].add(token)
    while any(each.found is None for each in sums):
        for each in sums:
            token = each.add(token)
    dec_u, dec_d = first.found
    enc_u, enc_d = third.found
    cross_q, cross_k, cross_v, cross_m = second.found
    dec_q, dec_k, dec_v, dec_m = fourth.found
    enc_q, enc_k, enc_v, enc_m, *small = fifth.found
    gains = [gain[0] for gain in small[:6]]
    tables = [small[6].T, small[7].T]
    return (
        enc_result[None], dec_result[None], enc_input_grad[None], dec_input_grad[None], row_norm[0],
        gains[0], enc_q, enc_k, enc_v, enc_m, tables[0], gains[1], enc_u, enc_d, gains[2],
        gains[3], dec_q, dec_k, dec_v, dec_m, tables[1], gains[4], cross_q, cross_k, cross_v, cross_m,
        gains[5], dec_u, dec_d,
    )


def solution(mesh):
    split, line, copied = P("rows", "seq", None), P("rows", None), P()
    in_specs = (split, split, line, line, split) + (copied,) * 24
    block, vector = P("rows", "seq"), P("rows")
    out_specs = (
        (split,) * 4 + (vector,)
        + (vector,) + (block,) * 4 + (copied, vector, block, block, vector)
        + (vector,) + (block,) * 4 + (copied, vector) + (block,) * 4 + (vector, block, block)
    )
    return jax.shard_map(
        functools.partial(on_device, mesh.shape["rows"]),
        mesh=mesh, in_specs=in_specs, out_specs=out_specs, check_vma=False,
    )
```

```python
import functools
import math

import jax
import jax.numpy as jnp
from jax import lax
from jax.experimental import pallas as pl
from jax.experimental.pallas import tpu as pltpu
from jax.sharding import PartitionSpec as P

D = 512
HEADS = 8
HEAD = 64
FF = 2048
BUCKETS = 32
MAX_DIST = 128
NDOC = 4
EPSILON = 1e-06
NEGATIVE = -1e30
BLOCK = 128
LANES = 256

LOW = jnp.bfloat16
FULL = jnp.float32
HIGH = lax.Precision.HIGHEST


def cut_points(exact_span, bucket_half, reach):
    points = []
    for target in range(exact_span + 1, bucket_half):
        reach_at = exact_span
        while (
            exact_span
            + int(
                math.log(reach_at / exact_span)
                / math.log(reach / exact_span)
                * (bucket_half - exact_span)
            )
            < target
        ):
            reach_at += 1
        points.append(reach_at)
    return points


def bucket_index(offset, both_ways):
    if both_ways:
        bucket_half = BUCKETS // 2
        base_index = jnp.where(offset > 0, bucket_half, 0).astype(jnp.int32)
        distance = jnp.abs(offset)
    else:
        bucket_half = BUCKETS
        base_index = jnp.zeros_like(offset)
        distance = jnp.maximum(-offset, 0)
    exact_span = bucket_half // 2
    result = base_index + jnp.minimum(distance, exact_span)
    for border in cut_points(exact_span, bucket_half, MAX_DIST):
        result = result + (distance >= border).astype(jnp.int32)
    return result


def dot(left, right, dims=((1,), (0,)), precision=None):
    return lax.dot_general(
        left, right, (dims, ((), ())), preferred_element_type=FULL, precision=precision
    )


def dot_cols(left, right):
    return dot(left, right, ((1,), (1,)))


def dot_rows(left, right):
    return dot(left, right, ((0,), (0,)))


def scale_of(values):
    return lax.rsqrt(jnp.mean(values * values, axis=-1, keepdims=True) + EPSILON)


def normed(values, gain):
    return (values * scale_of(values) * gain).astype(LOW)


def norm_back(values, gain, grad):
    scale = scale_of(values)
    unit = values * scale
    gain_grad = jnp.sum(grad * unit, axis=0, keepdims=True)
    grad = grad * gain
    return scale * (grad - unit * jnp.mean(grad * unit, axis=-1, keepdims=True)), gain_grad


def gelu_pair(values):
    root = math.sqrt(2.0 / math.pi)
    square = values * values
    tanh = jnp.tanh(root * values * (1.0 + 0.044715 * square))
    half = 0.5 + 0.5 * tanh
    slope = half + 0.5 * values * (1.0 - tanh * tanh) * (root + (3 * 0.044715 * root) * square)
    return values * half, slope


def iota(shape, axis):
    return lax.broadcasted_iota(jnp.int32, shape, axis)


def offsets(span, period, both_ways):
    place = iota((1, period), 1)
    offset = span - jnp.where(place < period - BLOCK, place, place - period)
    return (bucket_index(offset, both_ways) == iota((BUCKETS, period), 0)).astype(FULL)


def sheared(row, period):
    return pltpu.roll(
        jnp.broadcast_to(row, (BLOCK, period)), 0, 1, stride=1, stride_axis=0
    )


def unsheared(sums, period):
    rows = sums.shape[0]
    while rows > 8:
        rows //= 2
        sums = sums[:rows] + pltpu.roll(sums[rows:], period - rows, 1)
    total = sums[:1]
    for row in range(1, 8):
        total = total + pltpu.roll(sums[row : row + 1], period - row, 1)
    return total


def doc_columns(ids):
    wide = jnp.broadcast_to(ids.astype(FULL), (BLOCK, ids.shape[1]))
    return jnp.transpose(wide)


def doc_marks(ids):
    columns = doc_columns(ids)
    lane = iota(columns.shape, 1)
    same = columns == lane.astype(FULL)
    query_marks = jnp.where((lane < NDOC) & jnp.logical_not(same), NEGATIVE, 0.0).astype(LOW)
    return query_marks, same.astype(FULL).astype(LOW)


def apart(values):
    lane = iota(values.shape, 1)
    zeros = jnp.zeros_like(values)
    return jnp.concatenate([jnp.where(lane < HEAD, values, zeros), jnp.where(lane >= HEAD, values, zeros)], 0)


def pair_scores(key_pair, query_pair, key_marks, query_marks):
    left = jnp.concatenate([key_pair, key_marks], 1)
    right = jnp.concatenate([apart(query_pair), jnp.concatenate([query_marks, query_marks], 0)], 1)
    return dot_cols(left, right)


def put_pair(target, p, both):
    length = both.shape[1] // 2
    target[one(2 * p), :] = both[:HEAD, :length].astype(LOW)
    target[one(2 * p + 1), :] = both[HEAD:, length:].astype(LOW)


def softmax(scores):
    weights = jnp.exp(scores - jnp.max(scores, axis=0, keepdims=True))
    return (weights * (1.0 / jnp.sum(weights, axis=0, keepdims=True))).astype(LOW)


def score_back(probs, probs_grad):
    probs = probs.astype(FULL)
    inner = jnp.sum(probs * probs_grad, axis=0, keepdims=True)
    return (probs * (probs_grad - inner)).astype(LOW)


def one(head):
    return slice(head * HEAD, (head + 1) * HEAD)


def pair(index):
    return slice(index * 2 * HEAD, (index + 1) * 2 * HEAD)


def aligned(index, size):
    return pl.ds(pl.multiple_of(index * size, size), size)


class Lazy:
    def __init__(self, ref, copy):
        self.ref, self.copy = ref, copy

    @property
    def shape(self):
        return self.ref.shape

    def __getitem__(self, index):
        if self.copy is not None:
            self.copy.wait()
            self.copy = None
        return self.ref[index]


def cut(source, mode):
    if mode == "all":
        return source
    core = lax.axis_index("seq")
    rows, cols = source.shape
    at = 1 - core if mode.endswith("other") else core
    if mode.startswith("cols"):
        return source.at[:, aligned(at, cols // 2)]
    return source.at[aligned(at, rows // 2), :]


def cut_shape(shape, mode):
    if mode == "all":
        return shape
    return (shape[0], shape[1] // 2) if mode.startswith("cols") else (shape[0] // 2, shape[1])


ROUTES = {"dec_ff": "xywz", "cross": "zxyw", "enc_ff": "xzyw", "dec": "xzyw", "enc": "xyzw"}


def bit_orders(rows_count, payload):
    bits = list(range(rows_count.bit_length() - 1))
    if len(bits) < 4:
        return (bits, bits)
    first = ["xyzw".index(axis) for axis in ROUTES[payload]] + bits[4:]
    return (first, [{0: 1, 1: 0}.get(bit, bit) for bit in first])


def place_of(chunk, order):
    bits = len(order)
    return sum(((chunk >> order[s]) & 1) << (bits - 1 - s) for s in range(bits))


def chunk_of(place, order):
    bits = len(order)
    return sum(((place >> (bits - 1 - s)) & 1) << order[s] for s in range(bits))


def in_order(rows_count):
    return (D // rows_count) % 16 == 0


class Shares:
    def __init__(self, rows_count, payload, route):
        self.rows_count, self.payload, self.row = rows_count, payload, 0
        core, chip = lax.axis_index("seq"), lax.axis_index("rows")
        orders = bit_orders(rows_count, route)
        own = [place_of(chip, order) for order in orders]
        self.places = [
            jnp.where(core == 0, place_of(chunk, orders[0]) ^ own[0], place_of(chunk, orders[1]) ^ own[1])
            for chunk in range(rows_count)
        ] if in_order(rows_count) else [0]

    def put(self, grad):
        chunks = len(self.places)
        lead = grad.shape[0] // chunks
        for chunk in range(chunks):
            self.payload[self.places[chunk], self.row : self.row + lead, :] = grad[
                chunk * lead : (chunk + 1) * lead
            ].astype(LOW)
        self.row += lead

    def split(self, kept, sent):
        if not in_order(self.rows_count):
            kept[: self.row] = self.payload[0]
            return
        half = self.rows_count // 2
        shape = (half * self.row, LANES)
        sent[: half * self.row] = self.payload[half:].reshape(shape)
        kept[: half * self.row] = self.payload[:half].reshape(shape)


VMEM = pl.BlockSpec(memory_space=pltpu.VMEM)
HBM = pl.BlockSpec(memory_space=pltpu.HBM)
ANY = pl.BlockSpec(memory_space=pl.ANY)
MIB = 1024 * 1024


def call(token, kernel, ins, outs, scratch=(), limit=24, name=None, after=(), through=()):
    n_ins, n_outs = len(ins), len(outs)
    ins = list(ins) + [(token, "vmem")] * (token is not None) + [(array, "any") for array in (*after, *through)]
    outs = list(outs) + [(array.shape, array.dtype) for array in through] + [((8, BLOCK), FULL)]
    specs = [{"vmem": VMEM, "any": ANY}.get(how, HBM) for _, how in ins]
    arrays = [
        array if how in ("vmem", "any") else pltpu.with_memory_space_constraint(array, pltpu.HBM) for array, how in ins
    ]
    shapes = [jax.ShapeDtypeStruct(shape, kind) for shape, kind in outs]
    lazy = [i for i, (_, how) in enumerate(ins) if how not in ("vmem", "any")]
    scratch = [pltpu.VMEM(shape, kind) for shape, kind in scratch]
    n_own = len(scratch)
    scratch += [pltpu.VMEM(cut_shape(arrays[i].shape, ins[i][1]), arrays[i].dtype) for i in lazy]
    if lazy:
        scratch.append(pltpu.SemaphoreType.DMA((len(lazy),)))

    def body(*refs):
        operands = list(refs[: len(ins)])
        rest = refs[len(ins) :]
        results, own = rest[: len(outs)], rest[len(outs) : len(outs) + n_own]
        landing = rest[len(outs) + n_own :]
        for place, i in enumerate(lazy):
            copy = pltpu.make_async_copy(cut(operands[i], ins[i][1]), landing[place], landing[-1].at[place])
            copy.start()
            operands[i] = Lazy(landing[place], copy)
        results[-1][...] = jnp.zeros((8, BLOCK), FULL)
        kernel(*operands[:n_ins], *results[: n_outs], *own)
        for i in lazy:
            if operands[i].copy is not None:
                operands[i].copy.wait()

    found = pl.pallas_call(
        body,
        out_shape=shapes,
        in_specs=specs,
        out_specs=[VMEM] * n_outs + [ANY] * len(through) + [VMEM],
        input_output_aliases={len(ins) - len(through) + i: n_outs + i for i in range(len(through))},
        scratch_shapes=scratch,
        compiler_params=pltpu.CompilerParams(vmem_limit_bytes=limit * MIB),
        cost_estimate=pl.CostEstimate(
            flops=1000 + int(SCALE * COST.get(name, SUM_COST) * 1.15e9), bytes_accessed=1000, transcendentals=0
        ),
        name=name,
    )(*arrays)
    return found[-1], found[:-1]


def enc_attention_kernel(
    x_own, x_other, gain, ids, table, w_query, w_key, w_value,
    mixed, probs, queries, keys, values, x_normed,
    biases,
):
    core = lax.axis_index("seq")
    width = w_query.shape[1]
    half = x_own.shape[0]
    length = 2 * half
    for part, at in ((x_own, core), (x_other, 1 - core)):
        x_normed[aligned(at, half), :] = normed(part[...].astype(FULL), gain[...])
    span, period = length - BLOCK, 2 * length
    biases[...] = dot(table[...], offsets(span, period, True), precision=HIGH)
    query_marks, key_marks = doc_marks(ids[...])
    for weight, target in zip((w_query, w_key, w_value), (queries, keys, values)):
        target[...] = dot(x_normed[...], weight[...]).astype(LOW)
    values_t = jnp.transpose(values[...])
    for p in range(HEADS // 4):
        shift = []
        for head in (2 * p, 2 * p + 1):
            bias = sheared(biases[pl.ds(core * (HEADS // 2) + head, 1), :], period)
            shift.append(jnp.concatenate([bias[:, span - key : span - key + length] for key in range(0, length, BLOCK)], 0))
        scores = pair_scores(keys[:, pair(p)], queries[:, pair(p)], key_marks, query_marks)
        weights = softmax(scores + jnp.concatenate(shift, 1))
        probs[p] = weights
        put_pair(mixed, p, dot(values_t[pair(p)], weights))


def dec_attention_kernel(
    x_own, x_other, gain, ids, table, w_query, w_key, w_value,
    probs, queries, keys, values, x_normed, mixed, x_all,
):
    core = lax.axis_index("seq")
    half = x_own.shape[0]
    length = 2 * half
    for part, at in ((x_own, core), (x_other, 1 - core)):
        x_all[aligned(at, half), :] = part[...].astype(FULL)
    x_normed[...] = normed(x_all[...], gain[...])
    period = 2 * BLOCK
    biases = dot(table[...], offsets(0, period, False), precision=HIGH)
    query_marks, key_marks = doc_marks(ids[...])
    later = iota((BLOCK, BLOCK), 0) > iota((BLOCK, BLOCK), 1)
    for weight, target in zip((w_query, w_key, w_value), (queries, keys, values)):
        target[...] = dot(x_normed[...], weight[...]).astype(LOW)
    values_t = jnp.transpose(values[...])
    for p in range(HEADS // 2):
        bias = [
            jnp.where(later, NEGATIVE, sheared(biases[head : head + 1], period)[:, :length]) for head in (2 * p, 2 * p + 1)
        ]
        scores = pair_scores(keys[:, pair(p)], queries[:, pair(p)], key_marks, query_marks)
        weights = softmax(scores + jnp.concatenate(bias, 1))
        probs[p] = weights
        put_pair(mixed, p, dot(values_t[pair(p)], weights))


def dec_mid_kernel(x_all, mixed, w_mix, gain_cross, w_cross, mid, cross_in, cross_queries):
    mid[...] = x_all[...] + dot_rows(mixed[...], w_mix[...])
    cross_in[...] = normed(mid[...], gain_cross[...])
    cross_queries[...] = dot(cross_in[...], w_cross[...]).astype(LOW)


def enc_ff_kernel(
    x_own, x_other, mixed_own, mixed_other, mix_own, mix_other, gain, w_up, w_down,
    mid, after, after_low, active, ff_in,
):
    core = lax.axis_index("seq")
    hidden = w_up.shape[1] // 2
    half = x_own.shape[0]
    length = 2 * half
    for part, at in ((x_own, core), (x_other, 1 - core)):
        mid[aligned(at, half), :] = part[...].astype(FULL)
    mid[...] += dot_rows(mixed_own[...], mix_own[...]) + dot_rows(mixed_other[...], mix_other[...])
    ff_in[...] = normed(mid[...], gain[...])
    total = None
    for start in range(0, hidden, 512):
        cols = slice(start, start + 512)
        place = pl.ds(pl.multiple_of(core * hidden + start, 256), 512)
        act, grow = gelu_pair(dot(ff_in[...], w_up[:, place]))
        act = act.astype(LOW)
        active[:length, cols] = act
        active[length:, cols] = grow.astype(LOW)
        term = dot(act, w_down[place, :])
        total = term if total is None else total + term
    after[...] = mid[...] + total
    after_low[...] = total.astype(LOW)


def decoder_kernel(
    rows_count,
    after_part, came, gain_final, enc_ids, dec_ids, cross_queries, dec_mid, gain_ff, cot_own, cot_other,
    w_key, w_value, w_mix, w_up, w_down,
    enc_result, after, state, keys, values, probs, mixed, dec_result, stream, gain_grad, kept, sent,
    payload, cross, cot, out, before_grad, active,
):
    core = lax.axis_index("seq")
    length = dec_mid.shape[0]
    half, enc_half = length // 2, after.shape[0] // 2
    for part, at in ((cot_own, core), (cot_other, 1 - core)):
        cot[aligned(at, half), :] = part[...]
    after[...] = after_part[...] + came[...].astype(FULL)
    enc_result[...] = after[aligned(core, enc_half), :]
    state[...] = normed(after[...], gain_final[...])
    _, key_marks = doc_marks(enc_ids[...])
    query_marks, _ = doc_marks(dec_ids[...])
    keys[...] = dot(state[...], w_key[...]).astype(LOW)
    values[...] = dot(state[...], w_value[...]).astype(LOW)
    values_t = jnp.transpose(values[...])
    for p in range(HEADS // 2):
        weights = softmax(pair_scores(keys[:, pair(p)], cross_queries[:, pair(p)], key_marks, query_marks))
        probs[p] = weights
        put_pair(mixed, p, dot(values_t[pair(p)], weights))
    cross[...] = dec_mid[...] + dot_rows(mixed[...], w_mix[...])
    ff_in = normed(cross[...], gain_ff[...])
    total = cross[...]
    normed_grad = jnp.zeros_like(total)
    for start in range(0, FF, 2048):
        cols = slice(start, start + 2048)
        act, grow = gelu_pair(dot(ff_in, w_up[:, cols]))
        act = act.astype(LOW)
        active[:, cols] = act
        total = total + dot(act, w_down[cols, :])
        grad = (grow * dot_cols(cot[...], w_down[cols, :])).astype(LOW)
        before_grad[:, cols] = grad
        normed_grad = normed_grad + dot_cols(grad, w_up[:, cols])
    out[...] = total
    dec_result[...] = out[aligned(core, half), :]
    shares = Shares(rows_count, payload, "dec_ff")
    for start in range(0, FF // 2, LANES):
        shares.put(dot_rows(ff_in, before_grad[:, pl.ds(pl.multiple_of(core * (FF // 2) + start, LANES), LANES)]))
    shares.put(dot_rows(active[...], cot[:, aligned(core, LANES)]))
    shares.split(kept, sent)
    back, gain_grad[...] = norm_back(cross[...], gain_ff[...], normed_grad)
    stream[...] = cot[...].astype(FULL) + back


def cross_back_kernel(
    rows_count,
    stream, dec_mid, gain_cross, cross_in, queries, keys, values, probs, mixed, state, after, gain_final,
    w_mix, w_key, w_value, w_query,
    enc_stream, enc_low, gain_final_grad, stream_out, gain_grad, kept, sent,
    payload, low, query_grad_t, query_grad, key_grad, value_grad,
):
    core = lax.axis_index("seq")
    shares = Shares(rows_count, payload, "cross")
    low[...] = stream[...].astype(LOW)
    mixed_grad = dot_cols(low[...], w_mix[...]).astype(LOW)
    keys_t = jnp.transpose(keys[...])
    for p in range(HEADS // 2):
        weights, grads = probs[p], apart(mixed_grad[:, pair(p)])
        score_grad = score_back(weights, dot_cols(values[:, pair(p)], grads))
        put_pair(query_grad_t, p, dot(keys_t[pair(p)], score_grad))
        key_grad[:, pair(p)] = dot(score_grad, apart(queries[:, pair(p)])).astype(LOW)
        value_grad[:, pair(p)] = dot(weights, grads).astype(LOW)
    query_grad[...] = jnp.transpose(query_grad_t[...])
    state_grad = dot_cols(key_grad[...], w_key[...]) + dot_cols(value_grad[...], w_value[...])
    back, gain_final_grad[...] = norm_back(after[...], gain_final[...], state_grad)
    enc_stream[...] = back
    enc_low[...] = back.astype(LOW)
    back, gain_grad[...] = norm_back(dec_mid[...], gain_cross[...], dot_cols(query_grad[...], w_query[...]))
    stream_out[...] = stream[...] + back
    own = aligned(core, LANES)
    shares.put(dot_rows(cross_in[...], query_grad[:, own]))
    shares.put(dot_rows(state[...], key_grad[:, own]))
    shares.put(dot_rows(state[...], value_grad[:, own]))
    shares.put(dot(mixed[...], low[:, own]))
    shares.split(kept, sent)


def dec_back_kernel(
    rows_count,
    stream, x_own, x_other, gain, x_normed, queries, keys, values, probs, mixed,
    w_mix, w_query, w_key, w_value,
    input_grad, gain_grad, table_grad, squares, kept, sent,
    payload, low, query_grad_t, query_grad, key_grad, value_grad, sums, x_all, total,
):
    core = lax.axis_index("seq")
    shares = Shares(rows_count, payload, "dec")
    half = x_own.shape[0]
    length = 2 * half
    for part, at in ((x_own, core), (x_other, 1 - core)):
        x_all[aligned(at, half), :] = part[...].astype(FULL)
    low[...] = stream[...].astype(LOW)
    mixed_grad = dot_cols(low[...], w_mix[...]).astype(LOW)
    period = 2 * BLOCK
    keys_t = jnp.transpose(keys[...])
    for p in range(HEADS // 2):
        weights, grads = probs[p], apart(mixed_grad[:, pair(p)])
        score_grad = score_back(weights, dot_cols(values[:, pair(p)], grads))
        put_pair(query_grad_t, p, dot(keys_t[pair(p)], score_grad))
        key_grad[:, pair(p)] = dot(score_grad, apart(queries[:, pair(p)])).astype(LOW)
        value_grad[:, pair(p)] = dot(weights, grads).astype(LOW)
        for odd in range(2):
            head, grad = 2 * p + odd, score_grad[:, odd * length : (odd + 1) * length].astype(FULL)
            wide = jnp.concatenate([grad, jnp.zeros((BLOCK, BLOCK), FULL)], axis=1)
            sums[head : head + 1, :] = unsheared(wide, period)
    query_grad[...] = jnp.transpose(query_grad_t[...])
    table_grad[...] = dot(sums[...], offsets(0, period, False), ((1,), (1,)), HIGH)
    normed_grad = (
        dot_cols(query_grad[...], w_query[...])
        + dot_cols(key_grad[...], w_key[...])
        + dot_cols(value_grad[...], w_value[...])
    )
    back, gain_grad[...] = norm_back(x_all[...], gain[...], normed_grad)
    total[...] = stream[...] + back
    input_grad[...] = total[aligned(core, half), :]
    squares[...] = jnp.sum(total[...] * total[...], axis=0, keepdims=True)
    own = aligned(core, LANES)
    for grad in (query_grad, key_grad, value_grad):
        shares.put(dot_rows(x_normed[...], grad[:, own]))
    shares.put(dot(mixed[...], low[:, own]))
    shares.split(kept, sent)


def enc_ff_back_kernel(
    low, active_own, active_other, w_down, w_up,
    before_grad, part,
):
    core = lax.axis_index("seq")
    hidden = w_up.shape[1] // 2
    length = low.shape[0]
    total = None
    for active, at, own in ((active_own, core, 1), (active_other, 1 - core, 0)):
        for start in range(0, hidden, 512):
            cols = slice(start, start + 512)
            place = pl.ds(pl.multiple_of(at * hidden + start, 256), 512)
            grad = (active[length:, cols].astype(FULL) * dot_cols(low[...], w_down[place, :])).astype(LOW)
            if own:
                before_grad[:, cols] = grad
            term = dot_cols(grad, w_up[:, place])
            total = term if total is None else total + term
    part[...] = total


def enc_ff_weights_kernel(rows_count, ff_in, before_grad, active_own, active_other, low, kept, sent, payload, both):
    core = lax.axis_index("seq")
    shares = Shares(rows_count, payload, "enc_ff")
    for start in range(0, before_grad.shape[1], LANES):
        shares.put(dot_rows(ff_in[...], before_grad[:, start : start + LANES]))
    hidden, length = active_own.shape[1], low.shape[0]
    own = low[:, aligned(core, LANES)]
    both[aligned(core, hidden), :] = dot_rows(active_own[:length], own)
    both[aligned(1 - core, hidden), :] = dot_rows(active_other[:length], own)
    shares.put(both[...])
    shares.split(kept, sent)


def enc_attention_back_kernel(
    part, mid, gain, stream, w_mix, queries, keys, values, probs, w_query, w_key, w_value,
    low, stream_out, gain_grad, query_grad, key_grad, value_grad, table_grad, normed_part, normed_first, normed_last,
    diagonals, sums, query_grad_t,
):
    core = lax.axis_index("seq")
    width = w_query.shape[1]
    length = mid.shape[0]
    span, period = length - BLOCK, 2 * length
    back, gain_grad[...] = norm_back(mid[...], gain[...], part[...])
    stream_out[...] = stream[...] + back
    low[...] = stream_out[...].astype(LOW)
    mixed_grad = dot_cols(low[...], w_mix[...]).astype(LOW)
    sums[...] = jnp.zeros_like(sums)
    keys_t = jnp.transpose(keys[...])
    for p in range(HEADS // 4):
        weights, grads = probs[p], apart(mixed_grad[:, pair(p)])
        score_grad = score_back(weights, dot_cols(values[:, pair(p)], grads))
        put_pair(query_grad_t, p, dot(keys_t[pair(p)], score_grad))
        key_grad[:, pair(p)] = dot(score_grad, apart(queries[:, pair(p)])).astype(LOW)
        value_grad[:, pair(p)] = dot(weights, grads).astype(LOW)
        for odd in range(2):
            diagonals[...] = jnp.zeros_like(diagonals)
            for key in range(0, length, BLOCK):
                grad = score_grad[key : key + BLOCK, odd * length : (odd + 1) * length]
                diagonals[:, span - key : span - key + length] += grad.astype(FULL)
            sums[pl.ds(core * (HEADS // 2) + 2 * p + odd, 1), :] = unsheared(diagonals[...], period)
    query_grad[...] = jnp.transpose(query_grad_t[...])
    table_grad[...] = dot(sums[...], offsets(span, period, True), ((1,), (1,)), HIGH)
    normed_part[...] = (
        dot_cols(query_grad[...], w_query[...])
        + dot_cols(key_grad[...], w_key[...])
        + dot_cols(value_grad[...], w_value[...])
    )
    half = normed_first.shape[0]
    normed_first[...] = normed_part[:half].astype(LOW)
    normed_last[:half, :] = normed_part[half:].astype(LOW)
    normed_last[half:, :] = jnp.zeros((normed_last.shape[0] - half, D), LOW)
    normed_last[half : half + HEADS, :BUCKETS] = table_grad[...].astype(LOW)


def enc_finish_kernel(
    rows_count,
    normed_part, came_first, came_last, stream, x_own, x_other, gain, x_normed, query_grad, key_grad, value_grad,
    mixed_own, mixed_other, low, table_enc, table_dec, dec_squares,
    g_ff, g_final, g_self, g_cross, g_dec_ff,
    input_grad, row_norm, kept, sent,
    payload, x_all, total, both, small,
):
    core = lax.axis_index("seq")
    shares = Shares(rows_count, payload, "enc")
    half = x_own.shape[0]
    for part, at in ((x_own, core), (x_other, 1 - core)):
        x_all[aligned(at, half), :] = part[...].astype(FULL)
    for grad in (query_grad, key_grad, value_grad):
        shares.put(dot_rows(x_normed[...], grad[...]))
    width = mixed_own.shape[0]
    own = low[:, aligned(core, LANES)]
    both[aligned(core, width), :] = dot(mixed_own[...], own)
    both[aligned(1 - core, width), :] = dot(mixed_other[...], own)
    shares.put(both[...])
    normed_grad = normed_part[...] + jnp.concatenate([came_first[...], came_last[:half]], 0).astype(FULL)
    back, gain_grad = norm_back(x_all[...], gain[...], normed_grad)
    total[...] = stream[...] + back
    input_grad[...] = total[aligned(core, half), :]
    squares = jnp.sum(total[...] * total[...], axis=0, keepdims=True) + dec_squares[...]
    row_norm[...] = jnp.sqrt(jnp.sum(squares, axis=1, keepdims=True))
    small[...] = jnp.zeros_like(small)
    small[:HEADS, :BUCKETS] = table_enc[...] + came_last[half : half + HEADS, :BUCKETS].astype(FULL)
    small[:HEADS, BLOCK : BLOCK + BUCKETS] = table_dec[...]
    for row, grad in enumerate(
        (gain_grad, g_ff[...], g_final[...], g_self[...], g_cross[...], g_dec_ff[...])
    ):
        for part in range(2):
            small[HEADS + 2 * row + part : HEADS + 2 * row + part + 1, :] = grad[:, part * LANES : (part + 1) * LANES]
    shares.split(kept, sent)
    kept[kept.shape[0] - SMALL :, :] = small[...].astype(LOW)
    if in_order(rows_count):
        sent[sent.shape[0] - SMALL :, :] = small[...].astype(LOW)


def sum_kernel(*refs, segments, extra):
    new_kept, new_sent = refs[-2:]
    row = 0
    for index, sizes in enumerate(segments):
        kept, came = refs[2 * index : 2 * index + 2]
        at = 0
        for size in sizes:
            half = size // 2
            new_sent[row : row + half] = kept[at + half : at + size] + came[at + half : at + size]
            new_kept[row : row + half] = kept[at : at + half] + came[at : at + half]
            row, at = row + half, at + size
    if extra:
        both = kept[at:] + came[at:]
        new_kept[row:] = both
        new_sent[row:] = both


def last_sum(kept, came, rows):
    return kept[rows].astype(FULL) + came[rows].astype(FULL)


def last_kernel(kept, came, *outs):
    row = 0
    for out in outs:
        lead = out.shape[0]
        if out.shape[1] < LANES:
            break
        for start in range(0, out.shape[1], LANES):
            out[:, start : start + LANES] = last_sum(kept, came, slice(row, row + lead))
            row += lead
    else:
        return
    small = last_sum(kept, came, slice(row, kept.shape[0]))
    gains = jnp.concatenate(
        [
            jnp.concatenate([small[HEADS + 2 * i + part : HEADS + 2 * i + part + 1] for i in range(6)] + [small[:2]], 0)
            for part in range(2)
        ],
        1,
    )
    lead = outs[-8].shape[1]
    start = lax.axis_index("rows") * lead
    gains = pltpu.roll(gains, jnp.where(start == 0, 0, D - start), 1)
    for i in range(6):
        outs[i - 8][...] = gains[i : i + 1, :lead]
    outs[-2][...] = small[:HEADS, :BUCKETS]
    outs[-1][...] = small[:HEADS, BLOCK : BLOCK + BUCKETS]


SMALL = 32
TAIL = [0, 1, 1, 3, 0, 2, 4, 3, 2, 1, 4, 3, 0, 4, 2, 3, 4]
COST = {
    "enc_attention": 5.0, "dec_attention": 2.9, "dec_mid": 1.9, "enc_ff": 4.5, "decoder": 9.1, "cross_back": 5.0, "enc_ff_back": 3.2,
    "enc_ff_weights": 1.9, "enc_attention_back": 6.2, "dec_back": 4.6, "enc_finish": 3.5,
}
SCALE = 1.0
SUM_COST = 0.5


def on_device(
    rows_count,
    enc_input,
    dec_input,
    enc_segments,
    dec_segments,
    cotangent,
    enc_norm_attn,
    enc_query,
    enc_key,
    enc_value,
    enc_mix,
    enc_table,
    enc_norm_ff,
    enc_up,
    enc_down,
    enc_norm_final,
    dec_norm_self,
    dec_query,
    dec_key,
    dec_value,
    dec_mix,
    dec_table,
    dec_norm_cross,
    cross_query,
    cross_key,
    cross_value,
    cross_mix,
    dec_norm_ff,
    dec_up,
    dec_down,
):
    chip, core = lax.axis_index("rows"), lax.axis_index("seq")
    x_own, d_own, c_own = enc_input[0], dec_input[0], cotangent[0]
    half, d_half = x_own.shape[0], d_own.shape[0]
    enc, dec = 2 * half, 2 * d_half
    width, hidden = D // 2, FF // 2

    def swap(values):
        return lax.ppermute(values, "seq", [(0, 1), (1, 0)])

    def row(gain):
        return gain.reshape(1, -1)

    def v(*arrays):
        return [(array, "vmem") for array in arrays]

    def h(*arrays):
        return [(array, "all") for array in arrays]

    def cols(*arrays):
        return [(array, "cols") for array in arrays]

    square = (D, D)
    ordered = in_order(rows_count)

    def payload(total, extra=0):
        if ordered:
            return [((total // 2 + extra, LANES), LOW)] * 2, [((rows_count, total // rows_count, LANES), LOW)]
        return [((total + extra, LANES), LOW), ((16, LANES), LOW)], [((1, total, LANES), LOW)]

    squares, ffs, last = payload(4 * D), payload(4 * D + FF), payload(4 * D, SMALL)

    lead = D // rows_count

    def arranged(pay, leads, extra, orders):
        if ordered:
            return pay
        places = jnp.array([[chunk_of(q, order) for q in range(rows_count)] for order in orders], jnp.int32)
        parts, start = [], 0
        for count in leads:
            parts.append(pay[0][start : start + count].reshape(rows_count, -1, LANES))
            start += count
        chunks = jnp.take(jnp.concatenate(parts, 1), places[core] ^ chip, axis=0)
        return [
            jnp.concatenate([part.reshape(-1, LANES), pay[0][start : start + extra]], 0)
            for part in (chunks[: rows_count // 2], chunks[rows_count // 2 :])
        ]

    class Sum:
        def __init__(self, pay, leads, outs, name, extra=0):
            self.orders = bit_orders(rows_count, name)
            self.kept, self.sent = arranged(pay, leads, extra, self.orders)
            self.segments = [self.kept.shape[0] - extra]
            self.outs, self.extra, self.name, self.stage, self.found = outs, extra, name, 0, None
            self.send()

        def send(self):
            pairs = [
                (at * 2 + c, (at ^ (1 << self.orders[c][self.stage])) * 2 + c)
                for at in range(rows_count)
                for c in range(2)
            ]
            self.came = lax.ppermute(self.sent, ("rows", "seq"), pairs)
            self.stage += 1

        def add(self, token, *others, after=()):
            if self.found is not None:
                return token
            every = (self, *others)
            for other in others:
                assert other.stage == self.stage and other.orders[0][self.stage :] == self.orders[0][self.stage :]
                assert not self.extra
            name = f"sum_{self.name}_{self.stage}"
            operands = v(*[array for each in every for array in (each.kept, each.came)])
            if self.stage == len(self.orders[0]):
                token, self.found = call(
                    token, last_kernel, operands,
                    [out for each in every for out in each.outs], limit=8, name=name, after=after,
                )
                return token
            segments = [each.segments for each in every]
            self.extra = every[-1].extra
            self.segments = [size // 2 for sizes in segments for size in sizes]
            self.outs = [out for each in every for out in each.outs]
            shape = (sum(self.segments) + self.extra, LANES)
            token, (self.kept, self.sent) = call(
                token, functools.partial(sum_kernel, segments=segments, extra=self.extra), operands,
                [(shape, LOW)] * 2, limit=8, name=name, after=after,
            )
            self.send()
            return token

    ff_outs = [((lead, hidden), FULL), ((FF // rows_count, LANES), FULL)]
    square_outs = [((lead, LANES), FULL)] * 4
    small_outs = [((1, lead), FULL)] * 6 + [((HEADS, BUCKETS), FULL)] * 2

    x_other, d_other, c_other = swap(x_own), swap(d_own), swap(c_own)

    token, (mixed, probs, queries, keys, values, x_normed) = call(
        None,
        enc_attention_kernel,
        h(x_own) + v(x_other) + h(row(enc_norm_attn), enc_segments, enc_table.T) + cols(enc_query, enc_key, enc_value),
        [
            ((width, enc), LOW), ((HEADS // 4, enc, 2 * enc), LOW),
            ((enc, width), LOW), ((enc, width), LOW), ((enc, width), LOW), ((enc, D), LOW),
        ],
        [((HEADS, 2 * enc), FULL)],
        name="enc_attention",
    )
    mixed_other = swap(mixed)
    token, (d_probs, d_queries, d_keys, d_values, d_normed, d_mixed, d_all) = call(
        token,
        dec_attention_kernel,
        h(d_own) + v(d_other)
        + h(row(dec_norm_self), dec_segments, dec_table.T) + v(dec_query, dec_key, dec_value),
        [((HEADS // 2, dec, 2 * dec), LOW)] + [((dec, D), LOW)] * 4 + [((D, dec), LOW), ((dec, D), FULL)],
        name="dec_attention", after=[c_other],
    )
    token, (mid, after_part, after_low, active, ff_in) = call(
        token,
        enc_ff_kernel,
        h(x_own) + v(x_other, mixed, mixed_other)
        + [(enc_mix, "rows"), (enc_mix, "rows_other"), (row(enc_norm_ff), "all")] + v(enc_up, enc_down),
        [((enc, D), FULL), ((enc, D), FULL), ((enc, D), LOW), ((2 * enc, hidden), LOW), ((enc, D), LOW)],
        name="enc_ff",
    )
    after_came = swap(after_low)
    token, (d_mid, cross_in, cross_queries) = call(
        token,
        dec_mid_kernel,
        v(d_all, d_mixed, dec_mix) + h(row(dec_norm_cross)) + v(cross_query),
        [((dec, D), FULL), ((dec, D), LOW), ((dec, D), LOW)],
        name="dec_mid",
    )
    token, (
        enc_result, after, state, c_keys, c_values, c_probs, c_mixed, dec_result, stream, g_dec_ff, *pay_first, active,
    ) = call(
        token,
        functools.partial(decoder_kernel, rows_count),
        v(after_part, after_came) + h(row(enc_norm_final), enc_segments, dec_segments) + v(cross_queries, d_mid)
        + h(row(dec_norm_ff), c_own) + v(c_other, cross_key, cross_value, cross_mix, dec_up, dec_down),
        [
            ((half, D), FULL), ((enc, D), FULL), ((enc, D), LOW), ((enc, D), LOW), ((enc, D), LOW),
            ((HEADS // 2, enc, 2 * dec), LOW), ((D, dec), LOW), ((d_half, D), FULL), ((dec, D), FULL), ((1, D), FULL),
        ] + ffs[0],
        ffs[1] + [((dec, D), FULL), ((dec, D), LOW), ((dec, D), FULL), ((dec, FF), LOW), ((dec, FF), LOW)],
        name="decoder", through=[active],
    )
    active_other = swap(active)
    first = Sum(pay_first, [D] * 4 + [FF], ff_outs, "dec_ff")
    token, (enc_stream, enc_low, g_final, stream, g_cross, *pay_cross) = call(
        token,
        functools.partial(cross_back_kernel, rows_count),
        v(stream, d_mid) + h(row(dec_norm_cross)) + v(cross_in, cross_queries, c_keys, c_values, c_probs, c_mixed, state, after,
          )
        + h(row(enc_norm_final)) + v(cross_mix, cross_key, cross_value, cross_query),
        [((enc, D), FULL), ((enc, D), LOW), ((1, D), FULL), ((dec, D), FULL), ((1, D), FULL)] + squares[0],
        squares[1] + [((dec, D), LOW), ((D, dec), LOW), ((dec, D), LOW), ((enc, D), LOW), ((enc, D), LOW)],
        name="cross_back",
    )
    second = Sum(pay_cross, [D] * 4, square_outs, "cross")
    token, (before_grad, part) = call(
        token,
        enc_ff_back_kernel,
        v(enc_low, active, active_other)
        + v(enc_down, enc_up),
        [((enc, hidden), LOW), ((enc, D), FULL)],
        name="enc_ff_back",
    )
    token, pay_enc_ff = call(
        token,
        functools.partial(enc_ff_weights_kernel, rows_count),
        v(ff_in, before_grad, active, active_other, enc_low),
        ffs[0],
        ffs[1] + [((FF, LANES), FULL)],
        name="enc_ff_weights",
    )
    third = Sum(pay_enc_ff, [D] * 4 + [FF], ff_outs, "enc_ff")
    token = first.add(token)
    token, (low, enc_stream, g_ff, query_grad, key_grad, value_grad, table_enc, normed_part, *normed_low) = call(
        token,
        enc_attention_back_kernel,
        v(part, mid) + h(row(enc_norm_ff)) + v(enc_stream) + [(enc_mix, "rows")]
        + v(queries, keys, values, probs) + cols(enc_query, enc_key, enc_value),
        [
            ((enc, D), LOW), ((enc, D), FULL), ((1, D), FULL), ((enc, width), LOW), ((enc, width), LOW),
            ((enc, width), LOW), ((HEADS, BUCKETS), FULL), ((enc, D), FULL), ((half, D), LOW),
            ((half + 16, D), LOW),
        ],
        [((BLOCK, 2 * enc), FULL), ((HEADS, 2 * enc), FULL), ((width, enc), LOW)],
        name="enc_attention_back",
    )
    normed_came = [swap(part) for part in normed_low]
    token, (dec_input_grad, g_self, table_dec, dec_squares, *pay_dec) = call(
        token,
        functools.partial(dec_back_kernel, rows_count),
        v(stream) + h(d_own) + v(d_other) + h(row(dec_norm_self))
        + v(d_normed, d_queries, d_keys, d_values, d_probs, d_mixed)
        + v(dec_mix, dec_query, dec_key, dec_value),
        [((d_half, D), FULL), ((1, D), FULL), ((HEADS, BUCKETS), FULL), ((1, D), FULL)] + squares[0],
        squares[1] + [((dec, D), LOW), ((D, dec), LOW)] + [((dec, D), LOW)] * 3 + [((HEADS, 2 * BLOCK), FULL), ((dec, D), FULL), ((dec, D), FULL)],
        name="dec_back",
    )
    fourth = Sum(pay_dec, [D] * 4, square_outs, "dec")
    token = third.add(token)
    token = second.add(token)
    token, (enc_input_grad, row_norm, *pay_enc) = call(
        token,
        functools.partial(enc_finish_kernel, rows_count),
        v(normed_part, *normed_came, enc_stream) + h(x_own) + v(x_other) + h(row(enc_norm_attn)) + v(x_normed, query_grad, key_grad,
          value_grad, mixed, mixed_other, low, table_enc, table_dec, dec_squares, g_ff, g_final, g_self, g_cross,
          g_dec_ff),
        [((half, D), FULL), ((1, 1), FULL)] + last[0],
        last[1] + [((enc, D), FULL), ((enc, D), FULL), ((D, LANES), FULL), ((SMALL, LANES), FULL)],
        name="enc_finish",
    )

    fifth = Sum(pay_enc, [D] * 4, square_outs + small_outs, "enc", SMALL)
    sums = [first, second, third, fourth, fifth]
    for which in TAIL:
        token = sums[which].add(token)
    while any(each.found is None for each in sums):
        for each in sums:
            token = each.add(token)
    dec_u, dec_d = first.found
    enc_u, enc_d = third.found
    cross_q, cross_k, cross_v, cross_m = second.found
    dec_q, dec_k, dec_v, dec_m = fourth.found
    enc_q, enc_k, enc_v, enc_m, *small = fifth.found
    gains = [gain[0] for gain in small[:6]]
    tables = [small[6].T, small[7].T]
    return (
        enc_result[None], dec_result[None], enc_input_grad[None], dec_input_grad[None], row_norm[0],
        gains[0], enc_q, enc_k, enc_v, enc_m, tables[0], gains[1], enc_u, enc_d, gains[2],
        gains[3], dec_q, dec_k, dec_v, dec_m, tables[1], gains[4], cross_q, cross_k, cross_v, cross_m,
        gains[5], dec_u, dec_d,
    )


def solution(mesh):
    split, line, copied = P("rows", "seq", None), P("rows", None), P()
    in_specs = (split, split, line, line, split) + (copied,) * 24
    block, vector = P("rows", "seq"), P("rows")
    out_specs = (
        (split,) * 4 + (vector,)
        + (vector,) + (block,) * 4 + (copied, vector, block, block, vector)
        + (vector,) + (block,) * 4 + (copied, vector) + (block,) * 4 + (vector, block, block)
    )
    return jax.shard_map(
        functools.partial(on_device, mesh.shape["rows"]),
        mesh=mesh, in_specs=in_specs, out_specs=out_specs, check_vma=False,
    )
```

```python
import functools
import math

import jax
import jax.numpy as jnp
from jax import lax
from jax.experimental import pallas as pl
from jax.experimental.pallas import tpu as pltpu
from jax.sharding import PartitionSpec as P

D = 512
HEADS = 8
HEAD = 64
FF = 2048
BUCKETS = 32
MAX_DIST = 128
NDOC = 4
EPSILON = 1e-06
NEGATIVE = -1e30
BLOCK = 128
LANES = 256

LOW = jnp.bfloat16
FULL = jnp.float32
HIGH = lax.Precision.HIGHEST


def cut_points(exact_span, bucket_half, reach):
    points = []
    for target in range(exact_span + 1, bucket_half):
        reach_at = exact_span
        while (
            exact_span
            + int(
                math.log(reach_at / exact_span)
                / math.log(reach / exact_span)
                * (bucket_half - exact_span)
            )
            < target
        ):
            reach_at += 1
        points.append(reach_at)
    return points


def bucket_index(offset, both_ways):
    if both_ways:
        bucket_half = BUCKETS // 2
        base_index = jnp.where(offset > 0, bucket_half, 0).astype(jnp.int32)
        distance = jnp.abs(offset)
    else:
        bucket_half = BUCKETS
        base_index = jnp.zeros_like(offset)
        distance = jnp.maximum(-offset, 0)
    exact_span = bucket_half // 2
    result = base_index + jnp.minimum(distance, exact_span)
    for border in cut_points(exact_span, bucket_half, MAX_DIST):
        result = result + (distance >= border).astype(jnp.int32)
    return result


def dot(left, right, dims=((1,), (0,)), precision=None):
    return lax.dot_general(
        left, right, (dims, ((), ())), preferred_element_type=FULL, precision=precision
    )


def dot_cols(left, right):
    return dot(left, right, ((1,), (1,)))


def dot_rows(left, right):
    return dot(left, right, ((0,), (0,)))


def scale_of(values):
    return lax.rsqrt(jnp.mean(values * values, axis=-1, keepdims=True) + EPSILON)


def normed(values, gain):
    return (values * scale_of(values) * gain).astype(LOW)


def norm_back(values, gain, grad):
    scale = scale_of(values)
    unit = values * scale
    gain_grad = jnp.sum(grad * unit, axis=0, keepdims=True)
    grad = grad * gain
    return scale * (grad - unit * jnp.mean(grad * unit, axis=-1, keepdims=True)), gain_grad


def gelu_pair(values):
    root = math.sqrt(2.0 / math.pi)
    square = values * values
    tanh = jnp.tanh(root * values * (1.0 + 0.044715 * square))
    half = 0.5 + 0.5 * tanh
    slope = half + 0.5 * values * (1.0 - tanh * tanh) * (root + (3 * 0.044715 * root) * square)
    return values * half, slope


def iota(shape, axis):
    return lax.broadcasted_iota(jnp.int32, shape, axis)


def offsets(span, period, both_ways):
    place = iota((1, period), 1)
    offset = span - jnp.where(place < period - BLOCK, place, place - period)
    return (bucket_index(offset, both_ways) == iota((BUCKETS, period), 0)).astype(FULL)


def sheared(row, period):
    return pltpu.roll(
        jnp.broadcast_to(row, (BLOCK, period)), 0, 1, stride=1, stride_axis=0
    )


def unsheared(sums, period):
    rows = sums.shape[0]
    while rows > 8:
        rows //= 2
        sums = sums[:rows] + pltpu.roll(sums[rows:], period - rows, 1)
    total = sums[:1]
    for row in range(1, 8):
        total = total + pltpu.roll(sums[row : row + 1], period - row, 1)
    return total


def doc_columns(ids):
    wide = jnp.broadcast_to(ids.astype(FULL), (BLOCK, ids.shape[1]))
    return jnp.transpose(wide)


def doc_marks(ids):
    columns = doc_columns(ids)
    lane = iota(columns.shape, 1)
    same = columns == lane.astype(FULL)
    query_marks = jnp.where((lane < NDOC) & jnp.logical_not(same), NEGATIVE, 0.0).astype(LOW)
    return query_marks, same.astype(FULL).astype(LOW)


def apart(values):
    lane = iota(values.shape, 1)
    zeros = jnp.zeros_like(values)
    return jnp.concatenate([jnp.where(lane < HEAD, values, zeros), jnp.where(lane >= HEAD, values, zeros)], 0)


def pair_scores(key_pair, query_pair, key_marks, query_marks):
    left = jnp.concatenate([key_pair, key_marks], 1)
    right = jnp.concatenate([apart(query_pair), jnp.concatenate([query_marks, query_marks], 0)], 1)
    return dot_cols(left, right)


def put_pair(target, p, both):
    length = both.shape[1] // 2
    target[one(2 * p), :] = both[:HEAD, :length].astype(LOW)
    target[one(2 * p + 1), :] = both[HEAD:, length:].astype(LOW)


def softmax(scores):
    weights = jnp.exp(scores - jnp.max(scores, axis=0, keepdims=True))
    return (weights * (1.0 / jnp.sum(weights, axis=0, keepdims=True))).astype(LOW)


def score_back(probs, probs_grad):
    probs = probs.astype(FULL)
    inner = jnp.sum(probs * probs_grad, axis=0, keepdims=True)
    return (probs * (probs_grad - inner)).astype(LOW)


def one(head):
    return slice(head * HEAD, (head + 1) * HEAD)


def pair(index):
    return slice(index * 2 * HEAD, (index + 1) * 2 * HEAD)


def aligned(index, size):
    return pl.ds(pl.multiple_of(index * size, size), size)


class Lazy:
    def __init__(self, ref, copy):
        self.ref, self.copy = ref, copy

    @property
    def shape(self):
        return self.ref.shape

    def __getitem__(self, index):
        if self.copy is not None:
            self.copy.wait()
            self.copy = None
        return self.ref[index]


def cut(source, mode):
    if mode == "all":
        return source
    core = lax.axis_index("seq")
    rows, cols = source.shape
    at = 1 - core if mode.endswith("other") else core
    if mode.startswith("cols"):
        return source.at[:, aligned(at, cols // 2)]
    return source.at[aligned(at, rows // 2), :]


def cut_shape(shape, mode):
    if mode == "all":
        return shape
    return (shape[0], shape[1] // 2) if mode.startswith("cols") else (shape[0] // 2, shape[1])


ROUTES = {"dec_ff": "xywz", "cross": "zxyw", "enc_ff": "xzyw", "dec": "xzyw", "enc": "xyzw"}


def bit_orders(rows_count, payload):
    bits = list(range(rows_count.bit_length() - 1))
    if len(bits) < 4:
        return (bits, bits)
    first = ["xyzw".index(axis) for axis in ROUTES[payload]] + bits[4:]
    return (first, [{0: 1, 1: 0}.get(bit, bit) for bit in first])


def place_of(chunk, order):
    bits = len(order)
    return sum(((chunk >> order[s]) & 1) << (bits - 1 - s) for s in range(bits))


def chunk_of(place, order):
    bits = len(order)
    return sum(((place >> (bits - 1 - s)) & 1) << order[s] for s in range(bits))


def in_order(rows_count):
    return (D // rows_count) % 16 == 0


class Shares:
    def __init__(self, rows_count, payload, route):
        self.rows_count, self.payload, self.row = rows_count, payload, 0
        core, chip = lax.axis_index("seq"), lax.axis_index("rows")
        orders = bit_orders(rows_count, route)
        own = [place_of(chip, order) for order in orders]
        self.places = [
            jnp.where(core == 0, place_of(chunk, orders[0]) ^ own[0], place_of(chunk, orders[1]) ^ own[1])
            for chunk in range(rows_count)
        ] if in_order(rows_count) else [0]

    def put(self, grad):
        chunks = len(self.places)
        lead = grad.shape[0] // chunks
        for chunk in range(chunks):
            self.payload[self.places[chunk], self.row : self.row + lead, :] = grad[
                chunk * lead : (chunk + 1) * lead
            ].astype(LOW)
        self.row += lead

    def split(self, kept, sent):
        if not in_order(self.rows_count):
            kept[: self.row] = self.payload[0]
            return
        half = self.rows_count // 2
        shape = (half * self.row, LANES)
        sent[: half * self.row] = self.payload[half:].reshape(shape)
        kept[: half * self.row] = self.payload[:half].reshape(shape)


VMEM = pl.BlockSpec(memory_space=pltpu.VMEM)
HBM = pl.BlockSpec(memory_space=pltpu.HBM)
ANY = pl.BlockSpec(memory_space=pl.ANY)
MIB = 1024 * 1024


def call(token, kernel, ins, outs, scratch=(), limit=24, name=None, after=(), through=()):
    n_ins, n_outs = len(ins), len(outs)
    ins = list(ins) + [(token, "vmem")] * (token is not None) + [(array, "any") for array in (*after, *through)]
    outs = list(outs) + [(array.shape, array.dtype) for array in through] + [((8, BLOCK), FULL)]
    specs = [{"vmem": VMEM, "any": ANY}.get(how, HBM) for _, how in ins]
    arrays = [
        array if how in ("vmem", "any") else pltpu.with_memory_space_constraint(array, pltpu.HBM) for array, how in ins
    ]
    shapes = [jax.ShapeDtypeStruct(shape, kind) for shape, kind in outs]
    lazy = [i for i, (_, how) in enumerate(ins) if how not in ("vmem", "any")]
    scratch = [pltpu.VMEM(shape, kind) for shape, kind in scratch]
    n_own = len(scratch)
    scratch += [pltpu.VMEM(cut_shape(arrays[i].shape, ins[i][1]), arrays[i].dtype) for i in lazy]
    if lazy:
        scratch.append(pltpu.SemaphoreType.DMA((len(lazy),)))

    def body(*refs):
        operands = list(refs[: len(ins)])
        rest = refs[len(ins) :]
        results, own = rest[: len(outs)], rest[len(outs) : len(outs) + n_own]
        landing = rest[len(outs) + n_own :]
        for place, i in enumerate(lazy):
            copy = pltpu.make_async_copy(cut(operands[i], ins[i][1]), landing[place], landing[-1].at[place])
            copy.start()
            operands[i] = Lazy(landing[place], copy)
        results[-1][...] = jnp.zeros((8, BLOCK), FULL)
        kernel(*operands[:n_ins], *results[: n_outs], *own)
        for i in lazy:
            if operands[i].copy is not None:
                operands[i].copy.wait()

    found = pl.pallas_call(
        body,
        out_shape=shapes,
        in_specs=specs,
        out_specs=[VMEM] * n_outs + [ANY] * len(through) + [VMEM],
        input_output_aliases={len(ins) - len(through) + i: n_outs + i for i in range(len(through))},
        scratch_shapes=scratch,
        compiler_params=pltpu.CompilerParams(vmem_limit_bytes=limit * MIB),
        cost_estimate=pl.CostEstimate(
            flops=1000 + int(SCALE * COST.get(name, SUM_COST) * 1.15e9), bytes_accessed=1000, transcendentals=0
        ),
        name=name,
    )(*arrays)
    return found[-1], found[:-1]


def enc_attention_kernel(
    x_own, x_other, gain, ids, table, w_query, w_key, w_value,
    mixed, probs, queries, keys, values, x_normed,
    biases,
):
    core = lax.axis_index("seq")
    width = w_query.shape[1]
    half = x_own.shape[0]
    length = 2 * half
    for part, at in ((x_own, core), (x_other, 1 - core)):
        x_normed[aligned(at, half), :] = normed(part[...].astype(FULL), gain[...])
    span, period = length - BLOCK, 2 * length
    biases[...] = dot(table[...], offsets(span, period, True), precision=HIGH)
    query_marks, key_marks = doc_marks(ids[...])
    for weight, target in zip((w_query, w_key, w_value), (queries, keys, values)):
        target[...] = dot(x_normed[...], weight[...]).astype(LOW)
    values_t = jnp.transpose(values[...])
    for p in range(HEADS // 4):
        shift = []
        for head in (2 * p, 2 * p + 1):
            bias = sheared(biases[pl.ds(core * (HEADS // 2) + head, 1), :], period)
            shift.append(jnp.concatenate([bias[:, span - key : span - key + length] for key in range(0, length, BLOCK)], 0))
        scores = pair_scores(keys[:, pair(p)], queries[:, pair(p)], key_marks, query_marks)
        weights = softmax(scores + jnp.concatenate(shift, 1))
        probs[p] = weights
        put_pair(mixed, p, dot(values_t[pair(p)], weights))


def dec_attention_kernel(
    x_own, x_other, gain, ids, table, w_query, w_key, w_value,
    probs, queries, keys, values, x_normed, mixed, x_all,
):
    core = lax.axis_index("seq")
    half = x_own.shape[0]
    length = 2 * half
    for part, at in ((x_own, core), (x_other, 1 - core)):
        x_all[aligned(at, half), :] = part[...].astype(FULL)
    x_normed[...] = normed(x_all[...], gain[...])
    period = 2 * BLOCK
    biases = dot(table[...], offsets(0, period, False), precision=HIGH)
    query_marks, key_marks = doc_marks(ids[...])
    later = iota((BLOCK, BLOCK), 0) > iota((BLOCK, BLOCK), 1)
    for weight, target in zip((w_query, w_key, w_value), (queries, keys, values)):
        target[...] = dot(x_normed[...], weight[...]).astype(LOW)
    values_t = jnp.transpose(values[...])
    for p in range(HEADS // 2):
        bias = [
            jnp.where(later, NEGATIVE, sheared(biases[head : head + 1], period)[:, :length]) for head in (2 * p, 2 * p + 1)
        ]
        scores = pair_scores(keys[:, pair(p)], queries[:, pair(p)], key_marks, query_marks)
        weights = softmax(scores + jnp.concatenate(bias, 1))
        probs[p] = weights
        put_pair(mixed, p, dot(values_t[pair(p)], weights))


def dec_mid_kernel(x_all, mixed, w_mix, gain_cross, w_cross, mid, cross_in, cross_queries):
    mid[...] = x_all[...] + dot_rows(mixed[...], w_mix[...])
    cross_in[...] = normed(mid[...], gain_cross[...])
    cross_queries[...] = dot(cross_in[...], w_cross[...]).astype(LOW)


def enc_ff_kernel(
    x_own, x_other, mixed_own, mixed_other, mix_own, mix_other, gain, w_up, w_down,
    mid, after, after_low, active, ff_in,
):
    core = lax.axis_index("seq")
    hidden = w_up.shape[1] // 2
    half = x_own.shape[0]
    length = 2 * half
    for part, at in ((x_own, core), (x_other, 1 - core)):
        mid[aligned(at, half), :] = part[...].astype(FULL)
    mid[...] += dot_rows(mixed_own[...], mix_own[...]) + dot_rows(mixed_other[...], mix_other[...])
    ff_in[...] = normed(mid[...], gain[...])
    total = None
    for start in range(0, hidden, 512):
        cols = slice(start, start + 512)
        place = pl.ds(pl.multiple_of(core * hidden + start, 256), 512)
        act, grow = gelu_pair(dot(ff_in[...], w_up[:, place]))
        act = act.astype(LOW)
        active[:length, cols] = act
        active[length:, cols] = grow.astype(LOW)
        term = dot(act, w_down[place, :])
        total = term if total is None else total + term
    after[...] = mid[...] + total
    after_low[...] = total.astype(LOW)


def decoder_kernel(
    rows_count,
    after_part, came, gain_final, enc_ids, dec_ids, cross_queries, dec_mid, gain_ff, cot_own, cot_other,
    w_key, w_value, w_mix, w_up, w_down,
    enc_result, after, state, keys, values, probs, mixed, dec_result, stream, gain_grad, kept, sent,
    payload, cross, cot, out, before_grad, active,
):
    core = lax.axis_index("seq")
    length = dec_mid.shape[0]
    half, enc_half = length // 2, after.shape[0] // 2
    for part, at in ((cot_own, core), (cot_other, 1 - core)):
        cot[aligned(at, half), :] = part[...]
    after[...] = after_part[...] + came[...].astype(FULL)
    enc_result[...] = after[aligned(core, enc_half), :]
    state[...] = normed(after[...], gain_final[...])
    _, key_marks = doc_marks(enc_ids[...])
    query_marks, _ = doc_marks(dec_ids[...])
    keys[...] = dot(state[...], w_key[...]).astype(LOW)
    values[...] = dot(state[...], w_value[...]).astype(LOW)
    values_t = jnp.transpose(values[...])
    for p in range(HEADS // 2):
        weights = softmax(pair_scores(keys[:, pair(p)], cross_queries[:, pair(p)], key_marks, query_marks))
        probs[p] = weights
        put_pair(mixed, p, dot(values_t[pair(p)], weights))
    cross[...] = dec_mid[...] + dot_rows(mixed[...], w_mix[...])
    ff_in = normed(cross[...], gain_ff[...])
    total = cross[...]
    normed_grad = jnp.zeros_like(total)
    for start in range(0, FF, 2048):
        cols = slice(start, start + 2048)
        act, grow = gelu_pair(dot(ff_in, w_up[:, cols]))
        act = act.astype(LOW)
        active[:, cols] = act
        total = total + dot(act, w_down[cols, :])
        grad = (grow * dot_cols(cot[...], w_down[cols, :])).astype(LOW)
        before_grad[:, cols] = grad
        normed_grad = normed_grad + dot_cols(grad, w_up[:, cols])
    out[...] = total
    dec_result[...] = out[aligned(core, half), :]
    shares = Shares(rows_count, payload, "dec_ff")
    for start in range(0, FF // 2, LANES):
        shares.put(dot_rows(ff_in, before_grad[:, pl.ds(pl.multiple_of(core * (FF // 2) + start, LANES), LANES)]))
    shares.put(dot_rows(active[...], cot[:, aligned(core, LANES)]))
    shares.split(kept, sent)
    back, gain_grad[...] = norm_back(cross[...], gain_ff[...], normed_grad)
    stream[...] = cot[...].astype(FULL) + back


def cross_back_kernel(
    rows_count,
    stream, dec_mid, gain_cross, cross_in, queries, keys, values, probs, mixed, state, after, gain_final,
    w_mix, w_key, w_value, w_query,
    enc_stream, enc_low, gain_final_grad, stream_out, gain_grad, kept, sent,
    payload, low, query_grad_t, query_grad, key_grad, value_grad,
):
    core = lax.axis_index("seq")
    shares = Shares(rows_count, payload, "cross")
    low[...] = stream[...].astype(LOW)
    mixed_grad = dot_cols(low[...], w_mix[...]).astype(LOW)
    keys_t = jnp.transpose(keys[...])
    for p in range(HEADS // 2):
        weights, grads = probs[p], apart(mixed_grad[:, pair(p)])
        score_grad = score_back(weights, dot_cols(values[:, pair(p)], grads))
        put_pair(query_grad_t, p, dot(keys_t[pair(p)], score_grad))
        key_grad[:, pair(p)] = dot(score_grad, apart(queries[:, pair(p)])).astype(LOW)
        value_grad[:, pair(p)] = dot(weights, grads).astype(LOW)
    query_grad[...] = jnp.transpose(query_grad_t[...])
    state_grad = dot_cols(key_grad[...], w_key[...]) + dot_cols(value_grad[...], w_value[...])
    back, gain_final_grad[...] = norm_back(after[...], gain_final[...], state_grad)
    enc_stream[...] = back
    enc_low[...] = back.astype(LOW)
    back, gain_grad[...] = norm_back(dec_mid[...], gain_cross[...], dot_cols(query_grad[...], w_query[...]))
    stream_out[...] = stream[...] + back
    own = aligned(core, LANES)
    shares.put(dot_rows(cross_in[...], query_grad[:, own]))
    shares.put(dot_rows(state[...], key_grad[:, own]))
    shares.put(dot_rows(state[...], value_grad[:, own]))
    shares.put(dot(mixed[...], low[:, own]))
    shares.split(kept, sent)


def dec_back_kernel(
    rows_count,
    stream, x_own, x_other, gain, x_normed, queries, keys, values, probs, mixed,
    w_mix, w_query, w_key, w_value,
    input_grad, gain_grad, table_grad, squares, kept, sent,
    payload, low, query_grad_t, query_grad, key_grad, value_grad, sums, x_all, total,
):
    core = lax.axis_index("seq")
    shares = Shares(rows_count, payload, "dec")
    half = x_own.shape[0]
    length = 2 * half
    for part, at in ((x_own, core), (x_other, 1 - core)):
        x_all[aligned(at, half), :] = part[...].astype(FULL)
    low[...] = stream[...].astype(LOW)
    mixed_grad = dot_cols(low[...], w_mix[...]).astype(LOW)
    period = 2 * BLOCK
    keys_t = jnp.transpose(keys[...])
    for p in range(HEADS // 2):
        weights, grads = probs[p], apart(mixed_grad[:, pair(p)])
        score_grad = score_back(weights, dot_cols(values[:, pair(p)], grads))
        put_pair(query_grad_t, p, dot(keys_t[pair(p)], score_grad))
        key_grad[:, pair(p)] = dot(score_grad, apart(queries[:, pair(p)])).astype(LOW)
        value_grad[:, pair(p)] = dot(weights, grads).astype(LOW)
        for odd in range(2):
            head, grad = 2 * p + odd, score_grad[:, odd * length : (odd + 1) * length].astype(FULL)
            wide = jnp.concatenate([grad, jnp.zeros((BLOCK, BLOCK), FULL)], axis=1)
            sums[head : head + 1, :] = unsheared(wide, period)
    query_grad[...] = jnp.transpose(query_grad_t[...])
    table_grad[...] = dot(sums[...], offsets(0, period, False), ((1,), (1,)), HIGH)
    normed_grad = (
        dot_cols(query_grad[...], w_query[...])
        + dot_cols(key_grad[...], w_key[...])
        + dot_cols(value_grad[...], w_value[...])
    )
    back, gain_grad[...] = norm_back(x_all[...], gain[...], normed_grad)
    total[...] = stream[...] + back
    input_grad[...] = total[aligned(core, half), :]
    squares[...] = jnp.sum(total[...] * total[...], axis=0, keepdims=True)
    own = aligned(core, LANES)
    for grad in (query_grad, key_grad, value_grad):
        shares.put(dot_rows(x_normed[...], grad[:, own]))
    shares.put(dot(mixed[...], low[:, own]))
    shares.split(kept, sent)


def enc_ff_back_kernel(
    low, active_own, active_other, w_down, w_up,
    before_grad, part,
):
    core = lax.axis_index("seq")
    hidden = w_up.shape[1] // 2
    length = low.shape[0]
    total = None
    for active, at, own in ((active_own, core, 1), (active_other, 1 - core, 0)):
        for start in range(0, hidden, 512):
            cols = slice(start, start + 512)
            place = pl.ds(pl.multiple_of(at * hidden + start, 256), 512)
            grad = (active[length:, cols].astype(FULL) * dot_cols(low[...], w_down[place, :])).astype(LOW)
            if own:
                before_grad[:, cols] = grad
            term = dot_cols(grad, w_up[:, place])
            total = term if total is None else total + term
    part[...] = total


def enc_ff_weights_kernel(rows_count, ff_in, before_grad, active_own, active_other, low, kept, sent, payload, both):
    core = lax.axis_index("seq")
    shares = Shares(rows_count, payload, "enc_ff")
    for start in range(0, before_grad.shape[1], LANES):
        shares.put(dot_rows(ff_in[...], before_grad[:, start : start + LANES]))
    hidden, length = active_own.shape[1], low.shape[0]
    own = low[:, aligned(core, LANES)]
    both[aligned(core, hidden), :] = dot_rows(active_own[:length], own)
    both[aligned(1 - core, hidden), :] = dot_rows(active_other[:length], own)
    shares.put(both[...])
    shares.split(kept, sent)


def enc_attention_back_kernel(
    part, mid, gain, stream, w_mix, queries, keys, values, probs, w_query, w_key, w_value,
    low, stream_out, gain_grad, query_grad, key_grad, value_grad, table_grad, normed_part, normed_first, normed_last,
    diagonals, sums, query_grad_t,
):
    core = lax.axis_index("seq")
    width = w_query.shape[1]
    length = mid.shape[0]
    span, period = length - BLOCK, 2 * length
    back, gain_grad[...] = norm_back(mid[...], gain[...], part[...])
    stream_out[...] = stream[...] + back
    low[...] = stream_out[...].astype(LOW)
    mixed_grad = dot_cols(low[...], w_mix[...]).astype(LOW)
    sums[...] = jnp.zeros_like(sums)
    keys_t = jnp.transpose(keys[...])
    for p in range(HEADS // 4):
        weights, grads = probs[p], apart(mixed_grad[:, pair(p)])
        score_grad = score_back(weights, dot_cols(values[:, pair(p)], grads))
        put_pair(query_grad_t, p, dot(keys_t[pair(p)], score_grad))
        key_grad[:, pair(p)] = dot(score_grad, apart(queries[:, pair(p)])).astype(LOW)
        value_grad[:, pair(p)] = dot(weights, grads).astype(LOW)
        for odd in range(2):
            diagonals[...] = jnp.zeros_like(diagonals)
            for key in range(0, length, BLOCK):
                grad = score_grad[key : key + BLOCK, odd * length : (odd + 1) * length]
                diagonals[:, span - key : span - key + length] += grad.astype(FULL)
            sums[pl.ds(core * (HEADS // 2) + 2 * p + odd, 1), :] = unsheared(diagonals[...], period)
    query_grad[...] = jnp.transpose(query_grad_t[...])
    table_grad[...] = dot(sums[...], offsets(span, period, True), ((1,), (1,)), HIGH)
    normed_part[...] = (
        dot_cols(query_grad[...], w_query[...])
        + dot_cols(key_grad[...], w_key[...])
        + dot_cols(value_grad[...], w_value[...])
    )
    half = normed_first.shape[0]
    normed_first[...] = normed_part[:half].astype(LOW)
    normed_last[:half, :] = normed_part[half:].astype(LOW)
    normed_last[half:, :] = jnp.zeros((normed_last.shape[0] - half, D), LOW)
    normed_last[half : half + HEADS, :BUCKETS] = table_grad[...].astype(LOW)


def enc_finish_kernel(
    rows_count,
    normed_part, came_first, came_last, stream, x_own, x_other, gain, x_normed, query_grad, key_grad, value_grad,
    mixed_own, mixed_other, low, table_enc, table_dec, dec_squares,
    g_ff, g_final, g_self, g_cross, g_dec_ff,
    input_grad, row_norm, kept, sent,
    payload, x_all, total, both, small,
):
    core = lax.axis_index("seq")
    shares = Shares(rows_count, payload, "enc")
    half = x_own.shape[0]
    for part, at in ((x_own, core), (x_other, 1 - core)):
        x_all[aligned(at, half), :] = part[...].astype(FULL)
    for grad in (query_grad, key_grad, value_grad):
        shares.put(dot_rows(x_normed[...], grad[...]))
    width = mixed_own.shape[0]
    own = low[:, aligned(core, LANES)]
    both[aligned(core, width), :] = dot(mixed_own[...], own)
    both[aligned(1 - core, width), :] = dot(mixed_other[...], own)
    shares.put(both[...])
    normed_grad = normed_part[...] + jnp.concatenate([came_first[...], came_last[:half]], 0).astype(FULL)
    back, gain_grad = norm_back(x_all[...], gain[...], normed_grad)
    total[...] = stream[...] + back
    input_grad[...] = total[aligned(core, half), :]
    squares = jnp.sum(total[...] * total[...], axis=0, keepdims=True) + dec_squares[...]
    row_norm[...] = jnp.sqrt(jnp.sum(squares, axis=1, keepdims=True))
    small[...] = jnp.zeros_like(small)
    small[:HEADS, :BUCKETS] = table_enc[...] + came_last[half : half + HEADS, :BUCKETS].astype(FULL)
    small[:HEADS, BLOCK : BLOCK + BUCKETS] = table_dec[...]
    for row, grad in enumerate(
        (gain_grad, g_ff[...], g_final[...], g_self[...], g_cross[...], g_dec_ff[...])
    ):
        for part in range(2):
            small[HEADS + 2 * row + part : HEADS + 2 * row + part + 1, :] = grad[:, part * LANES : (part + 1) * LANES]
    shares.split(kept, sent)
    kept[kept.shape[0] - SMALL :, :] = small[...].astype(LOW)
    if in_order(rows_count):
        sent[sent.shape[0] - SMALL :, :] = small[...].astype(LOW)


def sum_kernel(*refs, segments, extra):
    new_kept, new_sent = refs[-2:]
    row = 0
    for index, sizes in enumerate(segments):
        kept, came = refs[2 * index : 2 * index + 2]
        at = 0
        for size in sizes:
            half = size // 2
            new_sent[row : row + half] = kept[at + half : at + size] + came[at + half : at + size]
            new_kept[row : row + half] = kept[at : at + half] + came[at : at + half]
            row, at = row + half, at + size
    if extra:
        both = kept[at:] + came[at:]
        new_kept[row:] = both
        new_sent[row:] = both


def last_sum(kept, came, rows):
    return kept[rows].astype(FULL) + came[rows].astype(FULL)


def last_kernel(kept, came, *outs):
    row = 0
    for out in outs:
        lead = out.shape[0]
        if out.shape[1] < LANES:
            break
        for start in range(0, out.shape[1], LANES):
            out[:, start : start + LANES] = last_sum(kept, came, slice(row, row + lead))
            row += lead
    else:
        return
    small = last_sum(kept, came, slice(row, kept.shape[0]))
    gains = jnp.concatenate(
        [
            jnp.concatenate([small[HEADS + 2 * i + part : HEADS + 2 * i + part + 1] for i in range(6)] + [small[:2]], 0)
            for part in range(2)
        ],
        1,
    )
    lead = outs[-8].shape[1]
    start = lax.axis_index("rows") * lead
    gains = pltpu.roll(gains, jnp.where(start == 0, 0, D - start), 1)
    for i in range(6):
        outs[i - 8][...] = gains[i : i + 1, :lead]
    outs[-2][...] = small[:HEADS, :BUCKETS]
    outs[-1][...] = small[:HEADS, BLOCK : BLOCK + BUCKETS]


SMALL = 32
TAIL = [0, 1, 1, 3, 0, 2, 4, 3, 2, 1, 4, 3, 0, 4, 2, 4, 3]
COST = {
    "enc_attention": 5.0, "dec_attention": 2.9, "dec_mid": 1.9, "enc_ff": 4.5, "decoder": 9.1, "cross_back": 5.0, "enc_ff_back": 3.2,
    "enc_ff_weights": 1.9, "enc_attention_back": 6.2, "dec_back": 4.6, "enc_finish": 3.5,
}
SCALE = 1.0
SUM_COST = 0.5


def on_device(
    rows_count,
    enc_input,
    dec_input,
    enc_segments,
    dec_segments,
    cotangent,
    enc_norm_attn,
    enc_query,
    enc_key,
    enc_value,
    enc_mix,
    enc_table,
    enc_norm_ff,
    enc_up,
    enc_down,
    enc_norm_final,
    dec_norm_self,
    dec_query,
    dec_key,
    dec_value,
    dec_mix,
    dec_table,
    dec_norm_cross,
    cross_query,
    cross_key,
    cross_value,
    cross_mix,
    dec_norm_ff,
    dec_up,
    dec_down,
):
    chip, core = lax.axis_index("rows"), lax.axis_index("seq")
    x_own, d_own, c_own = enc_input[0], dec_input[0], cotangent[0]
    half, d_half = x_own.shape[0], d_own.shape[0]
    enc, dec = 2 * half, 2 * d_half
    width, hidden = D // 2, FF // 2

    def swap(values):
        return lax.ppermute(values, "seq", [(0, 1), (1, 0)])

    def row(gain):
        return gain.reshape(1, -1)

    def v(*arrays):
        return [(array, "vmem") for array in arrays]

    def h(*arrays):
        return [(array, "all") for array in arrays]

    def cols(*arrays):
        return [(array, "cols") for array in arrays]

    square = (D, D)
    ordered = in_order(rows_count)

    def payload(total, extra=0):
        if ordered:
            return [((total // 2 + extra, LANES), LOW)] * 2, [((rows_count, total // rows_count, LANES), LOW)]
        return [((total + extra, LANES), LOW), ((16, LANES), LOW)], [((1, total, LANES), LOW)]

    squares, ffs, last = payload(4 * D), payload(4 * D + FF), payload(4 * D, SMALL)

    lead = D // rows_count

    def arranged(pay, leads, extra, orders):
        if ordered:
            return pay
        places = jnp.array([[chunk_of(q, order) for q in range(rows_count)] for order in orders], jnp.int32)
        parts, start = [], 0
        for count in leads:
            parts.append(pay[0][start : start + count].reshape(rows_count, -1, LANES))
            start += count
        chunks = jnp.take(jnp.concatenate(parts, 1), places[core] ^ chip, axis=0)
        return [
            jnp.concatenate([part.reshape(-1, LANES), pay[0][start : start + extra]], 0)
            for part in (chunks[: rows_count // 2], chunks[rows_count // 2 :])
        ]

    class Sum:
        def __init__(self, pay, leads, outs, name, extra=0):
            self.orders = bit_orders(rows_count, name)
            self.kept, self.sent = arranged(pay, leads, extra, self.orders)
            self.segments = [self.kept.shape[0] - extra]
            self.outs, self.extra, self.name, self.stage, self.found = outs, extra, name, 0, None
            self.send()

        def send(self):
            pairs = [
                (at * 2 + c, (at ^ (1 << self.orders[c][self.stage])) * 2 + c)
                for at in range(rows_count)
                for c in range(2)
            ]
            self.came = lax.ppermute(self.sent, ("rows", "seq"), pairs)
            self.stage += 1

        def add(self, token, *others, after=()):
            if self.found is not None:
                return token
            every = (self, *others)
            for other in others:
                assert other.stage == self.stage and other.orders[0][self.stage :] == self.orders[0][self.stage :]
                assert not self.extra
            name = f"sum_{self.name}_{self.stage}"
            operands = v(*[array for each in every for array in (each.kept, each.came)])
            if self.stage == len(self.orders[0]):
                token, self.found = call(
                    token, last_kernel, operands,
                    [out for each in every for out in each.outs], limit=8, name=name, after=after,
                )
                return token
            segments = [each.segments for each in every]
            self.extra = every[-1].extra
            self.segments = [size // 2 for sizes in segments for size in sizes]
            self.outs = [out for each in every for out in each.outs]
            shape = (sum(self.segments) + self.extra, LANES)
            token, (self.kept, self.sent) = call(
                token, functools.partial(sum_kernel, segments=segments, extra=self.extra), operands,
                [(shape, LOW)] * 2, limit=8, name=name, after=after,
            )
            self.send()
            return token

    ff_outs = [((lead, hidden), FULL), ((FF // rows_count, LANES), FULL)]
    square_outs = [((lead, LANES), FULL)] * 4
    small_outs = [((1, lead), FULL)] * 6 + [((HEADS, BUCKETS), FULL)] * 2

    x_other, d_other, c_other = swap(x_own), swap(d_own), swap(c_own)

    token, (mixed, probs, queries, keys, values, x_normed) = call(
        None,
        enc_attention_kernel,
        h(x_own) + v(x_other) + h(row(enc_norm_attn), enc_segments, enc_table.T) + cols(enc_query, enc_key, enc_value),
        [
            ((width, enc), LOW), ((HEADS // 4, enc, 2 * enc), LOW),
            ((enc, width), LOW), ((enc, width), LOW), ((enc, width), LOW), ((enc, D), LOW),
        ],
        [((HEADS, 2 * enc), FULL)],
        name="enc_attention",
    )
    mixed_other = swap(mixed)
    token, (d_probs, d_queries, d_keys, d_values, d_normed, d_mixed, d_all) = call(
        token,
        dec_attention_kernel,
        h(d_own) + v(d_other)
        + h(row(dec_norm_self), dec_segments, dec_table.T) + v(dec_query, dec_key, dec_value),
        [((HEADS // 2, dec, 2 * dec), LOW)] + [((dec, D), LOW)] * 4 + [((D, dec), LOW), ((dec, D), FULL)],
        name="dec_attention", after=[c_other],
    )
    token, (mid, after_part, after_low, active, ff_in) = call(
        token,
        enc_ff_kernel,
        h(x_own) + v(x_other, mixed, mixed_other)
        + [(enc_mix, "rows"), (enc_mix, "rows_other"), (row(enc_norm_ff), "all")] + v(enc_up, enc_down),
        [((enc, D), FULL), ((enc, D), FULL), ((enc, D), LOW), ((2 * enc, hidden), LOW), ((enc, D), LOW)],
        name="enc_ff",
    )
    after_came = swap(after_low)
    token, (d_mid, cross_in, cross_queries) = call(
        token,
        dec_mid_kernel,
        v(d_all, d_mixed, dec_mix) + h(row(dec_norm_cross)) + v(cross_query),
        [((dec, D), FULL), ((dec, D), LOW), ((dec, D), LOW)],
        name="dec_mid",
    )
    token, (
        enc_result, after, state, c_keys, c_values, c_probs, c_mixed, dec_result, stream, g_dec_ff, *pay_first, active,
    ) = call(
        token,
        functools.partial(decoder_kernel, rows_count),
        v(after_part, after_came) + h(row(enc_norm_final), enc_segments, dec_segments) + v(cross_queries, d_mid)
        + h(row(dec_norm_ff), c_own) + v(c_other, cross_key, cross_value, cross_mix, dec_up, dec_down),
        [
            ((half, D), FULL), ((enc, D), FULL), ((enc, D), LOW), ((enc, D), LOW), ((enc, D), LOW),
            ((HEADS // 2, enc, 2 * dec), LOW), ((D, dec), LOW), ((d_half, D), FULL), ((dec, D), FULL), ((1, D), FULL),
        ] + ffs[0],
        ffs[1] + [((dec, D), FULL), ((dec, D), LOW), ((dec, D), FULL), ((dec, FF), LOW), ((dec, FF), LOW)],
        name="decoder", through=[active],
    )
    active_other = swap(active)
    first = Sum(pay_first, [D] * 4 + [FF], ff_outs, "dec_ff")
    token, (enc_stream, enc_low, g_final, stream, g_cross, *pay_cross) = call(
        token,
        functools.partial(cross_back_kernel, rows_count),
        v(stream, d_mid) + h(row(dec_norm_cross)) + v(cross_in, cross_queries, c_keys, c_values, c_probs, c_mixed, state, after,
          )
        + h(row(enc_norm_final)) + v(cross_mix, cross_key, cross_value, cross_query),
        [((enc, D), FULL), ((enc, D), LOW), ((1, D), FULL), ((dec, D), FULL), ((1, D), FULL)] + squares[0],
        squares[1] + [((dec, D), LOW), ((D, dec), LOW), ((dec, D), LOW), ((enc, D), LOW), ((enc, D), LOW)],
        name="cross_back",
    )
    second = Sum(pay_cross, [D] * 4, square_outs, "cross")
    token, (before_grad, part) = call(
        token,
        enc_ff_back_kernel,
        v(enc_low, active, active_other)
        + v(enc_down, enc_up),
        [((enc, hidden), LOW), ((enc, D), FULL)],
        name="enc_ff_back",
    )
    token, pay_enc_ff = call(
        token,
        functools.partial(enc_ff_weights_kernel, rows_count),
        v(ff_in, before_grad, active, active_other, enc_low),
        ffs[0],
        ffs[1] + [((FF, LANES), FULL)],
        name="enc_ff_weights",
    )
    third = Sum(pay_enc_ff, [D] * 4 + [FF], ff_outs, "enc_ff")
    token = first.add(token)
    token, (low, enc_stream, g_ff, query_grad, key_grad, value_grad, table_enc, normed_part, *normed_low) = call(
        token,
        enc_attention_back_kernel,
        v(part, mid) + h(row(enc_norm_ff)) + v(enc_stream) + [(enc_mix, "rows")]
        + v(queries, keys, values, probs) + cols(enc_query, enc_key, enc_value),
        [
            ((enc, D), LOW), ((enc, D), FULL), ((1, D), FULL), ((enc, width), LOW), ((enc, width), LOW),
            ((enc, width), LOW), ((HEADS, BUCKETS), FULL), ((enc, D), FULL), ((half, D), LOW),
            ((half + 16, D), LOW),
        ],
        [((BLOCK, 2 * enc), FULL), ((HEADS, 2 * enc), FULL), ((width, enc), LOW)],
        name="enc_attention_back",
    )
    normed_came = [swap(part) for part in normed_low]
    token, (dec_input_grad, g_self, table_dec, dec_squares, *pay_dec) = call(
        token,
        functools.partial(dec_back_kernel, rows_count),
        v(stream) + h(d_own) + v(d_other) + h(row(dec_norm_self))
        + v(d_normed, d_queries, d_keys, d_values, d_probs, d_mixed)
        + v(dec_mix, dec_query, dec_key, dec_value),
        [((d_half, D), FULL), ((1, D), FULL), ((HEADS, BUCKETS), FULL), ((1, D), FULL)] + squares[0],
        squares[1] + [((dec, D), LOW), ((D, dec), LOW)] + [((dec, D), LOW)] * 3 + [((HEADS, 2 * BLOCK), FULL), ((dec, D), FULL), ((dec, D), FULL)],
        name="dec_back",
    )
    fourth = Sum(pay_dec, [D] * 4, square_outs, "dec")
    token = third.add(token)
    token = second.add(token)
    token, (enc_input_grad, row_norm, *pay_enc) = call(
        token,
        functools.partial(enc_finish_kernel, rows_count),
        v(normed_part, *normed_came, enc_stream) + h(x_own) + v(x_other) + h(row(enc_norm_attn)) + v(x_normed, query_grad, key_grad,
          value_grad, mixed, mixed_other, low, table_enc, table_dec, dec_squares, g_ff, g_final, g_self, g_cross,
          g_dec_ff),
        [((half, D), FULL), ((1, 1), FULL)] + last[0],
        last[1] + [((enc, D), FULL), ((enc, D), FULL), ((D, LANES), FULL), ((SMALL, LANES), FULL)],
        name="enc_finish",
    )

    fifth = Sum(pay_enc, [D] * 4, square_outs + small_outs, "enc", SMALL)
    sums = [first, second, third, fourth, fifth]
    for which in TAIL:
        token = sums[which].add(token)
    while any(each.found is None for each in sums):
        for each in sums:
            token = each.add(token)
    dec_u, dec_d = first.found
    enc_u, enc_d = third.found
    cross_q, cross_k, cross_v, cross_m = second.found
    dec_q, dec_k, dec_v, dec_m = fourth.found
    enc_q, enc_k, enc_v, enc_m, *small = fifth.found
    gains = [gain[0] for gain in small[:6]]
    tables = [small[6].T, small[7].T]
    return (
        enc_result[None], dec_result[None], enc_input_grad[None], dec_input_grad[None], row_norm[0],
        gains[0], enc_q, enc_k, enc_v, enc_m, tables[0], gains[1], enc_u, enc_d, gains[2],
        gains[3], dec_q, dec_k, dec_v, dec_m, tables[1], gains[4], cross_q, cross_k, cross_v, cross_m,
        gains[5], dec_u, dec_d,
    )


def solution(mesh):
    split, line, copied = P("rows", "seq", None), P("rows", None), P()
    in_specs = (split, split, line, line, split) + (copied,) * 24
    block, vector = P("rows", "seq"), P("rows")
    out_specs = (
        (split,) * 4 + (vector,)
        + (vector,) + (block,) * 4 + (copied, vector, block, block, vector)
        + (vector,) + (block,) * 4 + (copied, vector) + (block,) * 4 + (vector, block, block)
    )
    return jax.shard_map(
        functools.partial(on_device, mesh.shape["rows"]),
        mesh=mesh, in_specs=in_specs, out_specs=out_specs, check_vma=False,
    )
```
